512 devices in a mesh: index: 128 (over y, z, core), reader: 4 (over x).
Axes of the slice: x: 4, y: 4, z: 16, core: 2. Of those that a mesh axis runs over, the one named last changes fastest.
Arguments:
- index_emb: float32 [65536, 768], P('index'), may hold values from -6 to 6
- query_feat: bfloat16 [512, 768], P(('index', 'reader')), may hold values from -24 to 24
- query_proj: bfloat16 [768, 768], replicated, may hold values from -0.21875 to 0.21875
- passage_id: int32 [512, 20], P(('index', 'reader')), may hold values from 0 to 65535, as said below
- passage_len: int32 [512, 20], P('index'), may hold values from 1 to 8
- enc_out: bfloat16 [512, 20, 8, 4096], P('index', None, None, 'reader'), may hold values from -6 to 6
- key_proj: bfloat16 [4096, 4096], P('index', 'reader'), may hold values from -0.09375 to 0.09375
- key_gain: bfloat16 [4096], P('reader'), may hold values from 0.5 to 1.5
- dec_query: bfloat16 [512, 16, 4096], P('index', None, 'reader'), may hold values from -6 to 6
Outputs:
- grad_proj: float32 [768, 768], P('index')
- slab_best: float32 [512], P(('index', 'reader'))
- retr_loss: float32 [512], P(('index', 'reader'))
- log_target: float32 [512, 20], P(('index', 'reader'))
The draws below stay inside these ranges and needn't reach their ends.
Inputs may be any that keep to these rules, and one draw needn't show every extreme that they name: `passage_id`: passage p is row p % 512 of index shard p // 512.
All inputs are finite; a program needn't handle non-finite values.
Results may differ from the reference program's by a relative error of at most 0.0003.
Values may be sent and summed in bfloat16 or wider, within the bound.
No kernel may reach another device: no remote copies, remote signals or barrier semaphores. Data moves between devices by JAX's collectives and lax.ppermute only.
A program may use at most 128 MiB of HBM per device.

```python
import math
import jax
import jax.numpy as jnp
from jax import lax

D = 768
HEADS = 64
DH = 64
TOPK = 20
ANS = 16
LP = 8
ROWS = 512
HD = 4096
QUERIES = 512
PASSAGES = 65536
N_INDEX = 128


def draw_passage_id(key, part):
    key = jax.random.fold_in(key, 31)
    streams = jax.random.split(key, 7)
    layout = (QUERIES, TOPK)
    lowest = jnp.minimum(jax.random.randint(streams[0], layout, 0, N_INDEX), jax.random.randint(streams[1], layout, 0, N_INDEX))
    lowest = jnp.minimum(lowest, jax.random.randint(streams[2], layout, 0, N_INDEX))
    offset = jax.random.randint(streams[3], (), 0, N_INDEX)
    owners = (lowest + offset) % N_INDEX
    within = jax.random.randint(streams[4], layout, 0, ROWS)
    passage = owners * ROWS + within
    places = jnp.arange(QUERIES * TOPK, dtype=jnp.int32).reshape(layout)
    top_place = jax.random.randint(streams[5], (), 0, QUERIES * TOPK)
    low_place = (top_place + 1 + jax.random.randint(streams[6], (), 0, QUERIES * TOPK - 1)) % (QUERIES * TOPK)
    passage = jnp.where(places == top_place, PASSAGES - 1, passage)
    passage = jnp.where(places == low_place, 0, passage)
    return passage.astype(jnp.int32)


def draw_enc_out(key, part):
    key = jax.random.fold_in(key, 32)
    first, second = jax.random.split(key)
    common = jax.random.normal(first, (QUERIES, TOPK, 1, HD), jnp.float32)
    detail = jax.random.normal(second, (QUERIES, TOPK, LP, HD), jnp.float32)
    mixed = 0.8 * common + 0.6 * detail
    return jnp.clip(mixed, -6.0, 6.0).astype(jnp.bfloat16)


def draw_dec_query(key, part):
    key = jax.random.fold_in(key, 33)
    first, second = jax.random.split(key)
    common = jax.random.normal(first, (QUERIES, 1, HD), jnp.float32)
    detail = jax.random.normal(second, (QUERIES, ANS, HD), jnp.float32)
    mixed = 0.8 * common + 0.6 * detail
    return jnp.clip(mixed, -6.0, 6.0).astype(jnp.bfloat16)


def set_ends(array, key, smallest, largest):
    spot = [jax.random.randint(jax.random.fold_in(key, axis), (), 0, length) for axis, length in enumerate(array.shape)]
    longest = array.shape.index(max(array.shape))
    beside = spot[:longest] + [(spot[longest] + 1) % array.shape[longest]] + spot[longest + 1:]
    return array.at[tuple(spot)].set(smallest).at[tuple(beside)].set(largest)


def with_spikes(values, own_key, source, target, parts, factor):
    def block_of(position):
        return (jnp.arange(values.shape[position]) // (values.shape[position] // parts)).reshape((-1,) + (1,) * (values.ndim - 1 - position))

    one_side = jax.random.permutation(own_key, parts)[block_of(target)]
    far = (block_of(target) + parts // 2) % parts
    return jnp.where((block_of(source) == one_side) | (block_of(source) == far), factor * values, values)


def levels(stream_key, shape, pieces, smallest, top_value):
    level = 1.0
    for dim, parts in pieces:
        draws = jax.random.uniform(jax.random.fold_in(jax.random.fold_in(stream_key, 6), dim), (parts,), jnp.float32, smallest / len(pieces), top_value / len(pieces))
        level = level * jnp.repeat(jnp.exp(draws), shape[dim] // parts).reshape((-1,) + (1,) * (len(shape) - 1 - dim))
    return level


def scatter_about(own_key, shape, spread, reach, pieces=(), kind=jnp.bfloat16):
    array = spread * jax.random.normal(own_key, shape, jnp.float32)
    if pieces:
        array = array * levels(own_key, shape, pieces, -0.22, 0.18)
    return jnp.clip(array, -reach, reach).astype(kind)


def heavy_noise(key, shape, deviation, reach, pieces, heavy, kind=jnp.bfloat16):
    values = deviation * jax.random.normal(key, shape, jnp.float32)
    if pieces:
        values = values * levels(key, shape, pieces, -0.22, 0.18)
    return jnp.clip(with_spikes(values, jax.random.fold_in(key, 3), *heavy), -reach, reach).astype(kind)


def setup_inputs(seed: int = 0) -> dict:
    seeds = jax.random.split(jax.random.key(seed), 10)
    return {
        "index_emb": scatter_about(seeds[0], (PASSAGES, D), 1.0, 6.0, ((0, 128),), jnp.float32),
        "query_feat": heavy_noise(seeds[1], (QUERIES, D), 1.0, 24.0, ((0, 512),), (0, 1, 256, 6.0)),
        "query_proj": scatter_about(seeds[2], (D, D), D ** -0.5, 0.21875),
        "passage_id": draw_passage_id(jax.random.fold_in(seeds[9], 71), 0),
        "passage_len": set_ends(jax.random.randint(seeds[4], (QUERIES, TOPK), 1, LP + 1), jax.random.fold_in(seeds[4], 1), 1, LP).astype(jnp.int32),
        "enc_out": draw_enc_out(jax.random.fold_in(seeds[9], 71), 0),
        "key_proj": scatter_about(seeds[6], (HD, HD), HD ** -0.5, 0.09375, ((0, 128), (1, 4))),
        "key_gain": jnp.clip(1.0 + 0.1 * jax.random.normal(seeds[7], (HD,), jnp.float32), 0.5, 1.5).astype(jnp.bfloat16),
        "dec_query": draw_dec_query(jax.random.fold_in(seeds[9], 71), 0),
    }


EPSILON = 1e-06
SOFTMAX_TEMPER = 0.05

def reference(index_emb, query_feat, query_proj, passage_id, passage_len, enc_out, key_proj, key_gain, dec_query):
    query_vec = jnp.dot(query_feat, query_proj, preferred_element_type=jnp.float32)
    query_scale = lax.rsqrt(lax.optimization_barrier(jnp.sum(query_vec * query_vec, axis=1, keepdims=True)) + EPSILON)
    normalized_query = query_vec * query_scale
    row_unit = index_emb * lax.rsqrt(lax.optimization_barrier(jnp.sum(index_emb * index_emb, axis=1, keepdims=True)) + EPSILON)
    shard_blocks = row_unit.reshape(N_INDEX, ROWS, D)

    def best_of(running, row_block_size):
        similarity_scores = lax.dot_general(normalized_query, row_block_size, (((1,), (1,)), ((), ())), precision=lax.Precision.HIGHEST) / SOFTMAX_TEMPER
        return (jnp.maximum(running, lax.optimization_barrier(jnp.max(similarity_scores, axis=1))), None)
    slab_best, _ = lax.scan(best_of, jnp.full((QUERIES,), -1e+30, jnp.float32), shard_blocks)
    selected_passages = row_unit[passage_id]
    fetched_passage_index = jnp.einsum('vh,vrh->vr', normalized_query, selected_passages, precision=lax.Precision.HIGHEST) / SOFTMAX_TEMPER
    expo = jnp.exp(fetched_passage_index)
    total = lax.optimization_barrier(jnp.sum(expo, axis=1, keepdims=True))
    retriever_probability = expo / total
    log_prob = fetched_passage_index - jnp.log(total)
    gain = key_gain.astype(jnp.float32).reshape(HEADS, DH)
    weight_full = key_proj.astype(jnp.float32)

    def per_query(items):
        tokens, decoder, lengths = items
        keys = jnp.dot(tokens.reshape(TOPK * LP, HD).astype(jnp.float32), weight_full).reshape(TOPK * LP, HEADS, DH)
        key_unit = (keys * lax.rsqrt(lax.optimization_barrier(jnp.mean(keys * keys, axis=2, keepdims=True)) + EPSILON) * gain).astype(jnp.bfloat16)
        decoded = decoder.astype(jnp.float32).reshape(ANS, HEADS, DH)
        dec_unit = (decoded * lax.rsqrt(lax.optimization_barrier(jnp.mean(decoded * decoded, axis=2, keepdims=True)) + EPSILON)).astype(jnp.bfloat16)
        similarity_scores = jnp.einsum('ahd,nhd->han', dec_unit.astype(jnp.float32), key_unit.astype(jnp.float32)) / math.sqrt(DH)
        positions = jnp.arange(LP).astype(jnp.int32)
        live = (positions[None, :] < lengths.astype(jnp.int32)[:, None]).reshape(TOPK * LP)
        weight = jnp.where(live, jnp.exp(similarity_scores), 0.0)
        attention = weight / lax.optimization_barrier(jnp.sum(weight, axis=2, keepdims=True))
        return lax.optimization_barrier(jnp.sum(attention.reshape(HEADS, ANS, TOPK, LP), axis=(0, 1, 3))) / (HEADS * ANS)
    attention_target = lax.map(per_query, (enc_out, dec_query, passage_len))
    log_target = jnp.log(attention_target)
    retr_loss = lax.optimization_barrier(jnp.sum(attention_target * (log_target - log_prob), axis=1))
    score_multiplier = (retriever_probability - attention_target) / SOFTMAX_TEMPER
    unit_grad = jnp.einsum('qk,qkd->qd', score_multiplier, selected_passages, precision=lax.Precision.HIGHEST)
    along_query = lax.optimization_barrier(jnp.sum(normalized_query * unit_grad, axis=1, keepdims=True))
    vec_grad = (unit_grad - normalized_query * along_query) * query_scale
    grad_proj = jnp.dot(query_feat.astype(jnp.float32).T, vec_grad, precision=lax.Precision.HIGHEST)
    return (grad_proj, slab_best, retr_loss, log_target)
```

```python
import math

import jax
import jax.numpy as jnp
from jax import lax
from jax.sharding import Mesh, PartitionSpec as P

HEADS = 64
DH = 64
ANS = 16
EPSILON = 1e-06
SOFTMAX_TEMPER = 0.05
EXACT = lax.Precision.HIGHEST
INDEX = ("y", "z", "core")


def shift(x, axis, step):
    size = lax.axis_size(axis)
    return lax.ppermute(x, axis, [((i + step) % size, i) for i in range(size)])


def gather_direct(x, axis):
    return jnp.stack([x if s == 0 else shift(x, axis, s) for s in range(lax.axis_size(axis))])


def gather_doubling(x, axis):
    held = x[None]
    step = 1
    while step < lax.axis_size(axis):
        held = jnp.concatenate([held, shift(held, axis, step)])
        step *= 2
    return held


def reduce_direct(x, axis, merge):
    total = x[0]
    for s in range(1, lax.axis_size(axis)):
        total = merge(total, shift(x[s], axis, -s))
    return total


def reduce_halving(x, axis, merge):
    step = lax.axis_size(axis) // 2
    while step >= 1:
        x = merge(x[:step], shift(x[step:], axis, -step))
        step //= 2
    return x[0]


def ring_halves(x, axis):
    half = x.shape[0] // 2
    after = shift(x, axis, 1)
    before = shift(x, axis, -1)
    far = jnp.concatenate([shift(after[:half], axis, 1), shift(before[half:], axis, -1)])
    return [x, after, far, before]


def ring_both_ways(x, axis):
    size = lax.axis_size(axis)
    blocks = [x] + [None] * (size - 1)
    up = down = x
    for step in range(1, size // 2 + 1):
        up = shift(up, axis, 1)
        blocks[step] = up
        if step < size // 2:
            down = shift(down, axis, -1)
            blocks[size - step] = down
    return jnp.stack(blocks)


def body(
    index_emb,
    query_feat,
    query_proj,
    passage_id,
    passage_len,
    enc_out,
    key_proj,
    key_gain,
    dec_query,
):
    y, z, core, r = (lax.axis_index(a) for a in ("y", "z", "core", "reader"))
    ny, nz, ncore, nx = (lax.axis_size(a) for a in ("y", "z", "core", "reader"))
    n_index = ny * nz * ncore
    my_shard = (y * nz + z) * ncore + core
    shard_rows, width = index_emb.shape
    topk = passage_id.shape[1]

    with jax.named_scope("gather_key_proj"):
        own_z = jnp.roll(ring_both_ways(key_proj, "z"), z, axis=0)
        own_core = ring_halves(own_z, "y")
        blocks = []
        for block in own_core:
            other = shift(block, "core", 1)
            low = jnp.where(core == 0, block, other)
            high = jnp.where(core == 0, other, block)
            blocks.append(jnp.stack([low, high], axis=1).reshape(-1, key_proj.shape[1]))
        weight_blocks = jnp.stack(blocks)

    group, _, plen, feats_here = enc_out.shape
    token_rows = group * topk * plen
    with jax.named_scope("gather_enc_out"):
        token_blocks = ring_halves(enc_out.reshape(token_rows, feats_here), "reader")

    with jax.named_scope("gather_queries"):
        ids_high = (passage_id // 256).astype(jnp.bfloat16)
        ids_low = (passage_id % 256).astype(jnp.bfloat16)
        packed = jnp.concatenate([query_feat, ids_high, ids_low], axis=1)
        packed = jnp.pad(packed, ((0, 0), (0, -packed.shape[1] % 128)))
        packed = jnp.roll(gather_direct(packed[0], "reader"), r, axis=0)
        packed = gather_doubling(packed, "z")
        packed = gather_direct(packed, "y")
        packed = gather_direct(packed, "core")
        packed = packed.reshape(n_index * nx, -1)
    feats = packed[:, :width]
    ids = packed[:, width : width + 2 * topk].astype(jnp.int32)
    ids = ids[:, :topk] * 256 + ids[:, topk:]
    row_index = ids - my_shard * shard_rows
    row_iota = lax.broadcasted_iota(jnp.int32, (1, shard_rows), 1)

    with jax.named_scope("scores"):
        query_vec = jnp.dot(feats, query_proj, preferred_element_type=jnp.float32)
        query_scale = lax.rsqrt(jnp.sum(query_vec * query_vec, axis=1, keepdims=True) + EPSILON)
        query_unit = query_vec * query_scale
        row_unit = index_emb * lax.rsqrt(
            jnp.sum(index_emb * index_emb, axis=1, keepdims=True) + EPSILON
        )
        share = lax.dynamic_index_in_dim(query_unit.reshape(n_index, nx, width), r, 1, False)
        share_rows = lax.dynamic_index_in_dim(row_index.reshape(n_index, nx, topk), r, 1, False)
        scores = (
            lax.dot_general(share, row_unit, (((1,), (1,)), ((), ())), precision=EXACT)
            / SOFTMAX_TEMPER
        )
        picked = [
            jnp.sum(
                jnp.where(share_rows[:, k : k + 1] == row_iota, scores, 0.0), axis=1, keepdims=True
            )
            for k in range(topk)
        ]
        state = jnp.concatenate(picked + [jnp.max(scores, axis=1, keepdims=True)], axis=1)

    def merge(a, b):
        lane = lax.broadcasted_iota(jnp.int32, a.shape, a.ndim - 1)
        return jnp.where(lane < topk, a + b, jnp.maximum(a, b))

    with jax.named_scope("reduce_scores"):
        state = state.reshape(ncore, ny, nz, topk + 1)
        state = reduce_direct(state, "core", merge)
        state = reduce_direct(state, "y", merge)
        state = reduce_halving(state, "z", merge)
        fetched_own = state[:topk]
        slab_best = state[topk:]
        fetched = jnp.roll(gather_direct(fetched_own, "reader"), r, axis=0)
    expo = jnp.exp(fetched)
    total = jnp.sum(expo, axis=1, keepdims=True)
    prob = expo / total
    log_prob = fetched - jnp.log(total)

    with jax.named_scope("attention"):
        answer = dec_query.shape[1]
        heads_here = feats_here // DH
        keys = 0.0
        for j, tokens in enumerate(token_blocks):
            rows = lax.dynamic_index_in_dim(weight_blocks, (r + j - y) % ny, 0, False)
            keys += jnp.dot(tokens, rows, preferred_element_type=jnp.float32)
        keys = keys.reshape(group, topk * plen, heads_here, DH)
        gain = key_gain.astype(jnp.float32).reshape(heads_here, DH)
        key_unit = (
            keys * lax.rsqrt(jnp.mean(keys * keys, axis=3, keepdims=True) + EPSILON) * gain
        ).astype(jnp.bfloat16)
        decoded = dec_query.astype(jnp.float32).reshape(group, answer, heads_here, DH)
        dec_unit = (
            decoded * lax.rsqrt(jnp.mean(decoded * decoded, axis=3, keepdims=True) + EPSILON)
        ).astype(jnp.bfloat16)
        similarity_scores = jnp.einsum(
            "gahd,gnhd->ghan", dec_unit, key_unit, preferred_element_type=jnp.float32
        ) / math.sqrt(DH)
        positions = lax.broadcasted_iota(jnp.int32, (group, topk, plen), 2)
        live = (positions < passage_len[:, :, None]).reshape(group, 1, 1, topk * plen)
        weight = jnp.where(live, jnp.exp(similarity_scores), 0.0)
        attention = weight / jnp.sum(weight, axis=3, keepdims=True)
        partial_mass = jnp.sum(
            attention.reshape(group, heads_here, answer, topk, plen), axis=(1, 2, 4)
        ) / (HEADS * ANS)

    with jax.named_scope("targets"):
        target = jnp.sum(gather_direct(partial_mass, "reader"), axis=0)
        coef = (prob - target) / SOFTMAX_TEMPER
        all_coef = gather_direct(coef, "z")
        all_coef = gather_direct(all_coef, "y")
        all_coef = gather_direct(all_coef, "core")
        all_coef = all_coef.reshape(n_index * nx, topk)

    with jax.named_scope("gradient"):
        cols = width // nx
        my_rows = lax.dynamic_slice_in_dim(row_unit, r * cols, cols, 1)
        my_unit = lax.dynamic_slice_in_dim(query_unit[:nx], r * cols, cols, 1)
        coef_matrix = jnp.zeros((n_index * nx, shard_rows), jnp.float32)
        for k in range(topk):
            coef_matrix = coef_matrix + jnp.where(
                row_index[:, k : k + 1] == row_iota, all_coef[:, k : k + 1], 0.0
            )
        along = SOFTMAX_TEMPER * jnp.sum(coef * fetched, axis=1, keepdims=True)
        part = jnp.dot(coef_matrix, my_rows, precision=EXACT)
        part = part - jnp.pad(my_unit * along, ((0, part.shape[0] - nx), (0, 0)))
        part = part * query_scale
        six = width // n_index
        place = lax.broadcasted_iota(jnp.int32, (1, width), 1)
        to_core, to_y = place // (ny * nz * six), place // (nz * six) % ny
        to_z, within = place // six % nz, place % six
        column = (((to_y + y) % ny * nz + to_z) * ncore + (to_core + core) % ncore) * six + within
        chosen = (lax.broadcasted_iota(jnp.int32, (width, 1), 0) == column).astype(jnp.bfloat16)
        ordered = jnp.dot(feats, chosen, preferred_element_type=jnp.float32)
        term = lax.dot_general(ordered, part, (((0,), (0,)), ((), ())), precision=EXACT)

    with jax.named_scope("reduce_gradient"):
        term = term.reshape(ncore, ny, nz, six, cols)
        term = reduce_direct(term, "core", jnp.add)
        term = reduce_direct(term, "y", jnp.add)
        term = jnp.sum(lax.all_to_all(term, "z", 0, 0, tiled=True), axis=0)
        grad_proj = jnp.roll(gather_direct(term, "reader"), r, axis=0)
        grad_proj = grad_proj.transpose(1, 0, 2).reshape(six, width)

    my_target = lax.dynamic_slice_in_dim(target, r, 1, 0)
    my_log_prob = lax.dynamic_slice_in_dim(log_prob, r, 1, 0)
    log_target = jnp.log(my_target)
    retr_loss = jnp.sum(my_target * (log_target - my_log_prob), axis=1)
    return (grad_proj, slab_best, retr_loss, log_target)


def solution(mesh):
    split = Mesh(mesh.devices.reshape(4, 16, 2, 4), INDEX + ("reader",))
    return jax.shard_map(
        body,
        mesh=split,
        in_specs=(
            P(INDEX, None),
            P(INDEX + ("reader",), None),
            P(),
            P(INDEX + ("reader",), None),
            P(INDEX, None),
            P(INDEX, None, None, "reader"),
            P(INDEX, "reader"),
            P("reader"),
            P(INDEX, None, "reader"),
        ),
        out_specs=(
            P(INDEX, None),
            P(INDEX + ("reader",)),
            P(INDEX + ("reader",)),
            P(INDEX + ("reader",), None),
        ),
        check_vma=False,
    )
```

```python
import math

import jax
import jax.numpy as jnp
from jax import lax
from jax.sharding import Mesh, PartitionSpec as P

HEADS = 64
DH = 64
ANS = 16
EPSILON = 1e-06
SOFTMAX_TEMPER = 0.05
EXACT = lax.Precision.HIGHEST
INDEX = ("y", "z", "core")


def shift(x, axis, step):
    size = lax.axis_size(axis)
    return lax.ppermute(x, axis, [((i + step) % size, i) for i in range(size)])


def reduce_direct(x, axis, merge):
    total = x[0]
    for s in range(1, lax.axis_size(axis)):
        total = merge(total, shift(x[s], axis, -s))
    return total


def ring_halves(x, axis):
    half = x.shape[0] // 2
    after = shift(x, axis, 1)
    before = shift(x, axis, -1)
    far = jnp.concatenate([shift(after[:half], axis, 1), shift(before[half:], axis, -1)])
    return [x, after, far, before]


def body(
    index_emb,
    query_feat,
    query_proj,
    passage_id,
    passage_len,
    enc_out,
    key_proj,
    key_gain,
    dec_query,
):
    y, z, core, r = (lax.axis_index(a) for a in ("y", "z", "core", "reader"))
    ny, nz, ncore, nx = (lax.axis_size(a) for a in ("y", "z", "core", "reader"))
    n_index = ny * nz * ncore
    my_shard = (y * nz + z) * ncore + core
    shard_rows, width = index_emb.shape
    topk = passage_id.shape[1]

    chip_pair = ("y", "core")
    n_pair = ny * ncore
    my_pair = y * ncore + core

    with jax.named_scope("gather_key_proj"):
        own_core = ring_halves(lax.all_gather(key_proj, "z"), "y")
        blocks = []
        for block in own_core:
            other = shift(block, "core", 1)
            low = jnp.where(core == 0, block, other)
            high = jnp.where(core == 0, other, block)
            blocks.append(jnp.stack([low, high], axis=1).reshape(-1, key_proj.shape[1]))
        weight_blocks = jnp.stack(blocks)

    group, _, plen, feats_here = enc_out.shape
    token_rows = group * topk * plen
    with jax.named_scope("gather_enc_out"):
        token_blocks = lax.all_gather(enc_out.reshape(token_rows, feats_here), "reader")

    with jax.named_scope("gather_queries"):
        ids_high = (passage_id // 256).astype(jnp.bfloat16)
        ids_low = (passage_id % 256).astype(jnp.bfloat16)
        packed = jnp.concatenate([query_feat, ids_high, ids_low], axis=1)
        packed = jnp.pad(packed, ((0, 0), (0, -packed.shape[1] % 128)))
        packed = lax.all_gather(packed[0], "reader")
        packed = lax.all_gather(packed, "z")
        packed = lax.all_gather(packed, chip_pair)
        packed = packed.reshape(n_index * nx, -1)
    feats = packed[:, :width]
    ids = packed[:, width : width + 2 * topk].astype(jnp.int32)
    ids = ids[:, :topk] * 256 + ids[:, topk:]
    row_index = ids - my_shard * shard_rows
    row_iota = lax.broadcasted_iota(jnp.int32, (1, shard_rows), 1)

    with jax.named_scope("scores"):
        query_vec = jnp.dot(feats, query_proj, preferred_element_type=jnp.float32)
        query_scale = lax.rsqrt(jnp.sum(query_vec * query_vec, axis=1, keepdims=True) + EPSILON)
        query_unit = query_vec * query_scale
        row_unit = index_emb * lax.rsqrt(
            jnp.sum(index_emb * index_emb, axis=1, keepdims=True) + EPSILON
        )
        share = lax.dynamic_index_in_dim(query_unit.reshape(n_index, nx, width), r, 1, False)
        share_rows = lax.dynamic_index_in_dim(row_index.reshape(n_index, nx, topk), r, 1, False)
        scores = (
            lax.dot_general(share, row_unit, (((1,), (1,)), ((), ())), precision=EXACT)
            / SOFTMAX_TEMPER
        )
        picked = [
            jnp.sum(
                jnp.where(share_rows[:, k : k + 1] == row_iota, scores, 0.0), axis=1, keepdims=True
            )
            for k in range(topk)
        ]
        state = jnp.concatenate(picked + [jnp.max(scores, axis=1, keepdims=True)], axis=1)

    def merge(a, b):
        lane = lax.broadcasted_iota(jnp.int32, a.shape, a.ndim - 1)
        return jnp.where(lane < topk, a + b, jnp.maximum(a, b))

    def merge_all(x):
        total = x[0]
        for part in range(1, x.shape[0]):
            total = merge(total, x[part])
        return total

    with jax.named_scope("reduce_scores"):
        state = state.reshape(n_pair, nz, topk + 1)
        state = merge_all(lax.all_to_all(state, chip_pair, 0, 0, tiled=True))
        state = merge_all(lax.all_to_all(state, "z", 0, 0, tiled=True))
        slab_best = state[topk:]
        fetched = lax.all_gather(state[:topk], "reader")
    expo = jnp.exp(fetched)
    total = jnp.sum(expo, axis=1, keepdims=True)
    prob = expo / total
    log_prob = fetched - jnp.log(total)

    with jax.named_scope("attention"):
        answer = dec_query.shape[1]
        heads_here = feats_here // DH
        keys = 0.0
        for j in range(nx):
            rows = lax.dynamic_index_in_dim(weight_blocks, (j - y) % ny, 0, False)
            keys += jnp.dot(token_blocks[j], rows, preferred_element_type=jnp.float32)
        keys = keys.reshape(group, topk * plen, heads_here, DH)
        gain = key_gain.astype(jnp.float32).reshape(heads_here, DH)
        key_unit = (
            keys * lax.rsqrt(jnp.mean(keys * keys, axis=3, keepdims=True) + EPSILON) * gain
        ).astype(jnp.bfloat16)
        decoded = dec_query.astype(jnp.float32).reshape(group, answer, heads_here, DH)
        dec_unit = (
            decoded * lax.rsqrt(jnp.mean(decoded * decoded, axis=3, keepdims=True) + EPSILON)
        ).astype(jnp.bfloat16)
        similarity_scores = jnp.einsum(
            "gahd,gnhd->ghan", dec_unit, key_unit, preferred_element_type=jnp.float32
        ) / math.sqrt(DH)
        positions = lax.broadcasted_iota(jnp.int32, (group, topk, plen), 2)
        live = (positions < passage_len[:, :, None]).reshape(group, 1, 1, topk * plen)
        weight = jnp.where(live, jnp.exp(similarity_scores), 0.0)
        attention = weight / jnp.sum(weight, axis=3, keepdims=True)
        partial_mass = jnp.sum(
            attention.reshape(group, heads_here, answer, topk, plen), axis=(1, 2, 4)
        ) / (HEADS * ANS)

    with jax.named_scope("targets"):
        target = jnp.sum(lax.all_gather(partial_mass, "reader"), axis=0)
        coef = (prob - target) / SOFTMAX_TEMPER
        all_coef = lax.all_gather(coef, "z")
        all_coef = lax.all_gather(all_coef, chip_pair)
        all_coef = all_coef.reshape(n_index * nx, topk)

    with jax.named_scope("gradient"):
        cols = width // nx
        my_rows = lax.dynamic_slice_in_dim(row_unit, r * cols, cols, 1)
        unit_cols = lax.dynamic_slice_in_dim(query_unit, r * cols, cols, 1)
        coef_matrix = jnp.zeros((n_index * nx, shard_rows), jnp.float32)
        for k in range(topk):
            coef_matrix = coef_matrix + jnp.where(
                row_index[:, k : k + 1] == row_iota, all_coef[:, k : k + 1], 0.0
            )
        along = SOFTMAX_TEMPER * jnp.sum(coef * fetched, axis=1, keepdims=True)
        part = jnp.dot(coef_matrix, my_rows, precision=EXACT)
        along = lax.dynamic_update_slice_in_dim(
            jnp.zeros((n_index * nx, 1), jnp.float32), along, (my_pair * nz + z) * nx, 0
        )
        part = (part - unit_cols * along) * query_scale
        six = width // n_index
        place = lax.broadcasted_iota(jnp.int32, (1, width), 1)
        to_core, to_y = place // (ny * nz * six), place // (nz * six) % ny
        to_z, within = place // six % nz, place % six
        column = ((to_y * nz + to_z) * ncore + (to_core + core) % ncore) * six + within
        chosen = (lax.broadcasted_iota(jnp.int32, (width, 1), 0) == column).astype(jnp.bfloat16)
        ordered = jnp.dot(feats, chosen, preferred_element_type=jnp.float32)
        term = lax.dot_general(ordered, part, (((0,), (0,)), ((), ())), precision=EXACT)

    with jax.named_scope("reduce_gradient"):
        term = term.reshape(ncore, ny, nz * six, cols)
        term = reduce_direct(term, "core", jnp.add)
        term = jnp.sum(lax.all_to_all(term, "y", 0, 0, tiled=True), axis=0)
        term = term.reshape(nz, six, cols)
        term = jnp.sum(lax.all_to_all(term, "z", 0, 0, tiled=True), axis=0)
        grad_proj = lax.all_gather(term, "reader")
        grad_proj = grad_proj.transpose(1, 0, 2).reshape(six, width)

    my_target = lax.dynamic_slice_in_dim(target, r, 1, 0)
    my_log_prob = lax.dynamic_slice_in_dim(log_prob, r, 1, 0)
    log_target = jnp.log(my_target)
    retr_loss = jnp.sum(my_target * (log_target - my_log_prob), axis=1)
    return (grad_proj, slab_best, retr_loss, log_target)


def solution(mesh):
    split = Mesh(mesh.devices.reshape(4, 16, 2, 4), INDEX + ("reader",))
    return jax.shard_map(
        body,
        mesh=split,
        in_specs=(
            P(INDEX, None),
            P(INDEX + ("reader",), None),
            P(),
            P(INDEX + ("reader",), None),
            P(INDEX, None),
            P(INDEX, None, None, "reader"),
            P(INDEX, "reader"),
            P("reader"),
            P(INDEX, None, "reader"),
        ),
        out_specs=(
            P(INDEX, None),
            P(INDEX + ("reader",)),
            P(INDEX + ("reader",)),
            P(INDEX + ("reader",), None),
        ),
        check_vma=False,
    )
```

```python
import functools
import math

import jax
import jax.numpy as jnp
from jax import lax
from jax.experimental import pallas as pl
from jax.experimental.pallas import tpu as pltpu
from jax.sharding import Mesh, PartitionSpec as P

HEADS = 64
DH = 64
ANS = 16
EPSILON = 1e-06
SOFTMAX_TEMPER = 0.05
EXACT = lax.Precision.HIGHEST
INDEX = ("y", "zq", "zr", "core")
Z = ("zq", "zr")
NEAR = ("reader", "y", "core")
LANES = 128
SLOT = 32
TILE = 256
N_OWNERS = 128


def shift(x, axis, step):
    size = lax.axis_size(axis)
    return lax.ppermute(x, axis, [((i + step) % size, i) for i in range(size)])


def send_all(x, axis):
    size = lax.axis_size(axis)
    return lax.all_to_all(jnp.broadcast_to(x[None], (size, *x.shape)), axis, 0, 0, tiled=True)


def halves(x):
    high = x.astype(jnp.bfloat16)
    return high, (x - high.astype(jnp.float32)).astype(jnp.bfloat16)


def dot32(a, b):
    return jnp.dot(a, b, preferred_element_type=jnp.float32)


def attention_kernel(place, tokens, *refs):
    weights, refs = refs[:8], refs[8:]
    dec, gain, live, scores, out, token_v, weight_v, keys_v, column_v, token_sem, weight_sem = refs
    y, zr, core = place[0], place[1], place[2]
    group = dec.shape[0]
    n = live.shape[1]
    for c in range(4):
        pltpu.make_async_copy(tokens.at[c], token_v.at[c], token_sem.at[c]).start()

    def spot(row, residue, which):
        return weight_v.at[row, :, (zr + residue) % 4, (core + which) % 2]

    def weight_copy(ahead, which, residue):
        return pltpu.make_async_copy(
            weights[2 * ahead + which].at[pl.ds(4 * residue, 4)],
            spot((y + ahead) % 4, residue, which),
            weight_sem.at[(y + ahead) % 4, which, residue],
        )

    for ahead in range(4):
        for which in range(2):
            for residue in range(4):
                weight_copy(ahead, which, residue).start()
    for c in range(4):
        pltpu.make_async_copy(tokens.at[c], token_v.at[c], token_sem.at[c]).wait()
        for which in range(2):
            for residue in range(4):
                here = spot(c, residue, which)
                pltpu.make_async_copy(here, here, weight_sem.at[c, which, residue]).wait()

        @pl.loop(0, keys_v.shape[1] // TILE)
        def _(t):
            cols = pl.ds(pl.multiple_of(t * TILE, TILE), TILE)
            rows = weight_v[c, :, :, :, :, cols].reshape(-1, TILE)
            term = dot32(token_v[c], rows)
            if c == 0:
                keys_v[:, cols] = term
            else:
                keys_v[:, cols] += term

    column_v[...] = jnp.zeros_like(column_v)

    @pl.loop(0, keys_v.shape[1] // TILE)
    def _(t):
        cols = pl.ds(pl.multiple_of(t * TILE, TILE), TILE)
        same = (
            lax.broadcasted_iota(jnp.int32, (TILE, TILE), 0) // DH
            == lax.broadcasted_iota(jnp.int32, (TILE, TILE), 1) // DH
        ).astype(jnp.bfloat16)
        mine = (
            lax.broadcasted_iota(jnp.int32, (TILE // DH * ANS, TILE), 0) // ANS
            == lax.broadcasted_iota(jnp.int32, (TILE // DH * ANS, TILE), 1) // DH
        )
        keys = keys_v[:, cols]
        high, low = halves(keys * keys)
        square = (dot32(high, same) + dot32(low, same)) / DH
        unit = (keys * lax.rsqrt(square + EPSILON) * gain[:, cols]).astype(jnp.bfloat16)
        for g in range(group):
            answer = dec[g, :, cols].astype(jnp.float32)
            answer = jnp.concatenate([answer] * (TILE // DH), axis=0)
            answer = jnp.where(mine, answer, 0.0).astype(jnp.bfloat16)
            similarity = lax.dot_general(
                answer,
                unit[g * n : (g + 1) * n],
                (((1,), (1,)), ((), ())),
                preferred_element_type=jnp.float32,
            ) / math.sqrt(DH)
            weight = jnp.where(live[g : g + 1, :] > 0, jnp.exp(similarity), 0.0)
            weight = weight / jnp.sum(weight, axis=1, keepdims=True)
            column_v[g : g + 1, :] += jnp.sum(weight, axis=0, keepdims=True)

    mass = jnp.zeros((8, LANES), jnp.float32)
    for g in range(group):
        column = jnp.broadcast_to(column_v[g : g + 1, :], (8, n))
        to = (
            lax.broadcasted_iota(jnp.int32, (n, LANES), 0) // 8 + g * SLOT
            == lax.broadcasted_iota(jnp.int32, (n, LANES), 1)
        ).astype(jnp.float32)
        mass += jnp.dot(column, to, precision=EXACT, preferred_element_type=jnp.float32)
    out[:, :LANES] = jnp.broadcast_to(mass[:1] / (HEADS * ANS), (out.shape[0], LANES))
    out[:, LANES:] = jnp.broadcast_to(scores[...], (out.shape[0], LANES))


def attention_packet(place, tokens, weights, dec, gain, live, scores):
    vmem = pl.BlockSpec(memory_space=pltpu.VMEM)
    anywhere = pl.BlockSpec(memory_space=pl.ANY)
    _, rows, width = tokens.shape
    return pl.pallas_call(
        attention_kernel,
        out_shape=jax.ShapeDtypeStruct((32, 2 * LANES), jnp.float32),
        in_specs=[pl.BlockSpec(memory_space=pltpu.SMEM)] + [anywhere] * 9 + [vmem] * 4,
        out_specs=vmem,
        scratch_shapes=[
            pltpu.VMEM((4, rows, width), jnp.bfloat16),
            pltpu.VMEM((4, 4, 4, 2, *weights[0].shape[1:]), jnp.bfloat16),
            pltpu.VMEM((rows, width), jnp.float32),
            pltpu.VMEM((8, live.shape[1]), jnp.float32),
            pltpu.SemaphoreType.DMA((4,)),
            pltpu.SemaphoreType.DMA((4, 2, 4)),
        ],
        compiler_params=pltpu.CompilerParams(vmem_limit_bytes=40 << 20),
        cost_estimate=pl.CostEstimate(
            flops=2 * rows * 4 * width * width, bytes_accessed=14 << 20, transcendentals=200000
        ),
        name="attention",
    )(place, tokens, *weights, dec, gain, live, scores)


def coef_kernel(packets, out):
    lane = lax.broadcasted_iota(jnp.int32, (8, LANES), 1)
    target = prob = fetched = jnp.zeros((8, LANES), jnp.float32)
    for x in range(4):
        target += packets[x, :, :LANES]
        scores = packets[x, :, LANES:]
        own = (lane // SLOT == x) & (lane % SLOT < 20)
        moved = scores if x == 0 else pltpu.roll(scores, SLOT * x, 1)
        prob += jnp.where(own, moved, 0.0)
        moved = pltpu.roll(scores, (SLOT * x + LANES // 2) % LANES, 1)
        fetched += jnp.where(own, moved, 0.0)
    gap = prob - target
    to = (
        lax.broadcasted_iota(jnp.int32, (LANES, LANES), 0) // SLOT * SLOT + 20
        == lax.broadcasted_iota(jnp.int32, (LANES, LANES), 1)
    ).astype(jnp.float32)
    along = jnp.dot(gap * fetched, to, precision=EXACT, preferred_element_type=jnp.float32)
    packed = gap / SOFTMAX_TEMPER + along / N_OWNERS
    out[...] = jnp.broadcast_to(packed[None], out.shape)


def gradient_kernel(coef, slot, rows, unit, scale, ordered, keep, send, matrix_v):
    n_rows = matrix_v.shape[1]
    blocks = coef.shape[0]

    @pl.loop(0, blocks // 8)
    def _(b):
        eight = pl.ds(pl.multiple_of(b * 8, 8), 8)
        row = lax.broadcasted_iota(jnp.int32, (8, n_rows), 1)
        values, places = coef[eight, :], slot[eight, :]
        for x in range(4):
            total = jnp.zeros((8, n_rows), jnp.float32)
            for k in range(SLOT * x, SLOT * x + 20):
                total += jnp.where(places[:, k : k + 1] == row, values[:, k : k + 1], 0.0)
            matrix_v[pl.ds(pl.multiple_of(x * blocks + b * 8, 8), 8), :] = total

    row_high, row_low = halves(rows[...])
    parts_high, parts_low = [], []
    for x in range(4):
        mine = slice(x * blocks, (x + 1) * blocks)
        high, low = halves(matrix_v[mine, :])
        part = dot32(high, row_high) + (dot32(high, row_low) + dot32(low, row_high))
        along = coef[:, SLOT * x + 20 : SLOT * x + 21]
        part = (part - unit[mine, :] * along) * scale[mine, :]
        high, low = halves(part)
        parts_high.append(high)
        parts_low.append(low)
    high, low = jnp.concatenate(parts_high, axis=0), jnp.concatenate(parts_low, axis=0)
    half = keep.shape[0]
    keep[...] = dot32(ordered[:half, :], high) + dot32(ordered[:half, :], low)
    send[...] = dot32(ordered[half:, :], high) + dot32(ordered[half:, :], low)


def body(
    index_emb,
    query_feat,
    query_proj,
    passage_id,
    passage_len,
    enc_out,
    key_proj,
    key_gain,
    dec_query,
):
    y, zq, zr, core, r = (lax.axis_index(a) for a in (*INDEX, "reader"))
    ny, nz, ncore, nx = 4, 16, 2, 4
    z = zq * 4 + zr
    n_index = ny * nz * ncore
    n_pair = ny * ncore
    my_shard = (y * nz + z) * ncore + core
    shard_rows, width = index_emb.shape
    topk = passage_id.shape[1]

    group, _, plen, feats_here = enc_out.shape
    token_rows = group * topk * plen
    with jax.named_scope("gather_enc_out"):
        token_blocks = lax.all_gather(enc_out.reshape(token_rows, feats_here), "reader")

    with jax.named_scope("gather_key_proj"):
        own = send_all(key_proj, "zq")
        after, before = shift(own, Z, 1), shift(own, Z, -1)
        far = [shift(own[:2], Z, 2), shift(own[2:], Z, -2)]
        own = jnp.concatenate([own, after, *far, before])
        after, before = shift(own, "y", 1), shift(own, "y", -1)
        far = jnp.concatenate([shift(after[:8], "y", 1), shift(before[8:], "y", -1)])
        weights = []
        for block in (own, after, far, before):
            weights += [block, shift(block, "core", 1)]

    with jax.named_scope("gather_queries"):
        ids_high = (passage_id // 256).astype(jnp.bfloat16)
        ids_low = (passage_id % 256).astype(jnp.bfloat16)
        packed = jnp.concatenate([query_feat, ids_high, ids_low], axis=1)
        packed = jnp.pad(packed, ((0, 0), (0, -packed.shape[1] % LANES)))
        packed = send_all(packed[0], Z)
        packed = send_all(packed, NEAR)
        packed = packed.reshape(nx, n_pair, nz, -1).transpose(0, 2, 1, 3).reshape(n_index * nx, -1)
    feats = packed[:, :width]
    ids = packed[:, width : width + 2 * topk].astype(jnp.int32)
    ids = ids[:, :topk] * 256 + ids[:, topk:]
    row_index = (ids - my_shard * shard_rows).reshape(nx, n_index, topk)
    row_iota = lax.broadcasted_iota(jnp.int32, (1, shard_rows), 1)

    with jax.named_scope("scores"):
        query_vec = jnp.dot(feats, query_proj, preferred_element_type=jnp.float32)
        query_scale = lax.rsqrt(jnp.sum(query_vec * query_vec, axis=1, keepdims=True) + EPSILON)
        query_unit = query_vec * query_scale
        row_unit = index_emb * lax.rsqrt(
            jnp.sum(index_emb * index_emb, axis=1, keepdims=True) + EPSILON
        )
        share = lax.dynamic_index_in_dim(query_unit.reshape(nx, n_index, width), r, 0, False)
        share_rows = lax.dynamic_index_in_dim(row_index, r, 0, False)
        scores = (
            lax.dot_general(share, row_unit, (((1,), (1,)), ((), ())), precision=EXACT)
            / SOFTMAX_TEMPER
        )
        picked = [
            jnp.sum(
                jnp.where(share_rows[:, k : k + 1] == row_iota, scores, 0.0), axis=1, keepdims=True
            )
            for k in range(topk)
        ]
        state = jnp.concatenate(picked + [jnp.max(scores, axis=1, keepdims=True)], axis=1)

    def merge_all(x):
        lane = lax.broadcasted_iota(jnp.int32, x.shape[1:], x.ndim - 2)
        return jnp.where(lane < topk, jnp.sum(x, axis=0), jnp.max(x, axis=0))

    with jax.named_scope("reduce_scores"):
        state = state.reshape(nz, n_pair, topk + 1)
        state = merge_all(lax.all_to_all(state, Z, 0, 0, tiled=True))
        state = merge_all(lax.all_to_all(state, ("y", "core"), 0, 0, tiled=True))
        slab_best = state[topk:]
        fetched = state[:topk]
    expo = jnp.exp(fetched)
    total = jnp.sum(expo)
    prob = expo / total
    log_prob = fetched - jnp.log(total)
    score_row = jnp.zeros((1, LANES), jnp.float32)
    score_row = score_row.at[0, :topk].set(prob).at[0, LANES // 2 : LANES // 2 + topk].set(fetched)

    with jax.named_scope("gradient_operands"):
        cols = width // nx
        my_rows = lax.dynamic_slice_in_dim(row_unit, r * cols, cols, 1)
        my_unit = lax.dynamic_slice_in_dim(query_unit, r * cols, cols, 1)
        slot_rows = jnp.pad(row_index, ((0, 0), (0, 0), (0, SLOT - topk)), constant_values=-1)
        slot_rows = slot_rows.transpose(1, 0, 2).reshape(n_index, LANES)
        six = width // n_index
        place = lax.broadcasted_iota(jnp.int32, (1, width), 1)
        to_core, to_y = place // (ny * nz * six), place // (nz * six) % ny
        to_z, within = place // six % nz, place % six
        column = ((to_y * nz + to_z) * ncore + (to_core + core) % ncore) * six + within
        chosen = (lax.broadcasted_iota(jnp.int32, (width, 1), 0) == column).astype(jnp.bfloat16)
        ordered = lax.dot_general(
            chosen, feats, (((0,), (1,)), ((), ())), preferred_element_type=jnp.bfloat16
        )

    with jax.named_scope("attention"):
        answer = dec_query.shape[1]
        heads_here = feats_here // DH
        decoded = dec_query.astype(jnp.float32).reshape(group, answer, heads_here, DH)
        dec_unit = (
            decoded * lax.rsqrt(jnp.mean(decoded * decoded, axis=3, keepdims=True) + EPSILON)
        ).astype(jnp.bfloat16)
        positions = lax.broadcasted_iota(jnp.int32, (group, topk, plen), 2)
        live = (positions < passage_len[:, :, None]).reshape(group, topk * plen)
        packet = attention_packet(
            jnp.stack([y, zr, core]).astype(jnp.int32),
            token_blocks,
            weights,
            dec_unit.reshape(group, answer, feats_here),
            key_gain.astype(jnp.float32).reshape(1, feats_here),
            live.astype(jnp.float32),
            score_row,
        )

    with jax.named_scope("targets"):
        packets = lax.all_to_all(packet, NEAR, 0, 0, tiled=True).reshape(nx, n_pair, 2 * LANES)
        vmem = pl.BlockSpec(memory_space=pltpu.VMEM)
        coef = pl.pallas_call(
            coef_kernel,
            out_shape=jax.ShapeDtypeStruct((nz, n_pair, LANES), jnp.float32),
            in_specs=[vmem],
            out_specs=vmem,
            name="coef",
        )(packets)
        coef = lax.all_to_all(coef, Z, 0, 0, tiled=True).reshape(n_index, LANES)

    with jax.named_scope("gradient"):
        part = jax.ShapeDtypeStruct((width // ncore, cols), jnp.float32)
        keep, send = pl.pallas_call(
            gradient_kernel,
            out_shape=(part, part),
            in_specs=[vmem] * 6,
            out_specs=(vmem, vmem),
            scratch_shapes=[pltpu.VMEM((n_index * nx, shard_rows), jnp.float32)],
            compiler_params=pltpu.CompilerParams(vmem_limit_bytes=40 << 20),
            name="gradient",
        )(coef, slot_rows, my_rows, my_unit, query_scale, ordered)

    with jax.named_scope("reduce_gradient"):
        term = (keep + shift(send, "core", 1)).reshape(ny, nz * six, cols)
        term = jnp.sum(lax.all_to_all(term, "y", 0, 0, tiled=True), axis=0)
        term = term.reshape(nz, six, cols)
        term = jnp.sum(lax.all_to_all(term, Z, 0, 0, tiled=True), axis=0)
        grad_proj = send_all(term, "reader")
        grad_proj = grad_proj.transpose(1, 0, 2).reshape(six, width)

    mass = jnp.sum(lax.dynamic_index_in_dim(packets, y * ncore + core, 1, False), axis=0)
    my_target = lax.dynamic_slice_in_dim(mass, r * SLOT, topk, 0)
    log_target = jnp.log(my_target)
    retr_loss = jnp.sum(my_target * (log_target - log_prob))
    return (grad_proj, slab_best, retr_loss[None], log_target[None])


def solution(mesh):
    split = Mesh(mesh.devices.reshape(4, 4, 4, 2, 4), INDEX + ("reader",))
    return jax.shard_map(
        body,
        mesh=split,
        in_specs=(
            P(INDEX, None),
            P(INDEX + ("reader",), None),
            P(),
            P(INDEX + ("reader",), None),
            P(INDEX, None),
            P(INDEX, None, None, "reader"),
            P(INDEX, "reader"),
            P("reader"),
            P(INDEX, None, "reader"),
        ),
        out_specs=(
            P(INDEX, None),
            P(INDEX + ("reader",)),
            P(INDEX + ("reader",)),
            P(INDEX + ("reader",), None),
        ),
        check_vma=False,
    )
```

```python
import functools
import math

import jax
import jax.numpy as jnp
from jax import lax
from jax.experimental import pallas as pl
from jax.experimental.pallas import tpu as pltpu
from jax.sharding import Mesh, PartitionSpec as P

HEADS = 64
DH = 64
ANS = 16
EPSILON = 1e-06
SOFTMAX_TEMPER = 0.05
EXACT = lax.Precision.HIGHEST
INDEX = ("y", "zq", "zr", "core")
Z = ("zq", "zr")
Z_BY_CLASS = ("zr", "zq")
NEAR = ("reader", "y", "core")
LANES = 128
SLOT = 32
TILE = 256
N_OWNERS = 128
EARLY = (0, 1, 3)
LATE = 2


def shift(x, axis, step):
    size = lax.axis_size(axis)
    return lax.ppermute(x, axis, [((i + step) % size, i) for i in range(size)])


def send_all(x, axis):
    size = lax.axis_size(axis)
    return lax.all_to_all(jnp.broadcast_to(x[None], (size, *x.shape)), axis, 0, 0, tiled=True)


def halves(x):
    high = x.astype(jnp.bfloat16)
    return high, (x - high.astype(jnp.float32)).astype(jnp.bfloat16)


def dot32(a, b):
    return jnp.dot(a, b, preferred_element_type=jnp.float32)


def start_blocks(place, ahead, slot, tokens, weights, token_v, weight_v, sems):
    y, zr, core = place[0], place[1], place[2]
    copies = [pltpu.make_async_copy(tokens.at[(y + ahead) % 4], token_v.at[slot], sems.at[slot, 8])]
    for which in range(2):
        for residue in range(4):
            copies.append(
                pltpu.make_async_copy(
                    weights[which].at[pl.ds(4 * residue, 4)],
                    weight_v.at[slot, :, (zr + residue) % 4, (core + which) % 2],
                    sems.at[slot, 4 * which + residue],
                )
            )
    for copy in copies:
        copy.start()
    return copies


def early_keys_kernel(place, tokens, *refs):
    weights, (keys, token_v, weight_v, sems) = refs[:6], refs[6:]
    copies = [
        start_blocks(
            place, ahead, slot, tokens, weights[2 * slot : 2 * slot + 2], token_v, weight_v, sems
        )
        for slot, ahead in enumerate(EARLY)
    ]
    for slot in range(len(EARLY)):
        for copy in copies[slot]:
            copy.wait()

        @pl.loop(0, keys.shape[1] // TILE)
        def _(t):
            cols = pl.ds(pl.multiple_of(t * TILE, TILE), TILE)
            term = dot32(token_v[slot], weight_v[slot, :, :, :, :, cols].reshape(-1, TILE))
            if slot == 0:
                keys[:, cols] = term
            else:
                keys[:, cols] += term


def attention_kernel(place, tokens, *refs):
    weights, refs = refs[:2], refs[2:]
    early, dec, gain, live, scores, out, token_v, weight_v, column_v, sems = refs
    copies = start_blocks(place, LATE, 0, tokens, weights, token_v, weight_v, sems)
    group = dec.shape[0]
    n = live.shape[1]
    column_v[...] = jnp.zeros_like(column_v)
    for copy in copies:
        copy.wait()

    @pl.loop(0, early.shape[1] // TILE)
    def _(t):
        cols = pl.ds(pl.multiple_of(t * TILE, TILE), TILE)
        same = (
            lax.broadcasted_iota(jnp.int32, (TILE, TILE), 0) // DH
            == lax.broadcasted_iota(jnp.int32, (TILE, TILE), 1) // DH
        ).astype(jnp.bfloat16)
        mine = (
            lax.broadcasted_iota(jnp.int32, (TILE // DH * ANS, TILE), 0) // ANS
            == lax.broadcasted_iota(jnp.int32, (TILE // DH * ANS, TILE), 1) // DH
        )
        keys = early[:, cols] + dot32(
            token_v[0], weight_v[0, :, :, :, :, cols].reshape(-1, TILE)
        )
        high, low = halves(keys * keys)
        square = (dot32(high, same) + dot32(low, same)) / DH
        unit = (keys * lax.rsqrt(square + EPSILON) * gain[:, cols]).astype(jnp.bfloat16)
        for g in range(group):
            answer = dec[g, :, cols].astype(jnp.float32)
            answer = jnp.concatenate([answer] * (TILE // DH), axis=0)
            answer = jnp.where(mine, answer, 0.0).astype(jnp.bfloat16)
            similarity = lax.dot_general(
                answer,
                unit[g * n : (g + 1) * n],
                (((1,), (1,)), ((), ())),
                preferred_element_type=jnp.float32,
            ) / math.sqrt(DH)
            weight = jnp.where(live[g : g + 1, :] > 0, jnp.exp(similarity), 0.0)
            weight = weight / jnp.sum(weight, axis=1, keepdims=True)
            column_v[g : g + 1, :] += jnp.sum(weight, axis=0, keepdims=True)

    mass = jnp.zeros((8, LANES), jnp.float32)
    for g in range(group):
        column = jnp.broadcast_to(column_v[g : g + 1, :], (8, n))
        to = (
            lax.broadcasted_iota(jnp.int32, (n, LANES), 0) // 8 + g * SLOT
            == lax.broadcasted_iota(jnp.int32, (n, LANES), 1)
        ).astype(jnp.float32)
        mass += jnp.dot(column, to, precision=EXACT, preferred_element_type=jnp.float32)
    out[:, :LANES] = jnp.broadcast_to(mass[:1] / (HEADS * ANS), (out.shape[0], LANES))
    out[:, LANES:] = jnp.broadcast_to(scores[...], (out.shape[0], LANES))


def attention_packet(place, tokens, weights, dec, gain, live, scores):
    vmem = pl.BlockSpec(memory_space=pltpu.VMEM)
    anywhere = pl.BlockSpec(memory_space=pl.ANY)
    smem = pl.BlockSpec(memory_space=pltpu.SMEM)
    _, rows, width = tokens.shape

    def blocks(count):
        return [
            pltpu.VMEM((count, rows, width), jnp.bfloat16),
            pltpu.VMEM((count, 4, 4, 2, *weights[0][0].shape[1:]), jnp.bfloat16),
        ]

    def cost(count, size):
        return pl.CostEstimate(
            flops=2 * rows * count * width * width, bytes_accessed=size << 20, transcendentals=0
        )

    early = pl.pallas_call(
        early_keys_kernel,
        out_shape=jax.ShapeDtypeStruct((rows, width), jnp.float32),
        in_specs=[smem] + [anywhere] * 7,
        out_specs=vmem,
        scratch_shapes=blocks(3) + [pltpu.SemaphoreType.DMA((3, 9))],
        compiler_params=pltpu.CompilerParams(vmem_limit_bytes=48 << 20),
        cost_estimate=cost(3, 13),
        name="early_keys",
    )(place, tokens, *[block for ahead in EARLY for block in weights[ahead]])
    return pl.pallas_call(
        attention_kernel,
        out_shape=jax.ShapeDtypeStruct((32, 2 * LANES), jnp.float32),
        in_specs=[smem] + [anywhere] * 3 + [vmem] * 5,
        out_specs=vmem,
        scratch_shapes=blocks(1)
        + [pltpu.VMEM((8, live.shape[1]), jnp.float32), pltpu.SemaphoreType.DMA((1, 9))],
        compiler_params=pltpu.CompilerParams(vmem_limit_bytes=48 << 20),
        cost_estimate=cost(1, 6),
        name="attention",
    )(place, tokens, *weights[LATE], early, dec, gain, live, scores)


def scores_kernel(place, packed, proj, emb, chosen, state, slots, rows, unit, scale, ordered, unit_v, ids_v):
    shard, r = place[0], place[1]
    n_rows, width = emb.shape
    per_x = state.shape[0]
    cols = rows.shape[1]
    feats = packed[:, :, :width].reshape(4 * per_x, width)
    ordered[...] = lax.dot_general(
        chosen[...], feats, (((1,), (1,)), ((), ())), preferred_element_type=jnp.float32
    ).astype(jnp.bfloat16)

    lane = lax.broadcasted_iota(jnp.int32, (per_x, LANES), 1)
    spread = jnp.full((per_x, LANES), -1, jnp.int32)
    for x in range(4):
        coded = packed[8 * x : 8 * x + 8, :, width : width + LANES].reshape(per_x, LANES)
        coded = coded.astype(jnp.float32)
        ids = coded * 256 + pltpu.roll(coded, LANES // 2, 1)
        ids = ids.astype(jnp.int32) - shard * n_rows
        ids_v[x] = ids
        moved = ids if x == 0 else pltpu.roll(ids, SLOT * x, 1)
        spread = jnp.where((lane // SLOT == x) & (lane % SLOT < 20), moved, spread)
    slots[...] = spread

    vec = dot32(feats, proj[...])
    scale_all = lax.rsqrt(jnp.sum(vec * vec, axis=1, keepdims=True) + EPSILON)
    scale[...] = scale_all
    unit_all = vec * scale_all
    unit_v[...] = unit_all
    emb_all = emb[...]
    row_unit = emb_all * lax.rsqrt(jnp.sum(emb_all * emb_all, axis=1, keepdims=True) + EPSILON)
    for x in range(4):

        @pl.when(r == x)
        def _():
            rows[...] = row_unit[:, x * cols : (x + 1) * cols]
            unit[...] = unit_all[:, x * cols : (x + 1) * cols]

    share = unit_v[pl.ds(pl.multiple_of(r * per_x, per_x), per_x), :]
    found = (
        lax.dot_general(
            share,
            row_unit,
            (((1,), (1,)), ((), ())),
            precision=EXACT,
            preferred_element_type=jnp.float32,
        )
        / SOFTMAX_TEMPER
    )
    places = ids_v[r]
    row = lax.broadcasted_iota(jnp.int32, (per_x, n_rows), 1)
    total = jnp.where(lane == 20, jnp.max(found, axis=1, keepdims=True), 0.0)
    for k in range(20):
        picked = jnp.where(places[:, k : k + 1] == row, found, 0.0)
        total = jnp.where(lane == k, jnp.sum(picked, axis=1, keepdims=True), total)
    state[...] = total


def coef_kernel(packets, out):
    lane = lax.broadcasted_iota(jnp.int32, (8, LANES), 1)
    target = prob = fetched = jnp.zeros((8, LANES), jnp.float32)
    for x in range(4):
        target += packets[x, :, :LANES]
        scores = packets[x, :, LANES:]
        own = (lane // SLOT == x) & (lane % SLOT < 20)
        moved = scores if x == 0 else pltpu.roll(scores, SLOT * x, 1)
        prob += jnp.where(own, moved, 0.0)
        moved = pltpu.roll(scores, (SLOT * x + LANES // 2) % LANES, 1)
        fetched += jnp.where(own, moved, 0.0)
    gap = prob - target
    to = (
        lax.broadcasted_iota(jnp.int32, (LANES, LANES), 0) // SLOT * SLOT + 20
        == lax.broadcasted_iota(jnp.int32, (LANES, LANES), 1)
    ).astype(jnp.float32)
    along = jnp.dot(gap * fetched, to, precision=EXACT, preferred_element_type=jnp.float32)
    packed = gap / SOFTMAX_TEMPER + along / N_OWNERS
    out[...] = jnp.broadcast_to(packed[None], out.shape)


def gradient_kernel(coef, slot, rows, unit, scale, ordered, keep, send, matrix_v):
    n_rows = matrix_v.shape[1]
    blocks = coef.shape[0]

    @pl.loop(0, blocks // 8)
    def _(b):
        eight = pl.ds(pl.multiple_of(b * 8, 8), 8)
        row = lax.broadcasted_iota(jnp.int32, (8, n_rows), 1)
        values = coef[pl.ds(b // 2 + b % 2 * 64, 8, stride=8), :]
        places = slot[eight, :]
        for x in range(4):
            total = jnp.zeros((8, n_rows), jnp.float32)
            for k in range(SLOT * x, SLOT * x + 20):
                total += jnp.where(places[:, k : k + 1] == row, values[:, k : k + 1], 0.0)
            matrix_v[pl.ds(pl.multiple_of(x * blocks + b * 8, 8), 8), :] = total

    along_all = jnp.concatenate([coef[pl.ds(p, 16, stride=8), :] for p in range(8)], axis=0)
    row_high, row_low = halves(rows[...])
    parts_high, parts_low = [], []
    for x in range(4):
        mine = slice(x * blocks, (x + 1) * blocks)
        high, low = halves(matrix_v[mine, :])
        part = dot32(high, row_high) + (dot32(high, row_low) + dot32(low, row_high))
        along = along_all[:, SLOT * x + 20 : SLOT * x + 21]
        part = (part - unit[mine, :] * along) * scale[mine, :]
        high, low = halves(part)
        parts_high.append(high)
        parts_low.append(low)
    high, low = jnp.concatenate(parts_high, axis=0), jnp.concatenate(parts_low, axis=0)
    half = keep.shape[0]
    keep[...] = dot32(ordered[:half, :], high) + dot32(ordered[:half, :], low)
    send[...] = dot32(ordered[half:, :], high) + dot32(ordered[half:, :], low)


def body(
    index_emb,
    query_feat,
    query_proj,
    passage_id,
    passage_len,
    enc_out,
    key_proj,
    key_gain,
    dec_query,
):
    y, zq, zr, core, r = (lax.axis_index(a) for a in (*INDEX, "reader"))
    ny, nz, ncore, nx = 4, 16, 2, 4
    z = zq * 4 + zr
    n_index = ny * nz * ncore
    n_pair = ny * ncore
    my_shard = (y * nz + z) * ncore + core
    shard_rows, width = index_emb.shape
    topk = passage_id.shape[1]

    group, _, plen, feats_here = enc_out.shape
    token_rows = group * topk * plen
    with jax.named_scope("gather_enc_out"):
        token_blocks = lax.all_gather(enc_out.reshape(token_rows, feats_here), "reader")

    width_here = key_proj.shape[1]
    ids_high = (passage_id // 256).astype(jnp.bfloat16)
    ids_low = (passage_id % 256).astype(jnp.bfloat16)
    gap = ((0, 0), (0, LANES // 2 - topk))
    coded = jnp.concatenate([query_feat, jnp.pad(ids_high, gap), jnp.pad(ids_low, gap)], axis=1)
    coded = jnp.pad(coded, ((0, 0), (0, width_here - coded.shape[1])))
    with jax.named_scope("gather_key_proj"):
        own = send_all(jnp.concatenate([key_proj, coded]), "zq")
        after, before = shift(own, Z, 1), shift(own, Z, -1)
        far = [shift(own[:2], Z, 2), shift(own[2:], Z, -2)]
        classes = (own, after, *far, before)
        own = jnp.concatenate([block[:, :-1] for block in classes])
        after, before = shift(own, "y", 1), shift(own, "y", -1)
        far = jnp.concatenate([shift(after[:8], "y", 1), shift(before[8:], "y", -1)])
        weights = [(block, shift(block, "core", 1)) for block in (own, after, far, before)]

    with jax.named_scope("gather_queries"):
        coded = jnp.concatenate([block[:, -1] for block in classes])
        coded = jnp.roll(coded.reshape(4, 4, width_here), zr, axis=0).reshape(nz, width_here)
        packed = send_all(coded[:, : width + LANES], NEAR)

    cols = width // nx
    six = width // n_index
    place = lax.broadcasted_iota(jnp.int32, (width, 1), 0)
    to_core, to_y = place // (ny * nz * six), place // (nz * six) % ny
    to_z, within = place // six % nz, place % six
    column = ((to_y * nz + to_z) * ncore + (to_core + core) % ncore) * six + within
    chosen = (lax.broadcasted_iota(jnp.int32, (1, width), 1) == column).astype(jnp.bfloat16)

    vmem = pl.BlockSpec(memory_space=pltpu.VMEM)
    with jax.named_scope("scores"):
        queries = n_index * nx
        state, slots, my_rows, my_unit, query_scale, ordered = pl.pallas_call(
            scores_kernel,
            out_shape=(
                jax.ShapeDtypeStruct((n_index, LANES), jnp.float32),
                jax.ShapeDtypeStruct((n_index, LANES), jnp.int32),
                jax.ShapeDtypeStruct((shard_rows, cols), jnp.float32),
                jax.ShapeDtypeStruct((queries, cols), jnp.float32),
                jax.ShapeDtypeStruct((queries, 1), jnp.float32),
                jax.ShapeDtypeStruct((width, queries), jnp.bfloat16),
            ),
            in_specs=[pl.BlockSpec(memory_space=pltpu.SMEM)] + [vmem] * 4,
            out_specs=(vmem,) * 6,
            scratch_shapes=[
                pltpu.VMEM((queries, width), jnp.float32),
                pltpu.VMEM((nx, n_index, LANES), jnp.int32),
            ],
            compiler_params=pltpu.CompilerParams(vmem_limit_bytes=48 << 20),
            cost_estimate=pl.CostEstimate(
                flops=4 << 30, bytes_accessed=8 << 20, transcendentals=0
            ),
            name="scores",
        )(jnp.stack([my_shard, r]).astype(jnp.int32), packed, query_proj, index_emb, chosen)

    def merge_all(x):
        lane = lax.broadcasted_iota(jnp.int32, x.shape[1:], x.ndim - 2)
        return jnp.where(lane < topk, jnp.sum(x, axis=0), jnp.max(x, axis=0))

    with jax.named_scope("reduce_scores"):
        state = state.reshape(n_pair, nz, LANES)
        state = merge_all(lax.all_to_all(state, ("y", "core"), 0, 0, tiled=True))
        state = merge_all(lax.all_to_all(state, Z_BY_CLASS, 0, 0, tiled=True))
        slab_best = state[topk : topk + 1]
        fetched = state[:topk]
    expo = jnp.exp(fetched)
    total = jnp.sum(expo)
    prob = expo / total
    log_prob = fetched - jnp.log(total)
    score_row = jnp.zeros((1, LANES), jnp.float32)
    score_row = score_row.at[0, :topk].set(prob).at[0, LANES // 2 : LANES // 2 + topk].set(fetched)

    with jax.named_scope("attention"):
        answer = dec_query.shape[1]
        heads_here = feats_here // DH
        decoded = dec_query.astype(jnp.float32).reshape(group, answer, heads_here, DH)
        dec_unit = (
            decoded * lax.rsqrt(jnp.mean(decoded * decoded, axis=3, keepdims=True) + EPSILON)
        ).astype(jnp.bfloat16)
        positions = lax.broadcasted_iota(jnp.int32, (group, topk, plen), 2)
        live = (positions < passage_len[:, :, None]).reshape(group, topk * plen)
        packet = attention_packet(
            jnp.stack([y, zr, core]).astype(jnp.int32),
            token_blocks,
            weights,
            dec_unit.reshape(group, answer, feats_here),
            key_gain.astype(jnp.float32).reshape(1, feats_here),
            live.astype(jnp.float32),
            score_row,
        )

    with jax.named_scope("targets"):
        packets = lax.all_to_all(packet, NEAR, 0, 0, tiled=True).reshape(nx, n_pair, 2 * LANES)
        coef = pl.pallas_call(
            coef_kernel,
            out_shape=jax.ShapeDtypeStruct((nz, n_pair, LANES), jnp.float32),
            in_specs=[vmem],
            out_specs=vmem,
            name="coef",
        )(packets)
        coef = lax.all_to_all(coef, Z_BY_CLASS, 0, 0, tiled=True).reshape(n_index, LANES)

    with jax.named_scope("gradient"):
        part = jax.ShapeDtypeStruct((width // ncore, cols), jnp.float32)
        keep, send = pl.pallas_call(
            gradient_kernel,
            out_shape=(part, part),
            in_specs=[vmem] * 6,
            out_specs=(vmem, vmem),
            scratch_shapes=[pltpu.VMEM((queries, shard_rows), jnp.float32)],
            compiler_params=pltpu.CompilerParams(vmem_limit_bytes=40 << 20),
            name="gradient",
        )(coef, slots, my_rows, my_unit, query_scale, ordered)

    with jax.named_scope("reduce_gradient"):
        term = (keep + shift(send, "core", 1)).reshape(ny, nz * six, cols)
        term = jnp.sum(lax.all_to_all(term, "y", 0, 0, tiled=True), axis=0)
        term = term.reshape(nz, six, cols)
        term = jnp.sum(lax.all_to_all(term, Z, 0, 0, tiled=True), axis=0)
        grad_proj = send_all(term, "reader")
        grad_proj = grad_proj.transpose(1, 0, 2).reshape(six, width)

    mass = jnp.sum(lax.dynamic_index_in_dim(packets, y * ncore + core, 1, False), axis=0)
    my_target = lax.dynamic_slice_in_dim(mass, r * SLOT, topk, 0)
    log_target = jnp.log(my_target)
    retr_loss = jnp.sum(my_target * (log_target - log_prob))
    return (grad_proj, slab_best, retr_loss[None], log_target[None])


def solution(mesh):
    split = Mesh(mesh.devices.reshape(4, 4, 4, 2, 4), INDEX + ("reader",))
    return jax.shard_map(
        body,
        mesh=split,
        in_specs=(
            P(INDEX, None),
            P(INDEX + ("reader",), None),
            P(),
            P(INDEX + ("reader",), None),
            P(INDEX, None),
            P(INDEX, None, None, "reader"),
            P(INDEX, "reader"),
            P("reader"),
            P(INDEX, None, "reader"),
        ),
        out_specs=(
            P(INDEX, None),
            P(INDEX + ("reader",)),
            P(INDEX + ("reader",)),
            P(INDEX + ("reader",), None),
        ),
        check_vma=False,
    )
```

```python
import functools
import math

import jax
import jax.numpy as jnp
from jax import lax
from jax.experimental import pallas as pl
from jax.experimental.pallas import tpu as pltpu
from jax.sharding import Mesh, PartitionSpec as P

HEADS = 64
DH = 64
ANS = 16
EPSILON = 1e-06
SOFTMAX_TEMPER = 0.05
EXACT = lax.Precision.HIGHEST
INDEX = ("y", "zq", "zr", "core")
Z = ("zq", "zr")
NEAR = ("reader", "y", "core")
LANES = 128
SLOT = 32
TILE = 256
N_OWNERS = 128
EARLY = (0, 1, 3)
LATE = 2


def shift(x, axis, step):
    size = lax.axis_size(axis)
    return lax.ppermute(x, axis, [((i + step) % size, i) for i in range(size)])


def send_all(x, axis):
    size = lax.axis_size(axis)
    return lax.all_to_all(jnp.broadcast_to(x[None], (size, *x.shape)), axis, 0, 0, tiled=True)


def halves(x):
    high = x.astype(jnp.bfloat16)
    return high, (x - high.astype(jnp.float32)).astype(jnp.bfloat16)


def dot32(a, b):
    return jnp.dot(a, b, preferred_element_type=jnp.float32)


def start_blocks(place, ahead, slot, tokens, weights, token_v, weight_v, sems):
    y, core = place[0], place[1]
    copies = [pltpu.make_async_copy(tokens.at[(y + ahead) % 4], token_v.at[slot], sems.at[slot, 4])]
    for which in range(2):
        for half in range(2):
            copies.append(
                pltpu.make_async_copy(
                    weights[which][half],
                    weight_v.at[slot, :, (core + which) % 2, half],
                    sems.at[slot, 2 * which + half],
                )
            )
    for copy in copies:
        copy.start()
    return copies


def early_keys_kernel(place, tokens, *refs):
    weights, (keys, token_v, weight_v, sems) = refs[:4], refs[4:]
    copies = []
    for slot, ahead in enumerate(EARLY):
        blocks = [[weights[2 * which + half].at[slot] for half in range(2)] for which in range(2)]
        copies.append(start_blocks(place, ahead, slot, tokens, blocks, token_v, weight_v, sems))
    for slot in range(len(EARLY)):
        for copy in copies[slot]:
            copy.wait()

        @pl.loop(0, keys.shape[1] // TILE)
        def _(t):
            cols = pl.ds(pl.multiple_of(t * TILE, TILE), TILE)
            term = dot32(token_v[slot], weight_v[slot, :, :, :, :, cols].reshape(-1, TILE))
            if slot == 0:
                keys[:, cols] = term
            else:
                keys[:, cols] += term


def attention_kernel(place, tokens, *refs):
    weights, refs = refs[:2], refs[2:]
    early, dec, gain, live, scores, out, token_v, weight_v, column_v, sems = refs
    blocks = [[weights[which].at[half] for half in range(2)] for which in range(2)]
    copies = start_blocks(place, LATE, 0, tokens, blocks, token_v, weight_v, sems)
    group = dec.shape[0]
    n = live.shape[1]
    column_v[...] = jnp.zeros_like(column_v)
    for copy in copies:
        copy.wait()

    @pl.loop(0, early.shape[1] // TILE)
    def _(t):
        cols = pl.ds(pl.multiple_of(t * TILE, TILE), TILE)
        same = (
            lax.broadcasted_iota(jnp.int32, (TILE, TILE), 0) // DH
            == lax.broadcasted_iota(jnp.int32, (TILE, TILE), 1) // DH
        ).astype(jnp.bfloat16)
        mine = (
            lax.broadcasted_iota(jnp.int32, (TILE // DH * ANS, TILE), 0) // ANS
            == lax.broadcasted_iota(jnp.int32, (TILE // DH * ANS, TILE), 1) // DH
        )
        keys = early[:, cols] + dot32(
            token_v[0], weight_v[0, :, :, :, :, cols].reshape(-1, TILE)
        )
        high, low = halves(keys * keys)
        square = (dot32(high, same) + dot32(low, same)) / DH
        unit = (keys * lax.rsqrt(square + EPSILON) * gain[:, cols]).astype(jnp.bfloat16)
        for g in range(group):
            answer = dec[g, :, cols].astype(jnp.float32)
            answer = jnp.concatenate([answer] * (TILE // DH), axis=0)
            answer = jnp.where(mine, answer, 0.0).astype(jnp.bfloat16)
            similarity = lax.dot_general(
                answer,
                unit[g * n : (g + 1) * n],
                (((1,), (1,)), ((), ())),
                preferred_element_type=jnp.float32,
            ) / math.sqrt(DH)
            weight = jnp.where(live[g : g + 1, :] > 0, jnp.exp(similarity), 0.0)
            weight = weight / jnp.sum(weight, axis=1, keepdims=True)
            column_v[g : g + 1, :] += jnp.sum(weight, axis=0, keepdims=True)

    mass = jnp.zeros((8, LANES), jnp.float32)
    for g in range(group):
        column = jnp.broadcast_to(column_v[g : g + 1, :], (8, n))
        to = (
            lax.broadcasted_iota(jnp.int32, (n, LANES), 0) // 8 + g * SLOT
            == lax.broadcasted_iota(jnp.int32, (n, LANES), 1)
        ).astype(jnp.float32)
        mass += jnp.dot(column, to, precision=EXACT, preferred_element_type=jnp.float32)
    out[:, :LANES] = jnp.broadcast_to(mass[:1] / (HEADS * ANS), (out.shape[0], LANES))
    out[:, LANES:] = jnp.broadcast_to(scores[...], (out.shape[0], LANES))


def attention_packet(place, tokens, early_rows, late_rows, dec, gain, live, scores):
    vmem = pl.BlockSpec(memory_space=pltpu.VMEM)
    anywhere = pl.BlockSpec(memory_space=pl.ANY)
    smem = pl.BlockSpec(memory_space=pltpu.SMEM)
    _, rows, width = tokens.shape

    def blocks(count):
        return [
            pltpu.VMEM((count, rows, width), jnp.bfloat16),
            pltpu.VMEM((count, 16, 2, 2, *late_rows[0].shape[2:]), jnp.bfloat16),
        ]

    def cost(count, size):
        return pl.CostEstimate(
            flops=2 * rows * count * width * width, bytes_accessed=size << 20, transcendentals=0
        )

    early = pl.pallas_call(
        early_keys_kernel,
        out_shape=jax.ShapeDtypeStruct((rows, width), jnp.float32),
        in_specs=[smem] + [anywhere] * 5,
        out_specs=vmem,
        scratch_shapes=blocks(3) + [pltpu.SemaphoreType.DMA((3, 5))],
        compiler_params=pltpu.CompilerParams(vmem_limit_bytes=48 << 20),
        cost_estimate=cost(3, 13),
        name="early_keys",
    )(place, tokens, *early_rows)
    return pl.pallas_call(
        attention_kernel,
        out_shape=jax.ShapeDtypeStruct((32, 2 * LANES), jnp.float32),
        in_specs=[smem] + [anywhere] * 3 + [vmem] * 5,
        out_specs=vmem,
        scratch_shapes=blocks(1)
        + [pltpu.VMEM((8, live.shape[1]), jnp.float32), pltpu.SemaphoreType.DMA((1, 5))],
        compiler_params=pltpu.CompilerParams(vmem_limit_bytes=48 << 20),
        cost_estimate=cost(1, 6),
        name="attention",
    )(place, tokens, *late_rows, early, dec, gain, live, scores)


def scores_kernel(place, packed, proj, emb, chosen, state, slots, rows, unit, scale, ordered, unit_v, ids_v):
    shard, r = place[0], place[1]
    n_rows, width = emb.shape
    per_x = state.shape[0]
    cols = rows.shape[1]
    feats = packed[:, :, :width].reshape(4 * per_x, width)
    ordered[...] = lax.dot_general(
        chosen[...], feats, (((1,), (1,)), ((), ())), preferred_element_type=jnp.float32
    ).astype(jnp.bfloat16)

    lane = lax.broadcasted_iota(jnp.int32, (per_x, LANES), 1)
    spread = jnp.full((per_x, LANES), -1, jnp.int32)
    for x in range(4):
        coded = packed[8 * x : 8 * x + 8, :, width : width + LANES].reshape(per_x, LANES)
        coded = coded.astype(jnp.float32)
        ids = coded * 256 + pltpu.roll(coded, LANES // 2, 1)
        ids = ids.astype(jnp.int32) - shard * n_rows
        ids_v[x] = ids
        moved = ids if x == 0 else pltpu.roll(ids, SLOT * x, 1)
        spread = jnp.where((lane // SLOT == x) & (lane % SLOT < 20), moved, spread)
    slots[...] = spread

    vec = dot32(feats, proj[...])
    scale_all = lax.rsqrt(jnp.sum(vec * vec, axis=1, keepdims=True) + EPSILON)
    scale[...] = scale_all
    unit_all = vec * scale_all
    unit_v[...] = unit_all
    emb_all = emb[...]
    row_unit = emb_all * lax.rsqrt(jnp.sum(emb_all * emb_all, axis=1, keepdims=True) + EPSILON)
    for x in range(4):

        @pl.when(r == x)
        def _():
            rows[...] = row_unit[:, x * cols : (x + 1) * cols]
            unit[...] = unit_all[:, x * cols : (x + 1) * cols]

    share = unit_v[pl.ds(pl.multiple_of(r * per_x, per_x), per_x), :]
    found = (
        lax.dot_general(
            share,
            row_unit,
            (((1,), (1,)), ((), ())),
            precision=EXACT,
            preferred_element_type=jnp.float32,
        )
        / SOFTMAX_TEMPER
    )
    places = ids_v[r]
    row = lax.broadcasted_iota(jnp.int32, (per_x, n_rows), 1)
    total = jnp.where(lane == 20, jnp.max(found, axis=1, keepdims=True), 0.0)
    for k in range(20):
        picked = jnp.where(places[:, k : k + 1] == row, found, 0.0)
        total = jnp.where(lane == k, jnp.sum(picked, axis=1, keepdims=True), total)
    state[...] = total


def coef_kernel(packets, out):
    lane = lax.broadcasted_iota(jnp.int32, (8, LANES), 1)
    target = prob = fetched = jnp.zeros((8, LANES), jnp.float32)
    for x in range(4):
        target += packets[x, :, :LANES]
        scores = packets[x, :, LANES:]
        own = (lane // SLOT == x) & (lane % SLOT < 20)
        moved = scores if x == 0 else pltpu.roll(scores, SLOT * x, 1)
        prob += jnp.where(own, moved, 0.0)
        moved = pltpu.roll(scores, (SLOT * x + LANES // 2) % LANES, 1)
        fetched += jnp.where(own, moved, 0.0)
    gap = prob - target
    to = (
        lax.broadcasted_iota(jnp.int32, (LANES, LANES), 0) // SLOT * SLOT + 20
        == lax.broadcasted_iota(jnp.int32, (LANES, LANES), 1)
    ).astype(jnp.float32)
    along = jnp.dot(gap * fetched, to, precision=EXACT, preferred_element_type=jnp.float32)
    packed = gap / SOFTMAX_TEMPER + along / N_OWNERS
    out[...] = jnp.broadcast_to(packed[None], out.shape)


def gradient_kernel(coef, slot, *refs):
    far, (keep, send, matrix_v), near, sems = refs[:4], refs[4:7], refs[7:11], refs[11]
    copies = [pltpu.make_async_copy(a, b, sems.at[i]) for i, (a, b) in enumerate(zip(far, near))]
    for copy in copies:
        copy.start()
    rows, unit, scale, ordered = near
    n_rows = matrix_v.shape[1]
    blocks = coef.shape[0]

    @pl.loop(0, blocks // 8)
    def _(b):
        eight = pl.ds(pl.multiple_of(b * 8, 8), 8)
        row = lax.broadcasted_iota(jnp.int32, (8, n_rows), 1)
        values = coef[pl.ds(b // 2 + b % 2 * 64, 8, stride=8), :]
        places = slot[eight, :]
        for x in range(4):
            total = jnp.zeros((8, n_rows), jnp.float32)
            for k in range(SLOT * x, SLOT * x + 20):
                total += jnp.where(places[:, k : k + 1] == row, values[:, k : k + 1], 0.0)
            matrix_v[pl.ds(pl.multiple_of(x * blocks + b * 8, 8), 8), :] = total

    for copy in copies:
        copy.wait()
    along_all = jnp.concatenate([coef[pl.ds(p, 16, stride=8), :] for p in range(8)], axis=0)
    row_high, row_low = halves(rows[...])
    parts_high, parts_low = [], []
    for x in range(4):
        mine = slice(x * blocks, (x + 1) * blocks)
        high, low = halves(matrix_v[mine, :])
        part = dot32(high, row_high) + (dot32(high, row_low) + dot32(low, row_high))
        along = along_all[:, SLOT * x + 20 : SLOT * x + 21]
        part = (part - unit[mine, :] * along) * scale[mine, :]
        high, low = halves(part)
        parts_high.append(high)
        parts_low.append(low)
    high, low = jnp.concatenate(parts_high, axis=0), jnp.concatenate(parts_low, axis=0)
    half = keep.shape[0]
    keep[...] = dot32(ordered[:half, :], high) + dot32(ordered[:half, :], low)
    send[...] = dot32(ordered[half:, :], high) + dot32(ordered[half:, :], low)


def body(
    index_emb,
    query_feat,
    query_proj,
    passage_id,
    passage_len,
    enc_out,
    key_proj,
    key_gain,
    dec_query,
):
    y, zq, zr, core, r = (lax.axis_index(a) for a in (*INDEX, "reader"))
    ny, nz, ncore, nx = 4, 16, 2, 4
    z = zq * 4 + zr
    n_index = ny * nz * ncore
    n_pair = ny * ncore
    my_shard = (y * nz + z) * ncore + core
    shard_rows, width = index_emb.shape
    topk = passage_id.shape[1]

    group, _, plen, feats_here = enc_out.shape
    token_rows = group * topk * plen
    with jax.named_scope("gather_enc_out"):
        token_blocks = lax.all_gather(enc_out.reshape(token_rows, feats_here), "reader")

    half_rows, width_here = key_proj.shape[0] // 2, key_proj.shape[1]
    ids_high = (passage_id // 256).astype(jnp.bfloat16)
    ids_low = (passage_id % 256).astype(jnp.bfloat16)
    gap = ((0, 0), (0, LANES // 2 - topk))
    coded = jnp.concatenate([query_feat, jnp.pad(ids_high, gap), jnp.pad(ids_low, gap)], axis=1)
    coded = jnp.pad(coded, ((0, 0), (0, width_here - coded.shape[1]))).reshape(half_rows, -1)
    beside = coded.shape[1]
    coded = jnp.pad(coded, ((0, 0), (0, LANES - beside)))
    with jax.named_scope("gather_key_proj"):
        first = send_all(jnp.concatenate([key_proj[:half_rows], coded], axis=1), Z)
        coded = first[:, :, width_here : width_here + beside].reshape(nz, width_here)
        early_rows, late_rows = [], []
        for own in (first[:, :, :width_here], send_all(key_proj[half_rows:], Z)):
            after, before = shift(own, "y", 1), shift(own, "y", -1)
            early_rows.append(jnp.stack([own, after, before]))
            late_rows += [shift(after[:8], "y", 1), shift(before[8:], "y", -1)]
        late_rows = jnp.concatenate(late_rows).reshape(2, *first.shape[:2], width_here)
        early_rows += [shift(rows, "core", 1) for rows in early_rows]
        late_rows = [late_rows, shift(late_rows, "core", 1)]

    with jax.named_scope("gather_queries"):
        packed = send_all(coded[:, : width + LANES], NEAR)

    cols = width // nx
    six = width // n_index
    place = lax.broadcasted_iota(jnp.int32, (width, 1), 0)
    to_core, to_y = place // (ny * nz * six), place // (nz * six) % ny
    to_z, within = place // six % nz, place % six
    column = ((to_y * nz + to_z) * ncore + (to_core + core) % ncore) * six + within
    chosen = (lax.broadcasted_iota(jnp.int32, (1, width), 1) == column).astype(jnp.bfloat16)

    vmem = pl.BlockSpec(memory_space=pltpu.VMEM)
    with jax.named_scope("scores"):
        queries = n_index * nx
        state, slots, my_rows, my_unit, query_scale, ordered = pl.pallas_call(
            scores_kernel,
            out_shape=(
                jax.ShapeDtypeStruct((n_index, LANES), jnp.float32),
                jax.ShapeDtypeStruct((n_index, LANES), jnp.int32),
                jax.ShapeDtypeStruct((shard_rows, cols), jnp.float32),
                jax.ShapeDtypeStruct((queries, cols), jnp.float32),
                jax.ShapeDtypeStruct((queries, 1), jnp.float32),
                jax.ShapeDtypeStruct((width, queries), jnp.bfloat16),
            ),
            in_specs=[pl.BlockSpec(memory_space=pltpu.SMEM)] + [vmem] * 4,
            out_specs=(vmem,) * 6,
            scratch_shapes=[
                pltpu.VMEM((queries, width), jnp.float32),
                pltpu.VMEM((nx, n_index, LANES), jnp.int32),
            ],
            compiler_params=pltpu.CompilerParams(vmem_limit_bytes=48 << 20),
            cost_estimate=pl.CostEstimate(
                flops=4 << 30, bytes_accessed=8 << 20, transcendentals=0
            ),
            name="scores",
        )(jnp.stack([my_shard, r]).astype(jnp.int32), packed, query_proj, index_emb, chosen)

    def merge_all(x):
        lane = lax.broadcasted_iota(jnp.int32, x.shape[1:], x.ndim - 2)
        return jnp.where(lane < topk, jnp.sum(x, axis=0), jnp.max(x, axis=0))

    with jax.named_scope("reduce_scores"):
        state = state.reshape(n_pair, nz, LANES)
        state = merge_all(lax.all_to_all(state, ("y", "core"), 0, 0, tiled=True))
        state = merge_all(lax.all_to_all(state, Z, 0, 0, tiled=True))
        slab_best = state[topk : topk + 1]
        fetched = state[:topk]
    expo = jnp.exp(fetched)
    total = jnp.sum(expo)
    prob = expo / total
    log_prob = fetched - jnp.log(total)
    score_row = jnp.zeros((1, LANES), jnp.float32)
    score_row = score_row.at[0, :topk].set(prob).at[0, LANES // 2 : LANES // 2 + topk].set(fetched)

    with jax.named_scope("attention"):
        answer = dec_query.shape[1]
        heads_here = feats_here // DH
        decoded = dec_query.astype(jnp.float32).reshape(group, answer, heads_here, DH)
        dec_unit = (
            decoded * lax.rsqrt(jnp.mean(decoded * decoded, axis=3, keepdims=True) + EPSILON)
        ).astype(jnp.bfloat16)
        positions = lax.broadcasted_iota(jnp.int32, (group, topk, plen), 2)
        live = (positions < passage_len[:, :, None]).reshape(group, topk * plen)
        packet = attention_packet(
            jnp.stack([y, core]).astype(jnp.int32),
            token_blocks,
            early_rows,
            late_rows,
            dec_unit.reshape(group, answer, feats_here),
            key_gain.astype(jnp.float32).reshape(1, feats_here),
            live.astype(jnp.float32),
            score_row,
        )

    with jax.named_scope("targets"):
        packets = lax.all_to_all(packet, NEAR, 0, 0, tiled=True).reshape(nx, n_pair, 2 * LANES)
        coef = pl.pallas_call(
            coef_kernel,
            out_shape=jax.ShapeDtypeStruct((nz, n_pair, LANES), jnp.float32),
            in_specs=[vmem],
            out_specs=vmem,
            name="coef",
        )(packets)
        coef = lax.all_to_all(coef, Z, 0, 0, tiled=True).reshape(n_index, LANES)

    with jax.named_scope("gradient"):
        part = jax.ShapeDtypeStruct((width // ncore, cols), jnp.float32)
        keep, send = pl.pallas_call(
            gradient_kernel,
            out_shape=(part, part),
            in_specs=[vmem] * 2 + [pl.BlockSpec(memory_space=pl.ANY)] * 4,
            out_specs=(vmem, vmem),
            scratch_shapes=[
                pltpu.VMEM((queries, shard_rows), jnp.float32),
                *[pltpu.VMEM(x.shape, x.dtype) for x in (my_rows, my_unit, query_scale, ordered)],
                pltpu.SemaphoreType.DMA((4,)),
            ],
            compiler_params=pltpu.CompilerParams(vmem_limit_bytes=40 << 20),
            name="gradient",
        )(coef, slots, my_rows, my_unit, query_scale, ordered)

    with jax.named_scope("reduce_gradient"):
        term = (keep + shift(send, "core", 1)).reshape(ny, nz * six, cols)
        term = jnp.sum(lax.all_to_all(term, "y", 0, 0, tiled=True), axis=0)
        term = term.reshape(nz, six, cols)
        term = jnp.sum(lax.all_to_all(term, Z, 0, 0, tiled=True), axis=0)
        grad_proj = send_all(term, "reader")
        grad_proj = grad_proj.transpose(1, 0, 2).reshape(six, width)

    mass = jnp.sum(lax.dynamic_index_in_dim(packets, y * ncore + core, 1, False), axis=0)
    my_target = lax.dynamic_slice_in_dim(mass, r * SLOT, topk, 0)
    log_target = jnp.log(my_target)
    retr_loss = jnp.sum(my_target * (log_target - log_prob))
    return (grad_proj, slab_best, retr_loss[None], log_target[None])


def solution(mesh):
    split = Mesh(mesh.devices.reshape(4, 4, 4, 2, 4), INDEX + ("reader",))
    return jax.shard_map(
        body,
        mesh=split,
        in_specs=(
            P(INDEX, None),
            P(INDEX + ("reader",), None),
            P(),
            P(INDEX + ("reader",), None),
            P(INDEX, None),
            P(INDEX, None, None, "reader"),
            P(INDEX, "reader"),
            P("reader"),
            P(INDEX, None, "reader"),
        ),
        out_specs=(
            P(INDEX, None),
            P(INDEX + ("reader",)),
            P(INDEX + ("reader",)),
            P(INDEX + ("reader",), None),
        ),
        check_vma=False,
    )
```

```python
import functools
import math

import jax
import jax.numpy as jnp
from jax import lax
from jax.experimental import pallas as pl
from jax.experimental.pallas import tpu as pltpu
from jax.sharding import Mesh, PartitionSpec as P

HEADS = 64
DH = 64
ANS = 16
EPSILON = 1e-06
SOFTMAX_TEMPER = 0.05
EXACT = lax.Precision.HIGHEST
INDEX = ("y", "zq", "zr", "core")
Z = ("zq", "zr")
NEAR = ("reader", "y", "core")
LANES = 128
SLOT = 32
TILE = 256
N_OWNERS = 128
EARLY = (0, 1, 3)
LATE = 2


def shift(x, axis, step):
    size = lax.axis_size(axis)
    return lax.ppermute(x, axis, [((i + step) % size, i) for i in range(size)])


def send_all(x, axis):
    size = lax.axis_size(axis)
    return lax.all_to_all(jnp.broadcast_to(x[None], (size, *x.shape)), axis, 0, 0, tiled=True)


def halves(x):
    high = x.astype(jnp.bfloat16)
    return high, (x - high.astype(jnp.float32)).astype(jnp.bfloat16)


def dot32(a, b):
    return jnp.dot(a, b, preferred_element_type=jnp.float32)


def token_copies(r, chunk, tokens, target, sems):
    own, after, far_low, far_high, before = tokens
    half = target.shape[0] // 2
    low, high = target.at[pl.ds(0, half)], target.at[pl.ds(half, half)]
    for j, block in enumerate((own, after, None, before)):

        @pl.when((r + j) % 4 == chunk)
        def _():
            first = far_low if block is None else block.at[pl.ds(0, half)]
            second = far_high if block is None else block.at[pl.ds(half, half)]
            pltpu.make_async_copy(first, low, sems.at[0]).start()
            pltpu.make_async_copy(second, high, sems.at[1]).start()

    return [
        pltpu.make_async_copy(low, low, sems.at[0]),
        pltpu.make_async_copy(high, high, sems.at[1]),
    ]


def row_copies(core, own, other, target, sems):
    copies = [
        pltpu.make_async_copy(own, target.at[:, core], sems.at[0]),
        pltpu.make_async_copy(other, target.at[:, 1 - core], sems.at[1]),
    ]
    for copy in copies:
        copy.start()
    return copies


def early_keys_kernel(place, *refs):
    tokens, (own, other), (keys, token_v, weight_v, sems) = refs[:5], refs[5:7], refs[7:]
    y, core, r = place[0], place[1], place[2]
    copies = []
    for slot, ahead in enumerate(EARLY):
        waits = row_copies(core, own.at[slot], other.at[slot], weight_v.at[slot], sems.at[slot])
        target = token_v.at[slot]
        waits += token_copies(r, (y + ahead) % 4, tokens, target, sems.at[3 + slot])
        copies.append(waits)
    for slot in range(len(EARLY)):
        for copy in copies[slot]:
            copy.wait()

        @pl.loop(0, keys.shape[1] // TILE)
        def _(t):
            cols = pl.ds(pl.multiple_of(t * TILE, TILE), TILE)
            term = dot32(token_v[slot], weight_v[slot, :, :, :, cols].reshape(-1, TILE))
            if slot == 0:
                keys[:, cols] = term
            else:
                keys[:, cols] += term


def attend(keys, offset, dec, gain, live, column_v):
    group, n = dec.shape[0], live.shape[1]
    cols = pl.ds(pl.multiple_of(offset, TILE), TILE)
    same = (
        lax.broadcasted_iota(jnp.int32, (TILE, TILE), 0) // DH
        == lax.broadcasted_iota(jnp.int32, (TILE, TILE), 1) // DH
    ).astype(jnp.bfloat16)
    mine = (
        lax.broadcasted_iota(jnp.int32, (TILE // DH * ANS, TILE), 0) // ANS
        == lax.broadcasted_iota(jnp.int32, (TILE // DH * ANS, TILE), 1) // DH
    )
    high, low = halves(keys * keys)
    square = (dot32(high, same) + dot32(low, same)) / DH
    unit = (keys * lax.rsqrt(square + EPSILON) * gain[:, cols]).astype(jnp.bfloat16)
    for g in range(group):
        answer = dec[g, :, cols].astype(jnp.float32)
        answer = jnp.concatenate([answer] * (TILE // DH), axis=0)
        answer = jnp.where(mine, answer, 0.0).astype(jnp.bfloat16)
        similarity = lax.dot_general(
            answer,
            unit[g * n : (g + 1) * n],
            (((1,), (1,)), ((), ())),
            preferred_element_type=jnp.float32,
        ) / math.sqrt(DH)
        weight = jnp.where(live[g : g + 1, :] > 0, jnp.exp(similarity), 0.0)
        weight = weight / jnp.sum(weight, axis=1, keepdims=True)
        column_v[g : g + 1, :] += jnp.sum(weight, axis=0, keepdims=True)


def whole_heads_kernel(place, *refs):
    tokens, refs = refs[:5], refs[5:]
    rows, dec, gain, live, columns, token_v, weight_v, sems = refs
    r = place[2]
    copies = []
    for c in range(4):
        copy = pltpu.make_async_copy(rows.at[c], weight_v.at[c], sems.at[c, 2])
        copy.start()
        copies += [copy] + token_copies(r, c, tokens, token_v.at[c], sems.at[c])
    columns[...] = jnp.zeros_like(columns)
    for copy in copies:
        copy.wait()

    @pl.loop(0, weight_v.shape[2] // TILE)
    def _(t):
        cols = pl.ds(pl.multiple_of(t * TILE, TILE), TILE)
        keys = dot32(token_v[0], weight_v[0, :, cols])
        for c in range(1, 4):
            keys += dot32(token_v[c], weight_v[c, :, cols])
        attend(keys, weight_v.shape[2] + t * TILE, dec, gain, live, columns)


def late_heads_kernel(place, *refs):
    tokens, (own, other), refs = refs[:5], refs[5:7], refs[7:]
    early, columns, dec, gain, live, scores, out, token_v, weight_v, column_v, sems = refs
    y, core, r = place[0], place[1], place[2]
    copies = row_copies(core, own, other, weight_v, sems.at[0])
    copies += token_copies(r, (y + LATE) % 4, tokens, token_v, sems.at[1])
    column_v[...] = columns[...]
    for copy in copies:
        copy.wait()

    @pl.loop(0, early.shape[1] // TILE)
    def _(t):
        cols = pl.ds(pl.multiple_of(t * TILE, TILE), TILE)
        keys = early[:, cols] + dot32(token_v[...], weight_v[:, :, :, cols].reshape(-1, TILE))
        attend(keys, t * TILE, dec, gain, live, column_v)

    n = live.shape[1]
    mass = jnp.zeros((8, LANES), jnp.float32)
    for g in range(dec.shape[0]):
        column = jnp.broadcast_to(column_v[g : g + 1, :], (8, n))
        to = (
            lax.broadcasted_iota(jnp.int32, (n, LANES), 0) // 8 + g * SLOT
            == lax.broadcasted_iota(jnp.int32, (n, LANES), 1)
        ).astype(jnp.float32)
        mass += jnp.dot(column, to, precision=EXACT, preferred_element_type=jnp.float32)
    out[:, :LANES] = jnp.broadcast_to(mass[:1] / (HEADS * ANS), (out.shape[0], LANES))
    out[:, LANES:] = jnp.broadcast_to(scores[...], (out.shape[0], LANES))


def attention_packet(place, tokens, early_rows, late_rows, whole_rows, dec, gain, live, scores):
    vmem = pl.BlockSpec(memory_space=pltpu.VMEM)
    anywhere = pl.BlockSpec(memory_space=pl.ANY)
    smem = pl.BlockSpec(memory_space=pltpu.SMEM)
    rows, width = tokens[0].shape
    _, nz, chip_rows, half = early_rows[0].shape
    block = (nz, 2, chip_rows, half)
    params = pltpu.CompilerParams(vmem_limit_bytes=48 << 20)

    def cost(count, size):
        return pl.CostEstimate(
            flops=2 * rows * count * width * half, bytes_accessed=size << 20, transcendentals=0
        )

    early = pl.pallas_call(
        early_keys_kernel,
        out_shape=jax.ShapeDtypeStruct((rows, half), jnp.float32),
        in_specs=[smem] + [anywhere] * 7,
        out_specs=vmem,
        scratch_shapes=[
            pltpu.VMEM((3, rows, width), jnp.bfloat16),
            pltpu.VMEM((3, *block), jnp.bfloat16),
            pltpu.SemaphoreType.DMA((6, 2)),
        ],
        compiler_params=params,
        cost_estimate=cost(3, 8),
        name="early_keys",
    )(place, *tokens, *early_rows)
    columns = pl.pallas_call(
        whole_heads_kernel,
        out_shape=jax.ShapeDtypeStruct((8, live.shape[1]), jnp.float32),
        in_specs=[smem] + [anywhere] * 6 + [vmem] * 3,
        out_specs=vmem,
        scratch_shapes=[
            pltpu.VMEM((4, rows, width), jnp.bfloat16),
            pltpu.VMEM((4, width, half), jnp.bfloat16),
            pltpu.SemaphoreType.DMA((4, 3)),
        ],
        compiler_params=params,
        cost_estimate=cost(4, 9),
        name="whole_heads",
    )(place, *tokens, whole_rows, dec, gain, live)
    return pl.pallas_call(
        late_heads_kernel,
        out_shape=jax.ShapeDtypeStruct((32, 2 * LANES), jnp.float32),
        in_specs=[smem] + [anywhere] * 7 + [vmem] * 6,
        out_specs=vmem,
        scratch_shapes=[
            pltpu.VMEM((rows, width), jnp.bfloat16),
            pltpu.VMEM(block, jnp.bfloat16),
            pltpu.VMEM((8, live.shape[1]), jnp.float32),
            pltpu.SemaphoreType.DMA((2, 2)),
        ],
        compiler_params=params,
        cost_estimate=cost(1, 4),
        name="late_heads",
    )(place, *tokens, *late_rows, early, columns, dec, gain, live, scores)


def scores_kernel(place, packed, proj, emb, chosen, state, slots, rows, unit, scale, ordered, unit_v, ids_v):
    shard, r = place[0], place[1]
    n_rows, width = emb.shape
    per_x = state.shape[0]
    cols = rows.shape[1]
    feats = packed[:, :, :width].reshape(4 * per_x, width)
    ordered[...] = lax.dot_general(
        chosen[...], feats, (((1,), (1,)), ((), ())), preferred_element_type=jnp.float32
    ).astype(jnp.bfloat16)

    lane = lax.broadcasted_iota(jnp.int32, (per_x, LANES), 1)
    spread = jnp.full((per_x, LANES), -1, jnp.int32)
    for x in range(4):
        coded = packed[8 * x : 8 * x + 8, :, width : width + LANES].reshape(per_x, LANES)
        coded = coded.astype(jnp.float32)
        ids = coded * 256 + pltpu.roll(coded, LANES // 2, 1)
        ids = ids.astype(jnp.int32) - shard * n_rows
        ids_v[x] = ids
        moved = ids if x == 0 else pltpu.roll(ids, SLOT * x, 1)
        spread = jnp.where((lane // SLOT == x) & (lane % SLOT < 20), moved, spread)
    slots[...] = spread

    vec = dot32(feats, proj[...])
    scale_all = lax.rsqrt(jnp.sum(vec * vec, axis=1, keepdims=True) + EPSILON)
    scale[...] = scale_all
    unit_all = vec * scale_all
    unit_v[...] = unit_all
    emb_all = emb[...]
    row_unit = emb_all * lax.rsqrt(jnp.sum(emb_all * emb_all, axis=1, keepdims=True) + EPSILON)
    for x in range(4):

        @pl.when(r == x)
        def _():
            rows[...] = row_unit[:, x * cols : (x + 1) * cols]
            unit[...] = unit_all[:, x * cols : (x + 1) * cols]

    share = unit_v[pl.ds(pl.multiple_of(r * per_x, per_x), per_x), :]
    found = (
        lax.dot_general(
            share,
            row_unit,
            (((1,), (1,)), ((), ())),
            precision=EXACT,
            preferred_element_type=jnp.float32,
        )
        / SOFTMAX_TEMPER
    )
    places = ids_v[r]
    row = lax.broadcasted_iota(jnp.int32, (per_x, n_rows), 1)
    total = jnp.where(lane == 20, jnp.max(found, axis=1, keepdims=True), 0.0)
    for k in range(20):
        picked = jnp.where(places[:, k : k + 1] == row, found, 0.0)
        total = jnp.where(lane == k, jnp.sum(picked, axis=1, keepdims=True), total)
    state[...] = total


def coef_kernel(packets, out):
    lane = lax.broadcasted_iota(jnp.int32, (8, LANES), 1)
    target = prob = fetched = jnp.zeros((8, LANES), jnp.float32)
    for x in range(4):
        target += packets[x, :, :LANES]
        scores = packets[x, :, LANES:]
        own = (lane // SLOT == x) & (lane % SLOT < 20)
        moved = scores if x == 0 else pltpu.roll(scores, SLOT * x, 1)
        prob += jnp.where(own, moved, 0.0)
        moved = pltpu.roll(scores, (SLOT * x + LANES // 2) % LANES, 1)
        fetched += jnp.where(own, moved, 0.0)
    gap = prob - target
    to = (
        lax.broadcasted_iota(jnp.int32, (LANES, LANES), 0) // SLOT * SLOT + 20
        == lax.broadcasted_iota(jnp.int32, (LANES, LANES), 1)
    ).astype(jnp.float32)
    along = jnp.dot(gap * fetched, to, precision=EXACT, preferred_element_type=jnp.float32)
    packed = gap / SOFTMAX_TEMPER + along / N_OWNERS
    out[...] = jnp.broadcast_to(packed[None], out.shape)


def gradient_kernel(coef, slot, *refs):
    far, (keep, send, matrix_v), near, sems = refs[:4], refs[4:7], refs[7:11], refs[11]
    copies = [pltpu.make_async_copy(a, b, sems.at[i]) for i, (a, b) in enumerate(zip(far, near))]
    for copy in copies:
        copy.start()
    rows, unit, scale, ordered = near
    n_rows = matrix_v.shape[1]
    blocks = coef.shape[0]

    @pl.loop(0, blocks // 8)
    def _(b):
        eight = pl.ds(pl.multiple_of(b * 8, 8), 8)
        row = lax.broadcasted_iota(jnp.int32, (8, n_rows), 1)
        values = coef[pl.ds(b // 2 + b % 2 * 64, 8, stride=8), :]
        places = slot[eight, :]
        for x in range(4):
            total = jnp.zeros((8, n_rows), jnp.float32)
            for k in range(SLOT * x, SLOT * x + 20):
                total += jnp.where(places[:, k : k + 1] == row, values[:, k : k + 1], 0.0)
            matrix_v[pl.ds(pl.multiple_of(x * blocks + b * 8, 8), 8), :] = total

    for copy in copies:
        copy.wait()
    along_all = jnp.concatenate([coef[pl.ds(p, 16, stride=8), :] for p in range(8)], axis=0)
    row_high, row_low = halves(rows[...])
    parts_high, parts_low = [], []
    for x in range(4):
        mine = slice(x * blocks, (x + 1) * blocks)
        high, low = halves(matrix_v[mine, :])
        part = dot32(high, row_high) + (dot32(high, row_low) + dot32(low, row_high))
        along = along_all[:, SLOT * x + 20 : SLOT * x + 21]
        part = (part - unit[mine, :] * along) * scale[mine, :]
        high, low = halves(part)
        parts_high.append(high)
        parts_low.append(low)
    high, low = jnp.concatenate(parts_high, axis=0), jnp.concatenate(parts_low, axis=0)
    half = keep.shape[0]
    keep[...] = dot32(ordered[:half, :], high) + dot32(ordered[:half, :], low)
    send[...] = dot32(ordered[half:, :], high) + dot32(ordered[half:, :], low)


def body(
    index_emb,
    query_feat,
    query_proj,
    passage_id,
    passage_len,
    enc_out,
    key_proj,
    key_gain,
    dec_query,
):
    y, zq, zr, core, r = (lax.axis_index(a) for a in (*INDEX, "reader"))
    ny, nz, ncore, nx = 4, 16, 2, 4
    z = zq * 4 + zr
    n_index = ny * nz * ncore
    n_pair = ny * ncore
    my_shard = (y * nz + z) * ncore + core
    shard_rows, width = index_emb.shape
    topk = passage_id.shape[1]

    group, _, plen, feats_here = enc_out.shape
    token_rows = group * topk * plen
    with jax.named_scope("gather_enc_out"):
        own = enc_out.reshape(token_rows, feats_here)
        after, before = shift(own, "reader", 1), shift(own, "reader", -1)
        mid = token_rows // 2
        far_low, far_high = shift(after[:mid], "reader", 1), shift(before[mid:], "reader", -1)
        tokens = (own, after, far_low, far_high, before)

    rows_here, half = key_proj.shape[0], key_proj.shape[1] // 2
    ids_high = (passage_id // 256).astype(jnp.bfloat16)
    ids_low = (passage_id % 256).astype(jnp.bfloat16)
    gap = ((0, 0), (0, LANES // 2 - topk))
    coded = jnp.concatenate([query_feat, jnp.pad(ids_high, gap), jnp.pad(ids_low, gap)], axis=1)
    coded = jnp.pad(coded, ((0, 0), (0, -coded.shape[1] % (rows_here * 4)))).reshape(rows_here, -1)
    beside = coded.shape[1]
    coded = jnp.pad(coded, ((0, 0), (0, LANES - beside)))
    with jax.named_scope("gather_key_proj"):
        whole_rows = lax.all_gather(key_proj[:, half:], INDEX)
        whole_rows = whole_rows.reshape(ny, -1, half)
        first = send_all(jnp.concatenate([key_proj[:, :half], coded], axis=1), Z)
        coded = first[:, :, half : half + beside].reshape(nz, -1)
        own = first[:, :, :half]
        after, before = shift(own, "y", 1), shift(own, "y", -1)
        early_rows = jnp.stack([own, after, before])
        early_rows = [early_rows, shift(early_rows, "core", 1)]
        late_rows = jnp.concatenate([shift(after[:8], "y", 1), shift(before[8:], "y", -1)])
        late_rows = [late_rows, shift(late_rows, "core", 1)]

    with jax.named_scope("gather_queries"):
        packed = send_all(coded[:, : width + LANES], NEAR)

    cols = width // nx
    six = width // n_index
    place = lax.broadcasted_iota(jnp.int32, (width, 1), 0)
    to_core, to_y = place // (ny * nz * six), place // (nz * six) % ny
    to_z, within = place // six % nz, place % six
    column = ((to_y * nz + to_z) * ncore + (to_core + core) % ncore) * six + within
    chosen = (lax.broadcasted_iota(jnp.int32, (1, width), 1) == column).astype(jnp.bfloat16)

    vmem = pl.BlockSpec(memory_space=pltpu.VMEM)
    with jax.named_scope("scores"):
        queries = n_index * nx
        state, slots, my_rows, my_unit, query_scale, ordered = pl.pallas_call(
            scores_kernel,
            out_shape=(
                jax.ShapeDtypeStruct((n_index, LANES), jnp.float32),
                jax.ShapeDtypeStruct((n_index, LANES), jnp.int32),
                jax.ShapeDtypeStruct((shard_rows, cols), jnp.float32),
                jax.ShapeDtypeStruct((queries, cols), jnp.float32),
                jax.ShapeDtypeStruct((queries, 1), jnp.float32),
                jax.ShapeDtypeStruct((width, queries), jnp.bfloat16),
            ),
            in_specs=[pl.BlockSpec(memory_space=pltpu.SMEM)] + [vmem] * 4,
            out_specs=(vmem,) * 6,
            scratch_shapes=[
                pltpu.VMEM((queries, width), jnp.float32),
                pltpu.VMEM((nx, n_index, LANES), jnp.int32),
            ],
            compiler_params=pltpu.CompilerParams(vmem_limit_bytes=48 << 20),
            cost_estimate=pl.CostEstimate(
                flops=4 << 30, bytes_accessed=8 << 20, transcendentals=0
            ),
            name="scores",
        )(jnp.stack([my_shard, r]).astype(jnp.int32), packed, query_proj, index_emb, chosen)

    def merge_all(x):
        lane = lax.broadcasted_iota(jnp.int32, x.shape[1:], x.ndim - 2)
        return jnp.where(lane < topk, jnp.sum(x, axis=0), jnp.max(x, axis=0))

    with jax.named_scope("reduce_scores"):
        state = state.reshape(n_pair, nz, LANES)
        state = merge_all(lax.all_to_all(state, ("y", "core"), 0, 0, tiled=True))
        state = merge_all(lax.all_to_all(state, Z, 0, 0, tiled=True))
        slab_best = state[topk : topk + 1]
        fetched = state[:topk]
    expo = jnp.exp(fetched)
    total = jnp.sum(expo)
    prob = expo / total
    log_prob = fetched - jnp.log(total)
    score_row = jnp.zeros((1, LANES), jnp.float32)
    score_row = score_row.at[0, :topk].set(prob).at[0, LANES // 2 : LANES // 2 + topk].set(fetched)

    with jax.named_scope("attention"):
        answer = dec_query.shape[1]
        heads_here = feats_here // DH
        decoded = dec_query.astype(jnp.float32).reshape(group, answer, heads_here, DH)
        dec_unit = (
            decoded * lax.rsqrt(jnp.mean(decoded * decoded, axis=3, keepdims=True) + EPSILON)
        ).astype(jnp.bfloat16)
        positions = lax.broadcasted_iota(jnp.int32, (group, topk, plen), 2)
        live = (positions < passage_len[:, :, None]).reshape(group, topk * plen)
        packet = attention_packet(
            jnp.stack([y, core, r]).astype(jnp.int32),
            tokens,
            early_rows,
            late_rows,
            whole_rows,
            dec_unit.reshape(group, answer, feats_here),
            key_gain.astype(jnp.float32).reshape(1, feats_here),
            live.astype(jnp.float32),
            score_row,
        )

    with jax.named_scope("targets"):
        packets = lax.all_to_all(packet, NEAR, 0, 0, tiled=True).reshape(nx, n_pair, 2 * LANES)
        coef = pl.pallas_call(
            coef_kernel,
            out_shape=jax.ShapeDtypeStruct((nz, n_pair, LANES), jnp.float32),
            in_specs=[vmem],
            out_specs=vmem,
            name="coef",
        )(packets)
        coef = lax.all_to_all(coef, Z, 0, 0, tiled=True).reshape(n_index, LANES)

    with jax.named_scope("gradient"):
        part = jax.ShapeDtypeStruct((width // ncore, cols), jnp.float32)
        keep, send = pl.pallas_call(
            gradient_kernel,
            out_shape=(part, part),
            in_specs=[vmem] * 2 + [pl.BlockSpec(memory_space=pl.ANY)] * 4,
            out_specs=(vmem, vmem),
            scratch_shapes=[
                pltpu.VMEM((queries, shard_rows), jnp.float32),
                *[pltpu.VMEM(x.shape, x.dtype) for x in (my_rows, my_unit, query_scale, ordered)],
                pltpu.SemaphoreType.DMA((4,)),
            ],
            compiler_params=pltpu.CompilerParams(vmem_limit_bytes=40 << 20),
            name="gradient",
        )(coef, slots, my_rows, my_unit, query_scale, ordered)

    with jax.named_scope("reduce_gradient"):
        term = (keep + shift(send, "core", 1)).reshape(ny, nz * six, cols)
        term = jnp.sum(lax.all_to_all(term, "y", 0, 0, tiled=True), axis=0)
        term = term.reshape(nz, six, cols)
        term = jnp.sum(lax.all_to_all(term, Z, 0, 0, tiled=True), axis=0)
        grad_proj = send_all(term, "reader")
        grad_proj = grad_proj.transpose(1, 0, 2).reshape(six, width)

    mass = jnp.sum(lax.dynamic_index_in_dim(packets, y * ncore + core, 1, False), axis=0)
    my_target = lax.dynamic_slice_in_dim(mass, r * SLOT, topk, 0)
    log_target = jnp.log(my_target)
    retr_loss = jnp.sum(my_target * (log_target - log_prob))
    return (grad_proj, slab_best, retr_loss[None], log_target[None])


def solution(mesh):
    split = Mesh(mesh.devices.reshape(4, 4, 4, 2, 4), INDEX + ("reader",))
    return jax.shard_map(
        body,
        mesh=split,
        in_specs=(
            P(INDEX, None),
            P(INDEX + ("reader",), None),
            P(),
            P(INDEX + ("reader",), None),
            P(INDEX, None),
            P(INDEX, None, None, "reader"),
            P(INDEX, "reader"),
            P("reader"),
            P(INDEX, None, "reader"),
        ),
        out_specs=(
            P(INDEX, None),
            P(INDEX + ("reader",)),
            P(INDEX + ("reader",)),
            P(INDEX + ("reader",), None),
        ),
        check_vma=False,
    )
```

```python
import functools
import math

import jax
import jax.numpy as jnp
from jax import lax
from jax.experimental import pallas as pl
from jax.experimental.pallas import tpu as pltpu
from jax.sharding import Mesh, PartitionSpec as P

HEADS = 64
DH = 64
ANS = 16
EPSILON = 1e-06
SOFTMAX_TEMPER = 0.05
EXACT = lax.Precision.HIGHEST
INDEX = ("y", "zq", "zr", "core")
Z = ("zq", "zr")
NEAR = ("reader", "y", "core")
LANES = 128
SLOT = 32
TILE = 256
N_OWNERS = 128


def shift(x, axis, step):
    size = lax.axis_size(axis)
    return lax.ppermute(x, axis, [((i + step) % size, i) for i in range(size)])


def send_all(x, axis):
    size = lax.axis_size(axis)
    return lax.all_to_all(jnp.broadcast_to(x[None], (size, *x.shape)), axis, 0, 0, tiled=True)


def halves(x):
    high = x.astype(jnp.bfloat16)
    return high, (x - high.astype(jnp.float32)).astype(jnp.bfloat16)


def dot32(a, b):
    return jnp.dot(a, b, preferred_element_type=jnp.float32)


def token_copies(r, chunk, tokens, target, sems):
    own, after, far_low, far_high, before = tokens
    half = target.shape[0] // 2
    low, high = target.at[pl.ds(0, half)], target.at[pl.ds(half, half)]
    for j, block in enumerate((own, after, None, before)):

        @pl.when((r + j) % 4 == chunk)
        def _():
            first = far_low if block is None else block.at[pl.ds(0, half)]
            second = far_high if block is None else block.at[pl.ds(half, half)]
            pltpu.make_async_copy(first, low, sems.at[0]).start()
            pltpu.make_async_copy(second, high, sems.at[1]).start()

    return [
        pltpu.make_async_copy(low, low, sems.at[0]),
        pltpu.make_async_copy(high, high, sems.at[1]),
    ]


def row_copies(core, own, other, target, sem):
    for residue in range(4):
        to = target.at[:, residue]
        pltpu.make_async_copy(own.at[residue], to.at[:, core], sem).start()
        pltpu.make_async_copy(other.at[residue], to.at[:, 1 - core], sem).start()
    return [pltpu.make_async_copy(target, target, sem)]


def attend(keys, offset, dec, gain, live, column_v):
    group, n = dec.shape[0], live.shape[1]
    cols = pl.ds(pl.multiple_of(offset, TILE), TILE)
    same = (
        lax.broadcasted_iota(jnp.int32, (TILE, TILE), 0) // DH
        == lax.broadcasted_iota(jnp.int32, (TILE, TILE), 1) // DH
    ).astype(jnp.bfloat16)
    mine = (
        lax.broadcasted_iota(jnp.int32, (TILE // DH * ANS, TILE), 0) // ANS
        == lax.broadcasted_iota(jnp.int32, (TILE // DH * ANS, TILE), 1) // DH
    )
    high, low = halves(keys * keys)
    square = (dot32(high, same) + dot32(low, same)) / DH
    unit = (keys * lax.rsqrt(square + EPSILON) * gain[:, cols]).astype(jnp.bfloat16)
    for g in range(group):
        answer = dec[g, :, cols].astype(jnp.float32)
        answer = jnp.concatenate([answer] * (TILE // DH), axis=0)
        answer = jnp.where(mine, answer, 0.0).astype(jnp.bfloat16)
        similarity = lax.dot_general(
            answer,
            unit[g * n : (g + 1) * n],
            (((1,), (1,)), ((), ())),
            preferred_element_type=jnp.float32,
        ) / math.sqrt(DH)
        weight = jnp.where(live[g : g + 1, :] > 0, jnp.exp(similarity), 0.0)
        weight = weight / jnp.sum(weight, axis=1, keepdims=True)
        column_v[g : g + 1, :] += jnp.sum(weight, axis=0, keepdims=True)


def load_and_attend(place, offset, tokens, own, other, dec, gain, live, column_v, token_v, weight_v, sems):
    core, r = place[0], place[1]
    copies = []
    for c in range(4):
        copies.append(row_copies(core, own.at[c], other.at[c], weight_v.at[c], sems.at[2 * c, 0]))
        copies[c] += token_copies(r, c, tokens, token_v.at[c], sems.at[2 * c + 1])
    for c in range(4):
        for copy in copies[c]:
            copy.wait()

    @pl.loop(0, weight_v.shape[-1] // TILE)
    def _(t):
        cols = pl.ds(pl.multiple_of(t * TILE, TILE), TILE)
        keys = dot32(token_v[0], weight_v[0, :, :, :, :, cols].reshape(-1, TILE))
        for c in range(1, 4):
            keys += dot32(token_v[c], weight_v[c, :, :, :, :, cols].reshape(-1, TILE))
        attend(keys, offset + t * TILE, dec, gain, live, column_v)


def first_heads_kernel(place, *refs):
    tokens, (own, other, dec, gain, live, columns, token_v, weight_v, sems) = refs[:5], refs[5:]
    columns[...] = jnp.zeros_like(columns)
    load_and_attend(
        place, 0, tokens, own, other, dec, gain, live, columns, token_v, weight_v, sems
    )


def last_heads_kernel(place, *refs):
    tokens, refs = refs[:5], refs[5:]
    own, other, dec, gain, live, columns, scores, out, column_v, token_v, weight_v, sems = refs
    column_v[...] = columns[...]
    load_and_attend(
        place,
        weight_v.shape[-1],
        tokens,
        own,
        other,
        dec,
        gain,
        live,
        column_v,
        token_v,
        weight_v,
        sems,
    )
    n = live.shape[1]
    mass = jnp.zeros((8, LANES), jnp.float32)
    for g in range(dec.shape[0]):
        column = jnp.broadcast_to(column_v[g : g + 1, :], (8, n))
        to = (
            lax.broadcasted_iota(jnp.int32, (n, LANES), 0) // 8 + g * SLOT
            == lax.broadcasted_iota(jnp.int32, (n, LANES), 1)
        ).astype(jnp.float32)
        mass += jnp.dot(column, to, precision=EXACT, preferred_element_type=jnp.float32)
    out[:, :LANES] = jnp.broadcast_to(mass[:1] / (HEADS * ANS), (out.shape[0], LANES))
    out[:, LANES:] = jnp.broadcast_to(scores[...], (out.shape[0], LANES))


def attention_packet(place, tokens, first_rows, last_rows, dec, gain, live, scores):
    vmem = pl.BlockSpec(memory_space=pltpu.VMEM)
    anywhere = pl.BlockSpec(memory_space=pl.ANY)
    smem = pl.BlockSpec(memory_space=pltpu.SMEM)
    rows, width = tokens[0].shape
    ny, nzr, nzq, chip_rows, half = first_rows[0].shape
    common = dict(
        out_specs=vmem,
        compiler_params=pltpu.CompilerParams(vmem_limit_bytes=48 << 20),
        cost_estimate=pl.CostEstimate(
            flops=2 * rows * ny * width * half, bytes_accessed=9 << 20, transcendentals=0
        ),
    )
    columns = pltpu.VMEM((8, live.shape[1]), jnp.float32)
    scratch = [
        pltpu.VMEM((ny, rows, width), jnp.bfloat16),
        pltpu.VMEM((ny, nzq, nzr, 2, chip_rows, half), jnp.bfloat16),
        pltpu.SemaphoreType.DMA((8, 2)),
    ]
    first = pl.pallas_call(
        first_heads_kernel,
        out_shape=jax.ShapeDtypeStruct(columns.shape, jnp.float32),
        in_specs=[smem] + [anywhere] * 7 + [vmem] * 3,
        scratch_shapes=scratch,
        name="first_heads",
        **common,
    )(place, *tokens, *first_rows, dec, gain, live)
    return pl.pallas_call(
        last_heads_kernel,
        out_shape=jax.ShapeDtypeStruct((32, 2 * LANES), jnp.float32),
        in_specs=[smem] + [anywhere] * 7 + [vmem] * 5,
        scratch_shapes=[columns] + scratch,
        name="last_heads",
        **common,
    )(place, *tokens, *last_rows, dec, gain, live, first, scores)


def scores_kernel(place, packed, proj, emb, chosen, state, slots, rows, unit, scale, ordered, unit_v, ids_v):
    shard, r = place[0], place[1]
    n_rows, width = emb.shape
    per_x = state.shape[0]
    cols = rows.shape[1]
    feats = packed[:, :, :width].reshape(4 * per_x, width)
    ordered[...] = lax.dot_general(
        chosen[...], feats, (((1,), (1,)), ((), ())), preferred_element_type=jnp.float32
    ).astype(jnp.bfloat16)

    lane = lax.broadcasted_iota(jnp.int32, (per_x, LANES), 1)
    spread = jnp.full((per_x, LANES), -1, jnp.int32)
    for x in range(4):
        coded = packed[8 * x : 8 * x + 8, :, width : width + LANES].reshape(per_x, LANES)
        coded = coded.astype(jnp.float32)
        ids = coded * 256 + pltpu.roll(coded, LANES // 2, 1)
        ids = ids.astype(jnp.int32) - shard * n_rows
        ids_v[x] = ids
        moved = ids if x == 0 else pltpu.roll(ids, SLOT * x, 1)
        spread = jnp.where((lane // SLOT == x) & (lane % SLOT < 20), moved, spread)
    slots[...] = spread

    vec = dot32(feats, proj[...])
    scale_all = lax.rsqrt(jnp.sum(vec * vec, axis=1, keepdims=True) + EPSILON)
    scale[...] = scale_all
    unit_all = vec * scale_all
    unit_v[...] = unit_all
    emb_all = emb[...]
    row_unit = emb_all * lax.rsqrt(jnp.sum(emb_all * emb_all, axis=1, keepdims=True) + EPSILON)
    for x in range(4):

        @pl.when(r == x)
        def _():
            rows[...] = row_unit[:, x * cols : (x + 1) * cols]
            unit[...] = unit_all[:, x * cols : (x + 1) * cols]

    share = unit_v[pl.ds(pl.multiple_of(r * per_x, per_x), per_x), :]
    found = (
        lax.dot_general(
            share,
            row_unit,
            (((1,), (1,)), ((), ())),
            precision=EXACT,
            preferred_element_type=jnp.float32,
        )
        / SOFTMAX_TEMPER
    )
    places = ids_v[r]
    row = lax.broadcasted_iota(jnp.int32, (per_x, n_rows), 1)
    total = jnp.where(lane == 20, jnp.max(found, axis=1, keepdims=True), 0.0)
    for k in range(20):
        picked = jnp.where(places[:, k : k + 1] == row, found, 0.0)
        total = jnp.where(lane == k, jnp.sum(picked, axis=1, keepdims=True), total)
    state[...] = total


def coef_kernel(packets, out):
    lane = lax.broadcasted_iota(jnp.int32, (8, LANES), 1)
    target = prob = fetched = jnp.zeros((8, LANES), jnp.float32)
    for x in range(4):
        target += packets[x, :, :LANES]
        scores = packets[x, :, LANES:]
        own = (lane // SLOT == x) & (lane % SLOT < 20)
        moved = scores if x == 0 else pltpu.roll(scores, SLOT * x, 1)
        prob += jnp.where(own, moved, 0.0)
        moved = pltpu.roll(scores, (SLOT * x + LANES // 2) % LANES, 1)
        fetched += jnp.where(own, moved, 0.0)
    gap = prob - target
    to = (
        lax.broadcasted_iota(jnp.int32, (LANES, LANES), 0) // SLOT * SLOT + 20
        == lax.broadcasted_iota(jnp.int32, (LANES, LANES), 1)
    ).astype(jnp.float32)
    along = jnp.dot(gap * fetched, to, precision=EXACT, preferred_element_type=jnp.float32)
    packed = gap / SOFTMAX_TEMPER + along / N_OWNERS
    out[...] = jnp.broadcast_to(packed[None], out.shape)


def gradient_kernel(coef, slot, *refs):
    far, (keep, send, matrix_v), near, sems = refs[:4], refs[4:7], refs[7:11], refs[11]
    copies = [pltpu.make_async_copy(a, b, sems.at[i]) for i, (a, b) in enumerate(zip(far, near))]
    for copy in copies:
        copy.start()
    rows, unit, scale, ordered = near
    n_rows = matrix_v.shape[1]
    blocks = coef.shape[0]

    @pl.loop(0, blocks // 8)
    def _(b):
        eight = pl.ds(pl.multiple_of(b * 8, 8), 8)
        row = lax.broadcasted_iota(jnp.int32, (8, n_rows), 1)
        values = coef[pl.ds(b // 2 + b % 2 * 64, 8, stride=8), :]
        places = slot[eight, :]
        for x in range(4):
            total = jnp.zeros((8, n_rows), jnp.float32)
            for k in range(SLOT * x, SLOT * x + 20):
                total += jnp.where(places[:, k : k + 1] == row, values[:, k : k + 1], 0.0)
            matrix_v[pl.ds(pl.multiple_of(x * blocks + b * 8, 8), 8), :] = total

    for copy in copies:
        copy.wait()
    along_all = jnp.concatenate([coef[pl.ds(p, 16, stride=8), :] for p in range(8)], axis=0)
    row_high, row_low = halves(rows[...])
    parts_high, parts_low = [], []
    for x in range(4):
        mine = slice(x * blocks, (x + 1) * blocks)
        high, low = halves(matrix_v[mine, :])
        part = dot32(high, row_high) + (dot32(high, row_low) + dot32(low, row_high))
        along = along_all[:, SLOT * x + 20 : SLOT * x + 21]
        part = (part - unit[mine, :] * along) * scale[mine, :]
        high, low = halves(part)
        parts_high.append(high)
        parts_low.append(low)
    high, low = jnp.concatenate(parts_high, axis=0), jnp.concatenate(parts_low, axis=0)
    half = keep.shape[0]
    keep[...] = dot32(ordered[:half, :], high) + dot32(ordered[:half, :], low)
    send[...] = dot32(ordered[half:, :], high) + dot32(ordered[half:, :], low)


def body(
    index_emb,
    query_feat,
    query_proj,
    passage_id,
    passage_len,
    enc_out,
    key_proj,
    key_gain,
    dec_query,
):
    y, zq, zr, core, r = (lax.axis_index(a) for a in (*INDEX, "reader"))
    ny, nz, ncore, nx = 4, 16, 2, 4
    z = zq * 4 + zr
    n_index = ny * nz * ncore
    n_pair = ny * ncore
    my_shard = (y * nz + z) * ncore + core
    shard_rows, width = index_emb.shape
    topk = passage_id.shape[1]

    group, _, plen, feats_here = enc_out.shape
    token_rows = group * topk * plen
    with jax.named_scope("gather_enc_out"):
        own = enc_out.reshape(token_rows, feats_here)
        after, before = shift(own, "reader", 1), shift(own, "reader", -1)
        mid = token_rows // 2
        far_low, far_high = shift(after[:mid], "reader", 1), shift(before[mid:], "reader", -1)
        tokens = (own, after, far_low, far_high, before)

    half = key_proj.shape[1] // 2
    with jax.named_scope("gather_key_proj"):
        rows = lax.all_gather(key_proj, "zq")
        rows, query_feat, passage_id = lax.optimization_barrier((rows, query_feat, passage_id))
        rows = lax.all_gather(rows, "zr")
        heads = []
        for columns in (rows[..., :half], rows[..., half:]):
            own = lax.all_gather(columns, "y")
            heads.append((own, shift(own, "core", 1)))

    with jax.named_scope("gather_queries"):
        ids_high = (passage_id // 256).astype(jnp.bfloat16)
        ids_low = (passage_id % 256).astype(jnp.bfloat16)
        gap = ((0, 0), (0, LANES // 2 - topk))
        coded = [query_feat, jnp.pad(ids_high, gap), jnp.pad(ids_low, gap)]
        packed = send_all(send_all(jnp.concatenate(coded, axis=1)[0], Z), NEAR)

    cols = width // nx
    six = width // n_index
    place = lax.broadcasted_iota(jnp.int32, (width, 1), 0)
    to_core, to_y = place // (ny * nz * six), place // (nz * six) % ny
    to_z, within = place // six % nz, place % six
    column = ((to_y * nz + to_z) * ncore + (to_core + core) % ncore) * six + within
    chosen = (lax.broadcasted_iota(jnp.int32, (1, width), 1) == column).astype(jnp.bfloat16)

    vmem = pl.BlockSpec(memory_space=pltpu.VMEM)
    with jax.named_scope("scores"):
        queries = n_index * nx
        state, slots, my_rows, my_unit, query_scale, ordered = pl.pallas_call(
            scores_kernel,
            out_shape=(
                jax.ShapeDtypeStruct((n_index, LANES), jnp.float32),
                jax.ShapeDtypeStruct((n_index, LANES), jnp.int32),
                jax.ShapeDtypeStruct((shard_rows, cols), jnp.float32),
                jax.ShapeDtypeStruct((queries, cols), jnp.float32),
                jax.ShapeDtypeStruct((queries, 1), jnp.float32),
                jax.ShapeDtypeStruct((width, queries), jnp.bfloat16),
            ),
            in_specs=[pl.BlockSpec(memory_space=pltpu.SMEM)] + [vmem] * 4,
            out_specs=(vmem,) * 6,
            scratch_shapes=[
                pltpu.VMEM((queries, width), jnp.float32),
                pltpu.VMEM((nx, n_index, LANES), jnp.int32),
            ],
            compiler_params=pltpu.CompilerParams(vmem_limit_bytes=48 << 20),
            cost_estimate=pl.CostEstimate(
                flops=4 << 30, bytes_accessed=8 << 20, transcendentals=0
            ),
            name="scores",
        )(jnp.stack([my_shard, r]).astype(jnp.int32), packed, query_proj, index_emb, chosen)

    def merge_all(x):
        lane = lax.broadcasted_iota(jnp.int32, x.shape[1:], x.ndim - 2)
        return jnp.where(lane < topk, jnp.sum(x, axis=0), jnp.max(x, axis=0))

    with jax.named_scope("reduce_scores"):
        state = state.reshape(n_pair, nz, LANES)
        state = merge_all(lax.all_to_all(state, ("y", "core"), 0, 0, tiled=True))
        state = merge_all(lax.all_to_all(state, Z, 0, 0, tiled=True))
        slab_best = state[topk : topk + 1]
        fetched = state[:topk]
    expo = jnp.exp(fetched)
    total = jnp.sum(expo)
    prob = expo / total
    log_prob = fetched - jnp.log(total)
    score_row = jnp.zeros((1, LANES), jnp.float32)
    score_row = score_row.at[0, :topk].set(prob).at[0, LANES // 2 : LANES // 2 + topk].set(fetched)

    with jax.named_scope("attention"):
        answer = dec_query.shape[1]
        heads_here = feats_here // DH
        decoded = dec_query.astype(jnp.float32).reshape(group, answer, heads_here, DH)
        dec_unit = (
            decoded * lax.rsqrt(jnp.mean(decoded * decoded, axis=3, keepdims=True) + EPSILON)
        ).astype(jnp.bfloat16)
        positions = lax.broadcasted_iota(jnp.int32, (group, topk, plen), 2)
        live = (positions < passage_len[:, :, None]).reshape(group, topk * plen)
        packet = attention_packet(
            jnp.stack([core, r]).astype(jnp.int32),
            tokens,
            *heads,
            dec_unit.reshape(group, answer, feats_here),
            key_gain.astype(jnp.float32).reshape(1, feats_here),
            live.astype(jnp.float32),
            score_row,
        )

    with jax.named_scope("targets"):
        packets = lax.all_to_all(packet, NEAR, 0, 0, tiled=True).reshape(nx, n_pair, 2 * LANES)
        coef = pl.pallas_call(
            coef_kernel,
            out_shape=jax.ShapeDtypeStruct((nz, n_pair, LANES), jnp.float32),
            in_specs=[vmem],
            out_specs=vmem,
            name="coef",
        )(packets)
        coef = lax.all_to_all(coef, Z, 0, 0, tiled=True).reshape(n_index, LANES)

    with jax.named_scope("gradient"):
        part = jax.ShapeDtypeStruct((width // ncore, cols), jnp.float32)
        keep, send = pl.pallas_call(
            gradient_kernel,
            out_shape=(part, part),
            in_specs=[vmem] * 2 + [pl.BlockSpec(memory_space=pl.ANY)] * 4,
            out_specs=(vmem, vmem),
            scratch_shapes=[
                pltpu.VMEM((queries, shard_rows), jnp.float32),
                *[pltpu.VMEM(x.shape, x.dtype) for x in (my_rows, my_unit, query_scale, ordered)],
                pltpu.SemaphoreType.DMA((4,)),
            ],
            compiler_params=pltpu.CompilerParams(vmem_limit_bytes=40 << 20),
            name="gradient",
        )(coef, slots, my_rows, my_unit, query_scale, ordered)

    with jax.named_scope("reduce_gradient"):
        term = (keep + shift(send, "core", 1)).reshape(ny, nz * six, cols)
        term = jnp.sum(lax.all_to_all(term, "y", 0, 0, tiled=True), axis=0)
        term = term.reshape(nz, six, cols)
        term = jnp.sum(lax.all_to_all(term, Z, 0, 0, tiled=True), axis=0)
        grad_proj = send_all(term, "reader")
        grad_proj = grad_proj.transpose(1, 0, 2).reshape(six, width)

    mass = jnp.sum(lax.dynamic_index_in_dim(packets, y * ncore + core, 1, False), axis=0)
    my_target = lax.dynamic_slice_in_dim(mass, r * SLOT, topk, 0)
    log_target = jnp.log(my_target)
    retr_loss = jnp.sum(my_target * (log_target - log_prob))
    return (grad_proj, slab_best, retr_loss[None], log_target[None])


def solution(mesh):
    split = Mesh(mesh.devices.reshape(4, 4, 4, 2, 4), INDEX + ("reader",))
    return jax.shard_map(
        body,
        mesh=split,
        in_specs=(
            P(INDEX, None),
            P(INDEX + ("reader",), None),
            P(),
            P(INDEX + ("reader",), None),
            P(INDEX, None),
            P(INDEX, None, None, "reader"),
            P(INDEX, "reader"),
            P("reader"),
            P(INDEX, None, "reader"),
        ),
        out_specs=(
            P(INDEX, None),
            P(INDEX + ("reader",)),
            P(INDEX + ("reader",)),
            P(INDEX + ("reader",), None),
        ),
        check_vma=False,
    )
```

```python
import functools
import math

import jax
import jax.numpy as jnp
from jax import lax
from jax.experimental import pallas as pl
from jax.experimental.pallas import tpu as pltpu
from jax.sharding import Mesh, PartitionSpec as P

HEADS = 64
DH = 64
ANS = 16
EPSILON = 1e-06
SOFTMAX_TEMPER = 0.05
EXACT = lax.Precision.HIGHEST
INDEX = ("y", "zq", "zr", "core")
Z = ("zq", "zr")
NEAR = ("reader", "y", "core")
LANES = 128
SLOT = 32
TILE = 256
N_OWNERS = 128
EARLY = (0, 1, 3)
LATE = 2


def shift(x, axis, step):
    size = lax.axis_size(axis)
    return lax.ppermute(x, axis, [((i + step) % size, i) for i in range(size)])


def send_all(x, axis):
    size = lax.axis_size(axis)
    return lax.all_to_all(jnp.broadcast_to(x[None], (size, *x.shape)), axis, 0, 0, tiled=True)


def halves(x):
    high = x.astype(jnp.bfloat16)
    return high, (x - high.astype(jnp.float32)).astype(jnp.bfloat16)


def dot32(a, b):
    return jnp.dot(a, b, preferred_element_type=jnp.float32)


def token_copies(r, chunk, tokens, target, sems):
    own, after, far_low, far_high, before = tokens
    half = target.shape[0] // 2
    low, high = target.at[pl.ds(0, half)], target.at[pl.ds(half, half)]
    for j, block in enumerate((own, after, None, before)):

        @pl.when((r + j) % 4 == chunk)
        def _():
            first = far_low if block is None else block.at[pl.ds(0, half)]
            second = far_high if block is None else block.at[pl.ds(half, half)]
            pltpu.make_async_copy(first, low, sems.at[0]).start()
            pltpu.make_async_copy(second, high, sems.at[1]).start()

    return [
        pltpu.make_async_copy(low, low, sems.at[0]),
        pltpu.make_async_copy(high, high, sems.at[1]),
    ]


def row_copies(place, own, other, target, sem):
    zr, core = place[1], place[2]
    for residue in range(4):
        to = target.at[:, (zr + residue) % 4]
        four = pl.ds(4 * residue, 4)
        pltpu.make_async_copy(own.at[four], to.at[:, core], sem).start()
        pltpu.make_async_copy(other.at[four], to.at[:, 1 - core], sem).start()
    return [pltpu.make_async_copy(target, target, sem)]


def early_keys_kernel(place, *refs):
    tokens, rows, (keys, token_v, weight_v, sems) = refs[:5], refs[5:11], refs[11:]
    y, r = place[0], place[3]
    copies = []
    for slot, ahead in enumerate(EARLY):
        own, other = rows[2 * slot], rows[2 * slot + 1]
        waits = row_copies(place, own, other, weight_v.at[slot], sems.at[slot, 0])
        target = token_v.at[slot]
        waits += token_copies(r, (y + ahead) % 4, tokens, target, sems.at[3 + slot])
        copies.append(waits)
    for slot in range(len(EARLY)):
        for copy in copies[slot]:
            copy.wait()

        @pl.loop(0, keys.shape[1] // TILE)
        def _(t):
            cols = pl.ds(pl.multiple_of(t * TILE, TILE), TILE)
            term = dot32(token_v[slot], weight_v[slot, :, :, :, :, cols].reshape(-1, TILE))
            if slot == 0:
                keys[:, cols] = term
            else:
                keys[:, cols] += term


def attend(keys, offset, dec, gain, live, column_v):
    group, n = dec.shape[0], live.shape[1]
    cols = pl.ds(pl.multiple_of(offset, TILE), TILE)
    same = (
        lax.broadcasted_iota(jnp.int32, (TILE, TILE), 0) // DH
        == lax.broadcasted_iota(jnp.int32, (TILE, TILE), 1) // DH
    ).astype(jnp.bfloat16)
    mine = (
        lax.broadcasted_iota(jnp.int32, (TILE // DH * ANS, TILE), 0) // ANS
        == lax.broadcasted_iota(jnp.int32, (TILE // DH * ANS, TILE), 1) // DH
    )
    high, low = halves(keys * keys)
    square = (dot32(high, same) + dot32(low, same)) / DH
    unit = (keys * lax.rsqrt(square + EPSILON) * gain[:, cols]).astype(jnp.bfloat16)
    for g in range(group):
        answer = dec[g, :, cols].astype(jnp.float32)
        answer = jnp.concatenate([answer] * (TILE // DH), axis=0)
        answer = jnp.where(mine, answer, 0.0).astype(jnp.bfloat16)
        similarity = lax.dot_general(
            answer,
            unit[g * n : (g + 1) * n],
            (((1,), (1,)), ((), ())),
            preferred_element_type=jnp.float32,
        ) / math.sqrt(DH)
        weight = jnp.where(live[g : g + 1, :] > 0, jnp.exp(similarity), 0.0)
        weight = weight / jnp.sum(weight, axis=1, keepdims=True)
        column_v[g : g + 1, :] += jnp.sum(weight, axis=0, keepdims=True)


def late_heads_kernel(place, *refs):
    tokens, (own, other), refs = refs[:5], refs[5:7], refs[7:]
    early, dec, gain, live, states, out, own_scores, token_v, weight_v, column_v, sems = refs
    y, r = place[0], place[3]
    copies = row_copies(place, own, other, weight_v, sems.at[0, 0])
    copies += token_copies(r, (y + LATE) % 4, tokens, token_v, sems.at[1])
    column_v[...] = jnp.zeros_like(column_v)

    lane = lax.broadcasted_iota(jnp.int32, (1, LANES), 1)
    found = states[...]
    fetched = jnp.where(lane < 20, jnp.sum(found, axis=0, keepdims=True), 0.0)
    expo = jnp.where(lane < 20, jnp.exp(fetched), 0.0)
    total = jnp.sum(expo, axis=1, keepdims=True)
    log_prob = fetched - jnp.log(total)
    best = jnp.max(found, axis=0, keepdims=True)
    own_scores[...] = jnp.broadcast_to(jnp.where(lane == 20, best, log_prob), own_scores.shape)
    scores = expo / total + pltpu.roll(fetched, LANES // 2, 1)
    out[:, LANES:] = jnp.broadcast_to(scores, (out.shape[0], LANES))

    for copy in copies:
        copy.wait()

    @pl.loop(0, early.shape[1] // TILE)
    def _(t):
        cols = pl.ds(pl.multiple_of(t * TILE, TILE), TILE)
        keys = early[:, cols] + dot32(token_v[...], weight_v[:, :, :, :, cols].reshape(-1, TILE))
        attend(keys, t * TILE, dec, gain, live, column_v)

    n = live.shape[1]
    mass = jnp.zeros((8, LANES), jnp.float32)
    for g in range(dec.shape[0]):
        column = jnp.broadcast_to(column_v[g : g + 1, :], (8, n))
        to = (
            lax.broadcasted_iota(jnp.int32, (n, LANES), 0) // 8 + g * SLOT
            == lax.broadcasted_iota(jnp.int32, (n, LANES), 1)
        ).astype(jnp.float32)
        mass += jnp.dot(column, to, precision=EXACT, preferred_element_type=jnp.float32)
    out[:, :LANES] = jnp.broadcast_to(mass[:1] / (HEADS * ANS), (out.shape[0], LANES))


def attention_packet(place, tokens, rows, dec, gain, live, states):
    vmem = pl.BlockSpec(memory_space=pltpu.VMEM)
    anywhere = pl.BlockSpec(memory_space=pl.ANY)
    smem = pl.BlockSpec(memory_space=pltpu.SMEM)
    token_rows, width = tokens[0].shape
    block = (4, 4, 2, *rows[0][0].shape[1:])

    def cost(count, size):
        return pl.CostEstimate(
            flops=2 * token_rows * count * width * width,
            bytes_accessed=size << 20,
            transcendentals=0,
        )

    early = pl.pallas_call(
        early_keys_kernel,
        out_shape=jax.ShapeDtypeStruct((token_rows, width), jnp.float32),
        in_specs=[smem] + [anywhere] * 11,
        out_specs=vmem,
        scratch_shapes=[
            pltpu.VMEM((3, token_rows, width), jnp.bfloat16),
            pltpu.VMEM((3, *block), jnp.bfloat16),
            pltpu.SemaphoreType.DMA((6, 2)),
        ],
        compiler_params=pltpu.CompilerParams(vmem_limit_bytes=24 << 20),
        cost_estimate=cost(3, 13),
        name="early_keys",
    )(place, *tokens, *[part for ahead in EARLY for part in rows[ahead]])
    return pl.pallas_call(
        late_heads_kernel,
        out_shape=(
            jax.ShapeDtypeStruct((32, 2 * LANES), jnp.float32),
            jax.ShapeDtypeStruct((8, LANES), jnp.float32),
        ),
        in_specs=[smem] + [anywhere] * 7 + [vmem] * 5,
        out_specs=(vmem, vmem),
        scratch_shapes=[
            pltpu.VMEM((token_rows, width), jnp.bfloat16),
            pltpu.VMEM(block, jnp.bfloat16),
            pltpu.VMEM((8, live.shape[1]), jnp.float32),
            pltpu.SemaphoreType.DMA((2, 2)),
        ],
        compiler_params=pltpu.CompilerParams(vmem_limit_bytes=24 << 20),
        cost_estimate=cost(1, 6),
        name="late_heads",
    )(place, *tokens, *rows[LATE], early, dec, gain, live, states)


def scores_kernel(place, packed, proj, emb, chosen, state, slots, rows, unit, scale, ordered, unit_v, ids_v):
    shard, r = place[0], place[1]
    n_rows, width = emb.shape
    per_x = state.shape[0]
    cols = rows.shape[1]
    feats = packed[:, :, :width].reshape(4 * per_x, width)
    ordered[...] = lax.dot_general(
        chosen[...], feats, (((1,), (1,)), ((), ())), preferred_element_type=jnp.float32
    ).astype(jnp.bfloat16)

    lane = lax.broadcasted_iota(jnp.int32, (per_x, LANES), 1)
    spread = jnp.full((per_x, LANES), -1, jnp.int32)
    for x in range(4):
        coded = packed[8 * x : 8 * x + 8, :, width : width + LANES].reshape(per_x, LANES)
        coded = coded.astype(jnp.float32)
        ids = coded * 256 + pltpu.roll(coded, LANES // 2, 1)
        ids = ids.astype(jnp.int32) - shard * n_rows
        ids_v[x] = ids
        moved = ids if x == 0 else pltpu.roll(ids, SLOT * x, 1)
        spread = jnp.where((lane // SLOT == x) & (lane % SLOT < 20), moved, spread)
    slots[...] = spread

    vec = dot32(feats, proj[...])
    scale_all = lax.rsqrt(jnp.sum(vec * vec, axis=1, keepdims=True) + EPSILON)
    scale[...] = scale_all
    unit_all = vec * scale_all
    unit_v[...] = unit_all
    emb_all = emb[...]
    row_unit = emb_all * lax.rsqrt(jnp.sum(emb_all * emb_all, axis=1, keepdims=True) + EPSILON)
    for x in range(4):

        @pl.when(r == x)
        def _():
            rows[...] = row_unit[:, x * cols : (x + 1) * cols]
            unit[...] = unit_all[:, x * cols : (x + 1) * cols]

    share = unit_v[pl.ds(pl.multiple_of(r * per_x, per_x), per_x), :]
    found = (
        lax.dot_general(
            share,
            row_unit,
            (((1,), (1,)), ((), ())),
            precision=EXACT,
            preferred_element_type=jnp.float32,
        )
        / SOFTMAX_TEMPER
    )
    places = ids_v[r]
    row = lax.broadcasted_iota(jnp.int32, (per_x, n_rows), 1)
    total = jnp.where(lane == 20, jnp.max(found, axis=1, keepdims=True), 0.0)
    for k in range(20):
        picked = jnp.where(places[:, k : k + 1] == row, found, 0.0)
        total = jnp.where(lane == k, jnp.sum(picked, axis=1, keepdims=True), total)
    state[...] = total


def coef_kernel(packets, out):
    lane = lax.broadcasted_iota(jnp.int32, (8, LANES), 1)
    target = prob = fetched = jnp.zeros((8, LANES), jnp.float32)
    for x in range(4):
        target += packets[x, :, :LANES]
        scores = packets[x, :, LANES:]
        own = (lane // SLOT == x) & (lane % SLOT < 20)
        moved = scores if x == 0 else pltpu.roll(scores, SLOT * x, 1)
        prob += jnp.where(own, moved, 0.0)
        moved = pltpu.roll(scores, (SLOT * x + LANES // 2) % LANES, 1)
        fetched += jnp.where(own, moved, 0.0)
    gap = prob - target
    to = (
        lax.broadcasted_iota(jnp.int32, (LANES, LANES), 0) // SLOT * SLOT + 20
        == lax.broadcasted_iota(jnp.int32, (LANES, LANES), 1)
    ).astype(jnp.float32)
    along = jnp.dot(gap * fetched, to, precision=EXACT, preferred_element_type=jnp.float32)
    packed = gap / SOFTMAX_TEMPER + along / N_OWNERS
    out[...] = jnp.broadcast_to(packed[None], out.shape)


def gradient_kernel(coef, slot, *refs):
    far, (keep, send, matrix_v), near, sems = refs[:4], refs[4:7], refs[7:11], refs[11]
    copies = [pltpu.make_async_copy(a, b, sems.at[i]) for i, (a, b) in enumerate(zip(far, near))]
    for copy in copies:
        copy.start()
    rows, unit, scale, ordered = near
    n_rows = matrix_v.shape[1]
    blocks = coef.shape[0]

    @pl.loop(0, blocks // 8)
    def _(b):
        eight = pl.ds(pl.multiple_of(b * 8, 8), 8)
        row = lax.broadcasted_iota(jnp.int32, (8, n_rows), 1)
        values = coef[pl.ds(b // 2 + b % 2 * 64, 8, stride=8), :]
        places = slot[eight, :]
        for x in range(4):
            total = jnp.zeros((8, n_rows), jnp.float32)
            for k in range(SLOT * x, SLOT * x + 20):
                total += jnp.where(places[:, k : k + 1] == row, values[:, k : k + 1], 0.0)
            matrix_v[pl.ds(pl.multiple_of(x * blocks + b * 8, 8), 8), :] = total

    for copy in copies:
        copy.wait()
    along_all = jnp.concatenate([coef[pl.ds(p, 16, stride=8), :] for p in range(8)], axis=0)
    row_high, row_low = halves(rows[...])
    parts_high, parts_low = [], []
    for x in range(4):
        mine = slice(x * blocks, (x + 1) * blocks)
        high, low = halves(matrix_v[mine, :])
        part = dot32(high, row_high) + (dot32(high, row_low) + dot32(low, row_high))
        along = along_all[:, SLOT * x + 20 : SLOT * x + 21]
        part = (part - unit[mine, :] * along) * scale[mine, :]
        high, low = halves(part)
        parts_high.append(high)
        parts_low.append(low)
    high, low = jnp.concatenate(parts_high, axis=0), jnp.concatenate(parts_low, axis=0)
    half = keep.shape[0]
    keep[...] = dot32(ordered[:half, :], high) + dot32(ordered[:half, :], low)
    send[...] = dot32(ordered[half:, :], high) + dot32(ordered[half:, :], low)


def body(
    index_emb,
    query_feat,
    query_proj,
    passage_id,
    passage_len,
    enc_out,
    key_proj,
    key_gain,
    dec_query,
):
    y, zq, zr, core, r = (lax.axis_index(a) for a in (*INDEX, "reader"))
    ny, nz, ncore, nx = 4, 16, 2, 4
    z = zq * 4 + zr
    n_index = ny * nz * ncore
    n_pair = ny * ncore
    my_shard = (y * nz + z) * ncore + core
    shard_rows, width = index_emb.shape
    topk = passage_id.shape[1]

    group, _, plen, feats_here = enc_out.shape
    token_rows = group * topk * plen
    with jax.named_scope("gather_enc_out"):
        own = enc_out.reshape(token_rows, feats_here)
        after, before = shift(own, "reader", 1), shift(own, "reader", -1)
        mid = token_rows // 2
        far_low, far_high = shift(after[:mid], "reader", 1), shift(before[mid:], "reader", -1)
        tokens = (own, after, far_low, far_high, before)

    with jax.named_scope("gather_key_proj"):
        own = send_all(key_proj, "zq")
        own, query_feat, passage_id = lax.optimization_barrier((own, query_feat, passage_id))
        after, before = shift(own, Z, 1), shift(own, Z, -1)
        far = [shift(own[:2], Z, 2), shift(own[2:], Z, -2)]
        own = jnp.concatenate([own, after, *far, before])
        after, before = shift(own, "y", 1), shift(own, "y", -1)
        far = jnp.concatenate([shift(after[:8], "y", 1), shift(before[8:], "y", -1)])
        key_rows = [(block, shift(block, "core", 1)) for block in (own, after, far, before)]

    with jax.named_scope("gather_queries"):
        ids_high = (passage_id // 256).astype(jnp.bfloat16)
        ids_low = (passage_id % 256).astype(jnp.bfloat16)
        gap = ((0, 0), (0, LANES // 2 - topk))
        coded = [query_feat, jnp.pad(ids_high, gap), jnp.pad(ids_low, gap)]
        packed = send_all(send_all(jnp.concatenate(coded, axis=1)[0], Z), NEAR)

    cols = width // nx
    six = width // n_index
    place = lax.broadcasted_iota(jnp.int32, (width, 1), 0)
    to_core, to_y = place // (ny * nz * six), place // (nz * six) % ny
    to_z, within = place // six % nz, place % six
    column = ((to_y * nz + to_z) * ncore + (to_core + core) % ncore) * six + within
    chosen = (lax.broadcasted_iota(jnp.int32, (1, width), 1) == column).astype(jnp.bfloat16)

    vmem = pl.BlockSpec(memory_space=pltpu.VMEM)
    with jax.named_scope("scores"):
        queries = n_index * nx
        state, slots, my_rows, my_unit, query_scale, ordered = pl.pallas_call(
            scores_kernel,
            out_shape=(
                jax.ShapeDtypeStruct((n_index, LANES), jnp.float32),
                jax.ShapeDtypeStruct((n_index, LANES), jnp.int32),
                jax.ShapeDtypeStruct((shard_rows, cols), jnp.float32),
                jax.ShapeDtypeStruct((queries, cols), jnp.float32),
                jax.ShapeDtypeStruct((queries, 1), jnp.float32),
                jax.ShapeDtypeStruct((width, queries), jnp.bfloat16),
            ),
            in_specs=[pl.BlockSpec(memory_space=pltpu.SMEM)] + [vmem] * 4,
            out_specs=(vmem,) * 6,
            scratch_shapes=[
                pltpu.VMEM((queries, width), jnp.float32),
                pltpu.VMEM((nx, n_index, LANES), jnp.int32),
            ],
            compiler_params=pltpu.CompilerParams(vmem_limit_bytes=28 << 20),
            cost_estimate=pl.CostEstimate(
                flops=4 << 30, bytes_accessed=8 << 20, transcendentals=0
            ),
            name="scores",
        )(jnp.stack([my_shard, r]).astype(jnp.int32), packed, query_proj, index_emb, chosen)

    with jax.named_scope("reduce_scores"):
        states = lax.all_to_all(state, ("y", "core", *Z), 0, 0, tiled=True)

    with jax.named_scope("attention"):
        answer = dec_query.shape[1]
        heads_here = feats_here // DH
        decoded = dec_query.astype(jnp.float32).reshape(group, answer, heads_here, DH)
        dec_unit = (
            decoded * lax.rsqrt(jnp.mean(decoded * decoded, axis=3, keepdims=True) + EPSILON)
        ).astype(jnp.bfloat16)
        positions = lax.broadcasted_iota(jnp.int32, (group, topk, plen), 2)
        live = (positions < passage_len[:, :, None]).reshape(group, topk * plen)
        packet, own_scores = attention_packet(
            jnp.stack([y, zr, core, r]).astype(jnp.int32),
            tokens,
            key_rows,
            dec_unit.reshape(group, answer, feats_here),
            key_gain.astype(jnp.float32).reshape(1, feats_here),
            live.astype(jnp.float32),
            states,
        )

    with jax.named_scope("targets"):
        packets = lax.all_to_all(packet, NEAR, 0, 0, tiled=True).reshape(nx, n_pair, 2 * LANES)
        coef = pl.pallas_call(
            coef_kernel,
            out_shape=jax.ShapeDtypeStruct((nz, n_pair, LANES), jnp.float32),
            in_specs=[vmem],
            out_specs=vmem,
            name="coef",
        )(packets)
        coef = lax.all_to_all(coef, Z, 0, 0, tiled=True).reshape(n_index, LANES)

    with jax.named_scope("gradient"):
        part = jax.ShapeDtypeStruct((width // ncore, cols), jnp.float32)
        keep, send = pl.pallas_call(
            gradient_kernel,
            out_shape=(part, part),
            in_specs=[vmem] * 2 + [pl.BlockSpec(memory_space=pl.ANY)] * 4,
            out_specs=(vmem, vmem),
            scratch_shapes=[
                pltpu.VMEM((queries, shard_rows), jnp.float32),
                *[pltpu.VMEM(x.shape, x.dtype) for x in (my_rows, my_unit, query_scale, ordered)],
                pltpu.SemaphoreType.DMA((4,)),
            ],
            compiler_params=pltpu.CompilerParams(vmem_limit_bytes=16 << 20),
            name="gradient",
        )(coef, slots, my_rows, my_unit, query_scale, ordered)

    with jax.named_scope("reduce_gradient"):
        term = (keep + shift(send, "core", 1)).reshape(ny, nz * six, cols)
        term = jnp.sum(lax.all_to_all(term, "y", 0, 0, tiled=True), axis=0)
        term = term.reshape(nz, six, cols)
        term = jnp.sum(lax.all_to_all(term, Z, 0, 0, tiled=True), axis=0)
        grad_proj = send_all(term, "reader")
        grad_proj = grad_proj.transpose(1, 0, 2).reshape(six, width)

    mass = jnp.sum(lax.dynamic_index_in_dim(packets, y * ncore + core, 1, False), axis=0)
    my_target = lax.dynamic_slice_in_dim(mass, r * SLOT, topk, 0)
    log_target = jnp.log(my_target)
    retr_loss = jnp.sum(my_target * (log_target - own_scores[0, :topk]))
    slab_best = own_scores[0, topk : topk + 1]
    return (grad_proj, slab_best, retr_loss[None], log_target[None])


def solution(mesh):
    split = Mesh(mesh.devices.reshape(4, 4, 4, 2, 4), INDEX + ("reader",))
    return jax.shard_map(
        body,
        mesh=split,
        in_specs=(
            P(INDEX, None),
            P(INDEX + ("reader",), None),
            P(),
            P(INDEX + ("reader",), None),
            P(INDEX, None),
            P(INDEX, None, None, "reader"),
            P(INDEX, "reader"),
            P("reader"),
            P(INDEX, None, "reader"),
        ),
        out_specs=(
            P(INDEX, None),
            P(INDEX + ("reader",)),
            P(INDEX + ("reader",)),
            P(INDEX + ("reader",), None),
        ),
        check_vma=False,
    )
```

```python
import functools
import math

import jax
import jax.numpy as jnp
from jax import lax
from jax.experimental import pallas as pl
from jax.experimental.pallas import tpu as pltpu
from jax.sharding import Mesh, PartitionSpec as P

HEADS = 64
DH = 64
ANS = 16
EPSILON = 1e-06
SOFTMAX_TEMPER = 0.05
EXACT = lax.Precision.HIGHEST
INDEX = ("y", "zq", "zr", "core")
Z = ("zq", "zr")
NEAR = ("reader", "y", "core")
LANES = 128
SLOT = 32
TILE = 256
N_OWNERS = 128
GRANT = 56 << 20
EARLY = (0, 1, 3)
LATE = 2


def shift(x, axis, step):
    size = lax.axis_size(axis)
    return lax.ppermute(x, axis, [((i + step) % size, i) for i in range(size)])


def send_all(x, axis):
    size = lax.axis_size(axis)
    return lax.all_to_all(jnp.broadcast_to(x[None], (size, *x.shape)), axis, 0, 0, tiled=True)


def halves(x):
    high = x.astype(jnp.bfloat16)
    return high, (x - high.astype(jnp.float32)).astype(jnp.bfloat16)


def dot32(a, b):
    return jnp.dot(a, b, preferred_element_type=jnp.float32)


def load(far, near, sems):
    copies = [pltpu.make_async_copy(a, b, sems.at[i]) for i, (a, b) in enumerate(zip(far, near))]
    for copy in copies:
        copy.start()
    return copies


def like(*arrays):
    return [pltpu.VMEM(x.shape, x.dtype) for x in arrays]


def token_copies(r, chunk, tokens, target, sems):
    own, after, far_low, far_high, before = tokens
    half = target.shape[0] // 2
    low, high = target.at[pl.ds(0, half)], target.at[pl.ds(half, half)]
    for j, block in enumerate((own, after, None, before)):

        @pl.when((r + j) % 4 == chunk)
        def _():
            first = far_low if block is None else block.at[pl.ds(0, half)]
            second = far_high if block is None else block.at[pl.ds(half, half)]
            pltpu.make_async_copy(first, low, sems.at[0]).start()
            pltpu.make_async_copy(second, high, sems.at[1]).start()

    return [
        pltpu.make_async_copy(low, low, sems.at[0]),
        pltpu.make_async_copy(high, high, sems.at[1]),
    ]


def row_copies(place, own, other, target, sem):
    zr, core = place[1], place[2]
    for residue in range(4):
        to = target.at[:, (zr + residue) % 4]
        four = pl.ds(4 * residue, 4)
        pltpu.make_async_copy(own.at[four], to.at[:, core], sem).start()
        pltpu.make_async_copy(other.at[four], to.at[:, 1 - core], sem).start()
    return [pltpu.make_async_copy(target, target, sem)]


def early_keys_kernel(place, *refs):
    tokens, rows, (keys_out, keys, token_v, weight_v, sems) = refs[:5], refs[5:11], refs[11:]
    y, r = place[0], place[3]
    copies = []
    for slot, ahead in enumerate(EARLY):
        own, other = rows[2 * slot], rows[2 * slot + 1]
        waits = row_copies(place, own, other, weight_v.at[slot], sems.at[slot, 0])
        target = token_v.at[slot]
        waits += token_copies(r, (y + ahead) % 4, tokens, target, sems.at[3 + slot])
        copies.append(waits)
    for slot in range(len(EARLY)):
        for copy in copies[slot]:
            copy.wait()

        @pl.loop(0, keys.shape[1] // TILE)
        def _(t):
            cols = pl.ds(pl.multiple_of(t * TILE, TILE), TILE)
            term = dot32(token_v[slot], weight_v[slot, :, :, :, :, cols].reshape(-1, TILE))
            if slot == 0:
                keys[:, cols] = term
            else:
                keys[:, cols] += term

    copy = pltpu.make_async_copy(keys, keys_out, sems.at[0, 0])
    copy.start()
    copy.wait()


def attend(keys, offset, dec, gain, live, column_v):
    group, n = dec.shape[0], live.shape[1]
    cols = pl.ds(pl.multiple_of(offset, TILE), TILE)
    same = (
        lax.broadcasted_iota(jnp.int32, (TILE, TILE), 0) // DH
        == lax.broadcasted_iota(jnp.int32, (TILE, TILE), 1) // DH
    ).astype(jnp.bfloat16)
    mine = (
        lax.broadcasted_iota(jnp.int32, (TILE // DH * ANS, TILE), 0) // ANS
        == lax.broadcasted_iota(jnp.int32, (TILE // DH * ANS, TILE), 1) // DH
    )
    high, low = halves(keys * keys)
    square = (dot32(high, same) + dot32(low, same)) / DH
    unit = (keys * lax.rsqrt(square + EPSILON) * gain[:, cols]).astype(jnp.bfloat16)
    for g in range(group):
        answer = dec[g, :, cols].astype(jnp.float32)
        answer = jnp.concatenate([answer] * (TILE // DH), axis=0)
        answer = jnp.where(mine, answer, 0.0).astype(jnp.bfloat16)
        similarity = lax.dot_general(
            answer,
            unit[g * n : (g + 1) * n],
            (((1,), (1,)), ((), ())),
            preferred_element_type=jnp.float32,
        ) / math.sqrt(DH)
        weight = jnp.where(live[g : g + 1, :] > 0, jnp.exp(similarity), 0.0)
        weight = weight / jnp.sum(weight, axis=1, keepdims=True)
        column_v[g : g + 1, :] += jnp.sum(weight, axis=0, keepdims=True)


def late_heads_kernel(place, *refs):
    tokens, (own, other), refs = refs[:5], refs[5:7], refs[7:]
    far, (out, own_scores), near, refs = refs[:5], refs[5:7], refs[7:12], refs[12:]
    token_v, weight_v, column_v, load_sems, sems = refs
    y, r = place[0], place[3]
    loads = load(far, near, load_sems)
    early, dec, gain, live, states = near
    copies = row_copies(place, own, other, weight_v, sems.at[0, 0])
    copies += token_copies(r, (y + LATE) % 4, tokens, token_v, sems.at[1])
    column_v[...] = jnp.zeros_like(column_v)

    lane = lax.broadcasted_iota(jnp.int32, (1, LANES), 1)
    for copy in loads:
        copy.wait()
    found = states[...]
    fetched = jnp.where(lane < 20, jnp.sum(found, axis=0, keepdims=True), 0.0)
    expo = jnp.where(lane < 20, jnp.exp(fetched), 0.0)
    total = jnp.sum(expo, axis=1, keepdims=True)
    log_prob = fetched - jnp.log(total)
    best = jnp.max(found, axis=0, keepdims=True)
    own_scores[...] = jnp.broadcast_to(jnp.where(lane == 20, best, log_prob), own_scores.shape)
    scores = expo / total + pltpu.roll(fetched, LANES // 2, 1)
    out[:, LANES:] = jnp.broadcast_to(scores, (out.shape[0], LANES))

    for copy in copies:
        copy.wait()

    @pl.loop(0, early.shape[1] // TILE)
    def _(t):
        cols = pl.ds(pl.multiple_of(t * TILE, TILE), TILE)
        keys = early[:, cols] + dot32(token_v[...], weight_v[:, :, :, :, cols].reshape(-1, TILE))
        attend(keys, t * TILE, dec, gain, live, column_v)

    n = live.shape[1]
    mass = jnp.zeros((8, LANES), jnp.float32)
    for g in range(dec.shape[0]):
        column = jnp.broadcast_to(column_v[g : g + 1, :], (8, n))
        to = (
            lax.broadcasted_iota(jnp.int32, (n, LANES), 0) // 8 + g * SLOT
            == lax.broadcasted_iota(jnp.int32, (n, LANES), 1)
        ).astype(jnp.float32)
        mass += jnp.dot(column, to, precision=EXACT, preferred_element_type=jnp.float32)
    out[:, :LANES] = jnp.broadcast_to(mass[:1] / (HEADS * ANS), (out.shape[0], LANES))


def attention_packet(place, tokens, rows, dec, gain, live, states):
    vmem = pl.BlockSpec(memory_space=pltpu.VMEM)
    anywhere = pl.BlockSpec(memory_space=pl.ANY)
    smem = pl.BlockSpec(memory_space=pltpu.SMEM)
    token_rows, width = tokens[0].shape
    block = (4, 4, 2, *rows[0][0].shape[1:])

    def cost(count, size):
        return pl.CostEstimate(
            flops=2 * token_rows * count * width * width,
            bytes_accessed=size << 20,
            transcendentals=0,
        )

    early = pl.pallas_call(
        early_keys_kernel,
        out_shape=jax.ShapeDtypeStruct((token_rows, width), jnp.float32),
        in_specs=[smem] + [anywhere] * 11,
        out_specs=anywhere,
        scratch_shapes=[
            pltpu.VMEM((token_rows, width), jnp.float32),
            pltpu.VMEM((3, token_rows, width), jnp.bfloat16),
            pltpu.VMEM((3, *block), jnp.bfloat16),
            pltpu.SemaphoreType.DMA((6, 2)),
        ],
        compiler_params=pltpu.CompilerParams(vmem_limit_bytes=GRANT),
        cost_estimate=cost(12, 13),
        name="early_keys",
    )(place, *tokens, *[part for ahead in EARLY for part in rows[ahead]])
    return pl.pallas_call(
        late_heads_kernel,
        out_shape=(
            jax.ShapeDtypeStruct((32, 2 * LANES), jnp.float32),
            jax.ShapeDtypeStruct((8, LANES), jnp.float32),
        ),
        in_specs=[smem] + [anywhere] * 12,
        out_specs=(vmem, vmem),
        scratch_shapes=[
            *like(early, dec, gain, live, states),
            pltpu.VMEM((token_rows, width), jnp.bfloat16),
            pltpu.VMEM(block, jnp.bfloat16),
            pltpu.VMEM((8, live.shape[1]), jnp.float32),
            pltpu.SemaphoreType.DMA((5,)),
            pltpu.SemaphoreType.DMA((2, 2)),
        ],
        compiler_params=pltpu.CompilerParams(vmem_limit_bytes=GRANT),
        cost_estimate=cost(1, 6),
        name="late_heads",
    )(place, *tokens, *rows[LATE], early, dec, gain, live, states)


def scores_kernel(place, *refs):
    far, (state, *outs), near, refs = refs[:4], refs[4:10], refs[10:14], refs[14:]
    near_outs, (unit_v, ids_v, sems) = refs[:5], refs[5:]
    copies = load(far, near, sems)
    packed, proj, emb, chosen = near
    slots, rows, unit, scale, ordered = near_outs
    shard, r = place[0], place[1]
    n_rows, width = emb.shape
    per_x = state.shape[0]
    cols = rows.shape[1]
    for copy in copies:
        copy.wait()
    feats = packed[:, :, :width].reshape(4 * per_x, width)
    ordered[...] = lax.dot_general(
        chosen[...], feats, (((1,), (1,)), ((), ())), preferred_element_type=jnp.float32
    ).astype(jnp.bfloat16)

    lane = lax.broadcasted_iota(jnp.int32, (per_x, LANES), 1)
    spread = jnp.full((per_x, LANES), -1, jnp.int32)
    for x in range(4):
        coded = packed[8 * x : 8 * x + 8, :, width : width + LANES].reshape(per_x, LANES)
        coded = coded.astype(jnp.float32)
        ids = coded * 256 + pltpu.roll(coded, LANES // 2, 1)
        ids = ids.astype(jnp.int32) - shard * n_rows
        ids_v[x] = ids
        moved = ids if x == 0 else pltpu.roll(ids, SLOT * x, 1)
        spread = jnp.where((lane // SLOT == x) & (lane % SLOT < 20), moved, spread)
    slots[...] = spread

    vec = dot32(feats, proj[...])
    scale_all = lax.rsqrt(jnp.sum(vec * vec, axis=1, keepdims=True) + EPSILON)
    scale[...] = scale_all
    unit_all = vec * scale_all
    unit_v[...] = unit_all
    emb_all = emb[...]
    row_unit = emb_all * lax.rsqrt(jnp.sum(emb_all * emb_all, axis=1, keepdims=True) + EPSILON)
    for x in range(4):

        @pl.when(r == x)
        def _():
            rows[...] = row_unit[:, x * cols : (x + 1) * cols]
            unit[...] = unit_all[:, x * cols : (x + 1) * cols]

    copies = load(near_outs, outs, sems)
    share = unit_v[pl.ds(pl.multiple_of(r * per_x, per_x), per_x), :]
    found = (
        lax.dot_general(
            share,
            row_unit,
            (((1,), (1,)), ((), ())),
            precision=EXACT,
            preferred_element_type=jnp.float32,
        )
        / SOFTMAX_TEMPER
    )
    places = ids_v[r]
    row = lax.broadcasted_iota(jnp.int32, (per_x, n_rows), 1)
    total = jnp.where(lane == 20, jnp.max(found, axis=1, keepdims=True), 0.0)
    for k in range(20):
        picked = jnp.where(places[:, k : k + 1] == row, found, 0.0)
        total = jnp.where(lane == k, jnp.sum(picked, axis=1, keepdims=True), total)
    state[...] = total
    for copy in copies:
        copy.wait()


def coef_kernel(packets, out):
    lane = lax.broadcasted_iota(jnp.int32, (8, LANES), 1)
    target = prob = fetched = jnp.zeros((8, LANES), jnp.float32)
    for x in range(4):
        target += packets[x, :, :LANES]
        scores = packets[x, :, LANES:]
        own = (lane // SLOT == x) & (lane % SLOT < 20)
        moved = scores if x == 0 else pltpu.roll(scores, SLOT * x, 1)
        prob += jnp.where(own, moved, 0.0)
        moved = pltpu.roll(scores, (SLOT * x + LANES // 2) % LANES, 1)
        fetched += jnp.where(own, moved, 0.0)
    gap = prob - target
    to = (
        lax.broadcasted_iota(jnp.int32, (LANES, LANES), 0) // SLOT * SLOT + 20
        == lax.broadcasted_iota(jnp.int32, (LANES, LANES), 1)
    ).astype(jnp.float32)
    along = jnp.dot(gap * fetched, to, precision=EXACT, preferred_element_type=jnp.float32)
    packed = gap / SOFTMAX_TEMPER + along / N_OWNERS
    out[...] = jnp.broadcast_to(packed[None], out.shape)


def gradient_kernel(coef, *refs):
    far, (keep, send, matrix_v), near, sems = refs[:5], refs[5:8], refs[8:13], refs[13]
    copies = load(far, near, sems)
    slot, rows, unit, scale, ordered = near
    copies[0].wait()
    n_rows = matrix_v.shape[1]
    blocks = coef.shape[0]

    @pl.loop(0, blocks // 8)
    def _(b):
        eight = pl.ds(pl.multiple_of(b * 8, 8), 8)
        row = lax.broadcasted_iota(jnp.int32, (8, n_rows), 1)
        values = coef[pl.ds(b // 2 + b % 2 * 64, 8, stride=8), :]
        places = slot[eight, :]
        for x in range(4):
            total = jnp.zeros((8, n_rows), jnp.float32)
            for k in range(SLOT * x, SLOT * x + 20):
                total += jnp.where(places[:, k : k + 1] == row, values[:, k : k + 1], 0.0)
            matrix_v[pl.ds(pl.multiple_of(x * blocks + b * 8, 8), 8), :] = total

    for copy in copies[1:]:
        copy.wait()
    along_all = jnp.concatenate([coef[pl.ds(p, 16, stride=8), :] for p in range(8)], axis=0)
    row_high, row_low = halves(rows[...])
    parts_high, parts_low = [], []
    for x in range(4):
        mine = slice(x * blocks, (x + 1) * blocks)
        high, low = halves(matrix_v[mine, :])
        part = dot32(high, row_high) + (dot32(high, row_low) + dot32(low, row_high))
        along = along_all[:, SLOT * x + 20 : SLOT * x + 21]
        part = (part - unit[mine, :] * along) * scale[mine, :]
        high, low = halves(part)
        parts_high.append(high)
        parts_low.append(low)
    high, low = jnp.concatenate(parts_high, axis=0), jnp.concatenate(parts_low, axis=0)
    half = keep.shape[0]
    keep[...] = dot32(ordered[:half, :], high) + dot32(ordered[:half, :], low)
    send[...] = dot32(ordered[half:, :], high) + dot32(ordered[half:, :], low)


def body(
    index_emb,
    query_feat,
    query_proj,
    passage_id,
    passage_len,
    enc_out,
    key_proj,
    key_gain,
    dec_query,
):
    y, zq, zr, core, r = (lax.axis_index(a) for a in (*INDEX, "reader"))
    ny, nz, ncore, nx = 4, 16, 2, 4
    z = zq * 4 + zr
    n_index = ny * nz * ncore
    n_pair = ny * ncore
    my_shard = (y * nz + z) * ncore + core
    shard_rows, width = index_emb.shape
    topk = passage_id.shape[1]

    group, _, plen, feats_here = enc_out.shape
    token_rows = group * topk * plen
    with jax.named_scope("gather_enc_out"):
        own = enc_out.reshape(token_rows, feats_here)
        after, before = shift(own, "reader", 1), shift(own, "reader", -1)
        mid = token_rows // 2
        far_low, far_high = shift(after[:mid], "reader", 1), shift(before[mid:], "reader", -1)
        tokens = (own, after, far_low, far_high, before)

    with jax.named_scope("gather_key_proj"):
        own = send_all(key_proj, "zq")
        own, query_feat, passage_id = lax.optimization_barrier((own, query_feat, passage_id))
        after, before = shift(own, Z, 1), shift(own, Z, -1)
        far = [shift(own[:2], Z, 2), shift(own[2:], Z, -2)]
        own = jnp.concatenate([own, after, *far, before])
        after, before = shift(own, "y", 1), shift(own, "y", -1)
        far = jnp.concatenate([shift(after[:8], "y", 1), shift(before[8:], "y", -1)])
        key_rows = [(block, shift(block, "core", 1)) for block in (own, after, far, before)]

    with jax.named_scope("gather_queries"):
        ids_high = (passage_id // 256).astype(jnp.bfloat16)
        ids_low = (passage_id % 256).astype(jnp.bfloat16)
        gap = ((0, 0), (0, LANES // 2 - topk))
        coded = [query_feat, jnp.pad(ids_high, gap), jnp.pad(ids_low, gap)]
        packed = send_all(send_all(jnp.concatenate(coded, axis=1)[0], Z), NEAR)

    cols = width // nx
    six = width // n_index
    place = lax.broadcasted_iota(jnp.int32, (width, 1), 0)
    to_core, to_y = place // (ny * nz * six), place // (nz * six) % ny
    to_z, within = place // six % nz, place % six
    column = ((to_y * nz + to_z) * ncore + (to_core + core) % ncore) * six + within
    chosen = (lax.broadcasted_iota(jnp.int32, (1, width), 1) == column).astype(jnp.bfloat16)

    vmem = pl.BlockSpec(memory_space=pltpu.VMEM)
    with jax.named_scope("scores"):
        queries = n_index * nx
        operands = (packed, query_proj, index_emb, chosen)
        results = (
            jax.ShapeDtypeStruct((n_index, LANES), jnp.int32),
            jax.ShapeDtypeStruct((shard_rows, cols), jnp.float32),
            jax.ShapeDtypeStruct((queries, cols), jnp.float32),
            jax.ShapeDtypeStruct((queries, 1), jnp.float32),
            jax.ShapeDtypeStruct((width, queries), jnp.bfloat16),
        )
        anywhere = pl.BlockSpec(memory_space=pl.ANY)
        state, slots, my_rows, my_unit, query_scale, ordered = pl.pallas_call(
            scores_kernel,
            out_shape=(jax.ShapeDtypeStruct((n_index, LANES), jnp.float32), *results),
            in_specs=[pl.BlockSpec(memory_space=pltpu.SMEM)] + [anywhere] * 4,
            out_specs=(vmem,) + (anywhere,) * 5,
            scratch_shapes=[
                *like(*operands, *results),
                pltpu.VMEM((queries, width), jnp.float32),
                pltpu.VMEM((nx, n_index, LANES), jnp.int32),
                pltpu.SemaphoreType.DMA((5,)),
            ],
            compiler_params=pltpu.CompilerParams(vmem_limit_bytes=GRANT),
            cost_estimate=pl.CostEstimate(
                flops=64 << 30, bytes_accessed=8 << 20, transcendentals=0
            ),
            name="scores",
        )(jnp.stack([my_shard, r]).astype(jnp.int32), *operands)

    with jax.named_scope("reduce_scores"):
        states = lax.all_to_all(state, ("y", "core", *Z), 0, 0, tiled=True)

    with jax.named_scope("attention"):
        answer = dec_query.shape[1]
        heads_here = feats_here // DH
        decoded = dec_query.astype(jnp.float32).reshape(group, answer, heads_here, DH)
        dec_unit = (
            decoded * lax.rsqrt(jnp.mean(decoded * decoded, axis=3, keepdims=True) + EPSILON)
        ).astype(jnp.bfloat16)
        positions = lax.broadcasted_iota(jnp.int32, (group, topk, plen), 2)
        live = (positions < passage_len[:, :, None]).reshape(group, topk * plen)
        packet, own_scores = attention_packet(
            jnp.stack([y, zr, core, r]).astype(jnp.int32),
            tokens,
            key_rows,
            dec_unit.reshape(group, answer, feats_here),
            key_gain.astype(jnp.float32).reshape(1, feats_here),
            live.astype(jnp.float32),
            states,
        )

    with jax.named_scope("targets"):
        packets = lax.all_to_all(packet, NEAR, 0, 0, tiled=True).reshape(nx, n_pair, 2 * LANES)
        coef = pl.pallas_call(
            coef_kernel,
            out_shape=jax.ShapeDtypeStruct((nz, n_pair, LANES), jnp.float32),
            in_specs=[vmem],
            out_specs=vmem,
            name="coef",
        )(packets)
        coef = lax.all_to_all(coef, Z, 0, 0, tiled=True).reshape(n_index, LANES)

    with jax.named_scope("gradient"):
        part = jax.ShapeDtypeStruct((width // ncore, cols), jnp.float32)
        keep, send = pl.pallas_call(
            gradient_kernel,
            out_shape=(part, part),
            in_specs=[vmem] + [anywhere] * 5,
            out_specs=(vmem, vmem),
            scratch_shapes=[
                pltpu.VMEM((queries, shard_rows), jnp.float32),
                *like(slots, my_rows, my_unit, query_scale, ordered),
                pltpu.SemaphoreType.DMA((5,)),
            ],
            compiler_params=pltpu.CompilerParams(vmem_limit_bytes=GRANT),
            name="gradient",
        )(coef, slots, my_rows, my_unit, query_scale, ordered)

    with jax.named_scope("reduce_gradient"):
        term = (keep + shift(send, "core", 1)).reshape(ny, nz * six, cols)
        term = jnp.sum(lax.all_to_all(term, "y", 0, 0, tiled=True), axis=0)
        term = term.reshape(nz, six, cols)
        term = jnp.sum(lax.all_to_all(term, Z, 0, 0, tiled=True), axis=0)
        grad_proj = send_all(term, "reader")
        grad_proj = grad_proj.transpose(1, 0, 2).reshape(six, width)

    mass = jnp.sum(lax.dynamic_index_in_dim(packets, y * ncore + core, 1, False), axis=0)
    my_target = lax.dynamic_slice_in_dim(mass, r * SLOT, topk, 0)
    log_target = jnp.log(my_target)
    retr_loss = jnp.sum(my_target * (log_target - own_scores[0, :topk]))
    slab_best = own_scores[0, topk : topk + 1]
    return (grad_proj, slab_best, retr_loss[None], log_target[None])


def solution(mesh):
    split = Mesh(mesh.devices.reshape(4, 4, 4, 2, 4), INDEX + ("reader",))
    return jax.shard_map(
        body,
        mesh=split,
        in_specs=(
            P(INDEX, None),
            P(INDEX + ("reader",), None),
            P(),
            P(INDEX + ("reader",), None),
            P(INDEX, None),
            P(INDEX, None, None, "reader"),
            P(INDEX, "reader"),
            P("reader"),
            P(INDEX, None, "reader"),
        ),
        out_specs=(
            P(INDEX, None),
            P(INDEX + ("reader",)),
            P(INDEX + ("reader",)),
            P(INDEX + ("reader",), None),
        ),
        check_vma=False,
    )
```

```python
import functools
import math

import jax
import jax.numpy as jnp
from jax import lax
from jax.experimental import pallas as pl
from jax.experimental.pallas import tpu as pltpu
from jax.sharding import Mesh, PartitionSpec as P

HEADS = 64
DH = 64
ANS = 16
EPSILON = 1e-06
SOFTMAX_TEMPER = 0.05
EXACT = lax.Precision.HIGHEST
INDEX = ("y", "zq", "zr", "core")
Z = ("zq", "zr")
Z_BY_CLASS = ("zr", "zq")
NEAR = ("reader", "y", "core")
LANES = 128
SLOT = 32
TILE = 256
N_OWNERS = 128
GRANT = 56 << 20
EARLY = (0, 1, 3)
LATE = 2


def shift(x, axis, step):
    size = lax.axis_size(axis)
    return lax.ppermute(x, axis, [((i + step) % size, i) for i in range(size)])


def send_all(x, axis):
    size = lax.axis_size(axis)
    return lax.all_to_all(jnp.broadcast_to(x[None], (size, *x.shape)), axis, 0, 0, tiled=True)


def halves(x):
    high = x.astype(jnp.bfloat16)
    return high, (x - high.astype(jnp.float32)).astype(jnp.bfloat16)


def dot32(a, b):
    return jnp.dot(a, b, preferred_element_type=jnp.float32)


def load(far, near, sems):
    copies = [pltpu.make_async_copy(a, b, sems.at[i]) for i, (a, b) in enumerate(zip(far, near))]
    for copy in copies:
        copy.start()
    return copies


def like(*arrays):
    return [pltpu.VMEM(x.shape, x.dtype) for x in arrays]


def token_copies(r, chunk, tokens, target, sems):
    own, after, far_low, far_high, before = tokens
    half = target.shape[0] // 2
    low, high = target.at[pl.ds(0, half)], target.at[pl.ds(half, half)]
    for j, block in enumerate((own, after, None, before)):

        @pl.when((r + j) % 4 == chunk)
        def _():
            first = far_low if block is None else block.at[pl.ds(0, half)]
            second = far_high if block is None else block.at[pl.ds(half, half)]
            pltpu.make_async_copy(first, low, sems.at[0]).start()
            pltpu.make_async_copy(second, high, sems.at[1]).start()

    return [
        pltpu.make_async_copy(low, low, sems.at[0]),
        pltpu.make_async_copy(high, high, sems.at[1]),
    ]


def row_copies(place, own, other, target, sem):
    zr, core = place[1], place[2]
    for residue in range(4):
        to = target.at[:, (zr + residue) % 4]
        four = pl.ds(4 * residue, 4)
        pltpu.make_async_copy(own.at[four], to.at[:, core], sem).start()
        pltpu.make_async_copy(other.at[four], to.at[:, 1 - core], sem).start()
    return [pltpu.make_async_copy(target, target, sem)]


def early_keys_kernel(place, *refs):
    tokens, rows, (keys_out, keys, token_v, weight_v, sems) = refs[:5], refs[5:11], refs[11:]
    y, r = place[0], place[3]
    copies = []
    for slot, ahead in enumerate(EARLY):
        own, other = rows[2 * slot], rows[2 * slot + 1]
        waits = row_copies(place, own, other, weight_v.at[slot], sems.at[slot, 0])
        target = token_v.at[slot]
        waits += token_copies(r, (y + ahead) % 4, tokens, target, sems.at[3 + slot])
        copies.append(waits)
    for slot in range(len(EARLY)):
        for copy in copies[slot]:
            copy.wait()

        @pl.loop(0, keys.shape[1] // TILE)
        def _(t):
            cols = pl.ds(pl.multiple_of(t * TILE, TILE), TILE)
            term = dot32(token_v[slot], weight_v[slot, :, :, :, :, cols].reshape(-1, TILE))
            if slot == 0:
                keys[:, cols] = term
            else:
                keys[:, cols] += term

    copy = pltpu.make_async_copy(keys, keys_out, sems.at[0, 0])
    copy.start()
    copy.wait()


def attend(keys, offset, dec, gain, live, column_v):
    group, n = dec.shape[0], live.shape[1]
    cols = pl.ds(pl.multiple_of(offset, TILE), TILE)
    same = (
        lax.broadcasted_iota(jnp.int32, (TILE, TILE), 0) // DH
        == lax.broadcasted_iota(jnp.int32, (TILE, TILE), 1) // DH
    ).astype(jnp.bfloat16)
    mine = (
        lax.broadcasted_iota(jnp.int32, (TILE // DH * ANS, TILE), 0) // ANS
        == lax.broadcasted_iota(jnp.int32, (TILE // DH * ANS, TILE), 1) // DH
    )
    high, low = halves(keys * keys)
    square = (dot32(high, same) + dot32(low, same)) / DH
    unit = (keys * lax.rsqrt(square + EPSILON) * gain[:, cols]).astype(jnp.bfloat16)
    for g in range(group):
        answer = dec[g, :, cols].astype(jnp.float32)
        answer = jnp.concatenate([answer] * (TILE // DH), axis=0)
        answer = jnp.where(mine, answer, 0.0).astype(jnp.bfloat16)
        similarity = lax.dot_general(
            answer,
            unit[g * n : (g + 1) * n],
            (((1,), (1,)), ((), ())),
            preferred_element_type=jnp.float32,
        ) / math.sqrt(DH)
        weight = jnp.where(live[g : g + 1, :] > 0, jnp.exp(similarity), 0.0)
        weight = weight / jnp.sum(weight, axis=1, keepdims=True)
        column_v[g : g + 1, :] += jnp.sum(weight, axis=0, keepdims=True)


def late_heads_kernel(place, *refs):
    tokens, (own, other), refs = refs[:5], refs[5:7], refs[7:]
    far, (out, own_scores), near, refs = refs[:5], refs[5:7], refs[7:12], refs[12:]
    token_v, weight_v, column_v, load_sems, sems = refs
    y, r = place[0], place[3]
    loads = load(far, near, load_sems)
    early, dec, gain, live, states = near
    copies = row_copies(place, own, other, weight_v, sems.at[0, 0])
    copies += token_copies(r, (y + LATE) % 4, tokens, token_v, sems.at[1])
    column_v[...] = jnp.zeros_like(column_v)

    lane = lax.broadcasted_iota(jnp.int32, (1, LANES), 1)
    for copy in loads:
        copy.wait()
    found = states[...]
    fetched = jnp.where(lane < 20, jnp.sum(found, axis=0, keepdims=True), 0.0)
    expo = jnp.where(lane < 20, jnp.exp(fetched), 0.0)
    total = jnp.sum(expo, axis=1, keepdims=True)
    log_prob = fetched - jnp.log(total)
    best = jnp.max(found, axis=0, keepdims=True)
    own_scores[...] = jnp.broadcast_to(jnp.where(lane == 20, best, log_prob), own_scores.shape)
    scores = expo / total + pltpu.roll(fetched, LANES // 2, 1)
    out[:, LANES:] = jnp.broadcast_to(scores, (out.shape[0], LANES))

    for copy in copies:
        copy.wait()

    @pl.loop(0, early.shape[1] // TILE)
    def _(t):
        cols = pl.ds(pl.multiple_of(t * TILE, TILE), TILE)
        keys = early[:, cols] + dot32(token_v[...], weight_v[:, :, :, :, cols].reshape(-1, TILE))
        attend(keys, t * TILE, dec, gain, live, column_v)

    n = live.shape[1]
    mass = jnp.zeros((8, LANES), jnp.float32)
    for g in range(dec.shape[0]):
        column = jnp.broadcast_to(column_v[g : g + 1, :], (8, n))
        to = (
            lax.broadcasted_iota(jnp.int32, (n, LANES), 0) // 8 + g * SLOT
            == lax.broadcasted_iota(jnp.int32, (n, LANES), 1)
        ).astype(jnp.float32)
        mass += jnp.dot(column, to, precision=EXACT, preferred_element_type=jnp.float32)
    out[:, :LANES] = jnp.broadcast_to(mass[:1] / (HEADS * ANS), (out.shape[0], LANES))


def attention_packet(place, tokens, rows, dec, gain, live, states):
    vmem = pl.BlockSpec(memory_space=pltpu.VMEM)
    anywhere = pl.BlockSpec(memory_space=pl.ANY)
    smem = pl.BlockSpec(memory_space=pltpu.SMEM)
    token_rows, width = tokens[0].shape
    block = (4, 4, 2, *rows[0][0].shape[1:])

    def cost(count, size):
        return pl.CostEstimate(
            flops=2 * token_rows * count * width * width,
            bytes_accessed=size << 20,
            transcendentals=0,
        )

    early = pl.pallas_call(
        early_keys_kernel,
        out_shape=jax.ShapeDtypeStruct((token_rows, width), jnp.float32),
        in_specs=[smem] + [anywhere] * 11,
        out_specs=anywhere,
        scratch_shapes=[
            pltpu.VMEM((token_rows, width), jnp.float32),
            pltpu.VMEM((3, token_rows, width), jnp.bfloat16),
            pltpu.VMEM((3, *block), jnp.bfloat16),
            pltpu.SemaphoreType.DMA((6, 2)),
        ],
        compiler_params=pltpu.CompilerParams(vmem_limit_bytes=GRANT),
        cost_estimate=cost(12, 13),
        name="early_keys",
    )(place, *tokens, *[part for ahead in EARLY for part in rows[ahead]])
    return pl.pallas_call(
        late_heads_kernel,
        out_shape=(
            jax.ShapeDtypeStruct((32, 2 * LANES), jnp.float32),
            jax.ShapeDtypeStruct((8, LANES), jnp.float32),
        ),
        in_specs=[smem] + [anywhere] * 12,
        out_specs=(vmem, vmem),
        scratch_shapes=[
            *like(early, dec, gain, live, states),
            pltpu.VMEM((token_rows, width), jnp.bfloat16),
            pltpu.VMEM(block, jnp.bfloat16),
            pltpu.VMEM((8, live.shape[1]), jnp.float32),
            pltpu.SemaphoreType.DMA((5,)),
            pltpu.SemaphoreType.DMA((2, 2)),
        ],
        compiler_params=pltpu.CompilerParams(vmem_limit_bytes=GRANT),
        cost_estimate=cost(1, 6),
        name="late_heads",
    )(place, *tokens, *rows[LATE], early, dec, gain, live, states)


def scores_kernel(place, *refs):
    far, (state, *outs), near, refs = refs[:4], refs[4:10], refs[10:14], refs[14:]
    near_outs, (unit_v, ids_v, sems) = refs[:5], refs[5:]
    copies = load(far, near, sems)
    packed, proj, emb, chosen = near
    slots, rows, unit, scale, ordered = near_outs
    shard, r = place[0], place[1]
    n_rows, width = emb.shape
    per_x = state.shape[0]
    cols = rows.shape[1]
    for copy in copies:
        copy.wait()
    feats = packed[:, :, :width].reshape(4 * per_x, width)
    ordered[...] = lax.dot_general(
        chosen[...], feats, (((1,), (1,)), ((), ())), preferred_element_type=jnp.float32
    ).astype(jnp.bfloat16)

    lane = lax.broadcasted_iota(jnp.int32, (per_x, LANES), 1)
    spread = jnp.full((per_x, LANES), -1, jnp.int32)
    for x in range(4):
        coded = packed[8 * x : 8 * x + 8, :, width : width + LANES].reshape(per_x, LANES)
        coded = coded.astype(jnp.float32)
        ids = coded * 256 + pltpu.roll(coded, LANES // 2, 1)
        ids = ids.astype(jnp.int32) - shard * n_rows
        ids_v[x] = ids
        moved = ids if x == 0 else pltpu.roll(ids, SLOT * x, 1)
        spread = jnp.where((lane // SLOT == x) & (lane % SLOT < 20), moved, spread)
    slots[...] = spread

    vec = dot32(feats, proj[...])
    scale_all = lax.rsqrt(jnp.sum(vec * vec, axis=1, keepdims=True) + EPSILON)
    spread = jnp.zeros((per_x, LANES), jnp.float32)
    for x in range(4):
        spread = jnp.where(lane // SLOT == x, scale_all[x * per_x : (x + 1) * per_x], spread)
    scale[...] = spread
    unit_all = vec * scale_all
    unit_v[...] = unit_all
    emb_all = emb[...]
    row_unit = emb_all * lax.rsqrt(jnp.sum(emb_all * emb_all, axis=1, keepdims=True) + EPSILON)
    for x in range(4):

        @pl.when(r == x)
        def _():
            rows[...] = row_unit[:, x * cols : (x + 1) * cols]
            unit[...] = unit_all[:, x * cols : (x + 1) * cols]

    copies = load(near_outs, outs, sems)
    share = unit_v[pl.ds(pl.multiple_of(r * per_x, per_x), per_x), :]
    found = (
        lax.dot_general(
            share,
            row_unit,
            (((1,), (1,)), ((), ())),
            precision=EXACT,
            preferred_element_type=jnp.float32,
        )
        / SOFTMAX_TEMPER
    )
    places = ids_v[r]
    row = lax.broadcasted_iota(jnp.int32, (per_x, n_rows), 1)
    total = jnp.where(lane == 20, jnp.max(found, axis=1, keepdims=True), 0.0)
    for k in range(20):
        picked = jnp.where(places[:, k : k + 1] == row, found, 0.0)
        total = jnp.where(lane == k, jnp.sum(picked, axis=1, keepdims=True), total)
    state[...] = total
    for copy in copies:
        copy.wait()


def coef_kernel(packets, out):
    lane = lax.broadcasted_iota(jnp.int32, (8, LANES), 1)
    target = prob = fetched = jnp.zeros((8, LANES), jnp.float32)
    for x in range(4):
        target += packets[x, :, :LANES]
        scores = packets[x, :, LANES:]
        own = (lane // SLOT == x) & (lane % SLOT < 20)
        moved = scores if x == 0 else pltpu.roll(scores, SLOT * x, 1)
        prob += jnp.where(own, moved, 0.0)
        moved = pltpu.roll(scores, (SLOT * x + LANES // 2) % LANES, 1)
        fetched += jnp.where(own, moved, 0.0)
    gap = prob - target
    to = (
        lax.broadcasted_iota(jnp.int32, (LANES, LANES), 0) // SLOT * SLOT + 20
        == lax.broadcasted_iota(jnp.int32, (LANES, LANES), 1)
    ).astype(jnp.float32)
    along = jnp.dot(gap * fetched, to, precision=EXACT, preferred_element_type=jnp.float32)
    packed = gap / SOFTMAX_TEMPER + along / N_OWNERS
    out[...] = jnp.broadcast_to(packed[None], out.shape)


def gradient_kernel(coef, *refs):
    far, (keep, send, matrix_v), near, sems = refs[:5], refs[5:8], refs[8:13], refs[13]
    copies = load(far, near, sems)
    slot, scale, rows, unit, ordered = near
    copies[0].wait()
    copies[1].wait()
    n_rows = matrix_v.shape[1]
    blocks = coef.shape[0]

    @pl.loop(0, blocks // 8)
    def _(b):
        eight = pl.ds(pl.multiple_of(b * 8, 8), 8)
        row = lax.broadcasted_iota(jnp.int32, (8, n_rows), 1)
        values = coef[pl.ds(b // 2 + b % 2 * 64, 8, stride=8), :] * scale[eight, :]
        places = slot[eight, :]
        for x in range(4):
            total = jnp.zeros((8, n_rows), jnp.float32)
            for k in range(SLOT * x, SLOT * x + 20):
                total += jnp.where(places[:, k : k + 1] == row, values[:, k : k + 1], 0.0)
            matrix_v[pl.ds(pl.multiple_of(x * blocks + b * 8, 8), 8), :] = total

    for copy in copies[2:]:
        copy.wait()
    along_all = jnp.concatenate([coef[pl.ds(p, 16, stride=8), :] for p in range(8)], axis=0)
    along_all = along_all * scale[...]
    row_high, row_low = halves(rows[...])
    parts_high, parts_low = [], []
    for x in range(4):
        mine = slice(x * blocks, (x + 1) * blocks)
        high, low = halves(matrix_v[mine, :])
        part = dot32(high, row_high) + (dot32(high, row_low) + dot32(low, row_high))
        along = along_all[:, SLOT * x + 20 : SLOT * x + 21]
        part = part - unit[mine, :] * along
        high, low = halves(part)
        parts_high.append(high)
        parts_low.append(low)
    high, low = jnp.concatenate(parts_high, axis=0), jnp.concatenate(parts_low, axis=0)
    half = keep.shape[0]
    keep[...] = dot32(ordered[:half, :], high) + dot32(ordered[:half, :], low)
    send[...] = dot32(ordered[half:, :], high) + dot32(ordered[half:, :], low)


def body(
    index_emb,
    query_feat,
    query_proj,
    passage_id,
    passage_len,
    enc_out,
    key_proj,
    key_gain,
    dec_query,
):
    y, zq, zr, core, r = (lax.axis_index(a) for a in (*INDEX, "reader"))
    ny, nz, ncore, nx = 4, 16, 2, 4
    z = zq * 4 + zr
    n_index = ny * nz * ncore
    n_pair = ny * ncore
    my_shard = (y * nz + z) * ncore + core
    shard_rows, width = index_emb.shape
    topk = passage_id.shape[1]

    group, _, plen, feats_here = enc_out.shape
    token_rows = group * topk * plen
    with jax.named_scope("gather_enc_out"):
        own = enc_out.reshape(token_rows, feats_here)
        after, before = shift(own, "reader", 1), shift(own, "reader", -1)
        mid = token_rows // 2
        far_low, far_high = shift(after[:mid], "reader", 1), shift(before[mid:], "reader", -1)
        tokens = (own, after, far_low, far_high, before)

    width_here = key_proj.shape[1]
    ids_high = (passage_id // 256).astype(jnp.bfloat16)
    ids_low = (passage_id % 256).astype(jnp.bfloat16)
    gap = ((0, 0), (0, LANES // 2 - topk))
    coded = jnp.concatenate([query_feat, jnp.pad(ids_high, gap), jnp.pad(ids_low, gap)], axis=1)
    coded = jnp.pad(coded, ((0, 0), (0, width_here - coded.shape[1])))
    with jax.named_scope("gather_key_proj"):
        own = send_all(jnp.concatenate([key_proj, coded]), "zq")
        after, before = shift(own, Z, 1), shift(own, Z, -1)
        far = [shift(own[:2], Z, 2), shift(own[2:], Z, -2)]
        classes = (own, after, *far, before)
        own = jnp.concatenate([block[:, :-1] for block in classes])
        after, before = shift(own, "y", 1), shift(own, "y", -1)
        far = jnp.concatenate([shift(after[:8], "y", 1), shift(before[8:], "y", -1)])
        key_rows = [(block, shift(block, "core", 1)) for block in (own, after, far, before)]

    with jax.named_scope("gather_queries"):
        coded = jnp.concatenate([block[:, -1] for block in classes])
        coded = jnp.roll(coded.reshape(4, 4, width_here), zr, axis=0).reshape(nz, width_here)
        packed = send_all(coded[:, : width + LANES], NEAR)

    cols = width // nx
    six = width // n_index
    place = lax.broadcasted_iota(jnp.int32, (width, 1), 0)
    to_core, to_y = place // (ny * nz * six), place // (nz * six) % ny
    to_z, within = place // six % nz, place % six
    column = ((to_y * nz + to_z) * ncore + (to_core + core) % ncore) * six + within
    chosen = (lax.broadcasted_iota(jnp.int32, (1, width), 1) == column).astype(jnp.bfloat16)

    vmem = pl.BlockSpec(memory_space=pltpu.VMEM)
    with jax.named_scope("scores"):
        queries = n_index * nx
        operands = (packed, query_proj, index_emb, chosen)
        results = (
            jax.ShapeDtypeStruct((n_index, LANES), jnp.int32),
            jax.ShapeDtypeStruct((shard_rows, cols), jnp.float32),
            jax.ShapeDtypeStruct((queries, cols), jnp.float32),
            jax.ShapeDtypeStruct((n_index, LANES), jnp.float32),
            jax.ShapeDtypeStruct((width, queries), jnp.bfloat16),
        )
        anywhere = pl.BlockSpec(memory_space=pl.ANY)
        state, slots, my_rows, my_unit, query_scale, ordered = pl.pallas_call(
            scores_kernel,
            out_shape=(jax.ShapeDtypeStruct((n_index, LANES), jnp.float32), *results),
            in_specs=[pl.BlockSpec(memory_space=pltpu.SMEM)] + [anywhere] * 4,
            out_specs=(vmem,) + (anywhere,) * 5,
            scratch_shapes=[
                *like(*operands, *results),
                pltpu.VMEM((queries, width), jnp.float32),
                pltpu.VMEM((nx, n_index, LANES), jnp.int32),
                pltpu.SemaphoreType.DMA((5,)),
            ],
            compiler_params=pltpu.CompilerParams(vmem_limit_bytes=GRANT),
            cost_estimate=pl.CostEstimate(
                flops=64 << 30, bytes_accessed=8 << 20, transcendentals=0
            ),
            name="scores",
        )(jnp.stack([my_shard, r]).astype(jnp.int32), *operands)

    with jax.named_scope("reduce_scores"):
        states = lax.all_to_all(state, ("y", "core", *Z_BY_CLASS), 0, 0, tiled=True)

    with jax.named_scope("attention"):
        answer = dec_query.shape[1]
        heads_here = feats_here // DH
        decoded = dec_query.astype(jnp.float32).reshape(group, answer, heads_here, DH)
        dec_unit = (
            decoded * lax.rsqrt(jnp.mean(decoded * decoded, axis=3, keepdims=True) + EPSILON)
        ).astype(jnp.bfloat16)
        positions = lax.broadcasted_iota(jnp.int32, (group, topk, plen), 2)
        live = (positions < passage_len[:, :, None]).reshape(group, topk * plen)
        packet, own_scores = attention_packet(
            jnp.stack([y, zr, core, r]).astype(jnp.int32),
            tokens,
            key_rows,
            dec_unit.reshape(group, answer, feats_here),
            key_gain.astype(jnp.float32).reshape(1, feats_here),
            live.astype(jnp.float32),
            states,
        )

    with jax.named_scope("targets"):
        packets = lax.all_to_all(packet, NEAR, 0, 0, tiled=True).reshape(nx, n_pair, 2 * LANES)
        coef = pl.pallas_call(
            coef_kernel,
            out_shape=jax.ShapeDtypeStruct((nz, n_pair, LANES), jnp.float32),
            in_specs=[vmem],
            out_specs=vmem,
            name="coef",
        )(packets)
        coef = lax.all_to_all(coef, Z_BY_CLASS, 0, 0, tiled=True).reshape(n_index, LANES)

    with jax.named_scope("gradient"):
        part = jax.ShapeDtypeStruct((width // ncore, cols), jnp.float32)
        keep, send = pl.pallas_call(
            gradient_kernel,
            out_shape=(part, part),
            in_specs=[vmem] + [anywhere] * 5,
            out_specs=(vmem, vmem),
            scratch_shapes=[
                pltpu.VMEM((queries, shard_rows), jnp.float32),
                *like(slots, query_scale, my_rows, my_unit, ordered),
                pltpu.SemaphoreType.DMA((5,)),
            ],
            compiler_params=pltpu.CompilerParams(vmem_limit_bytes=GRANT),
            name="gradient",
        )(coef, slots, query_scale, my_rows, my_unit, ordered)

    with jax.named_scope("reduce_gradient"):
        term = (keep + shift(send, "core", 1)).reshape(ny, nz * six, cols)
        term = jnp.sum(lax.all_to_all(term, "y", 0, 0, tiled=True), axis=0)
        term = term.reshape(nz, six, cols)
        term = jnp.sum(lax.all_to_all(term, Z, 0, 0, tiled=True), axis=0)
        grad_proj = send_all(term, "reader")
        grad_proj = grad_proj.transpose(1, 0, 2).reshape(six, width)

    mass = jnp.sum(lax.dynamic_index_in_dim(packets, y * ncore + core, 1, False), axis=0)
    my_target = lax.dynamic_slice_in_dim(mass, r * SLOT, topk, 0)
    log_target = jnp.log(my_target)
    retr_loss = jnp.sum(my_target * (log_target - own_scores[0, :topk]))
    slab_best = own_scores[0, topk : topk + 1]
    return (grad_proj, slab_best, retr_loss[None], log_target[None])


def solution(mesh):
    split = Mesh(mesh.devices.reshape(4, 4, 4, 2, 4), INDEX + ("reader",))
    return jax.shard_map(
        body,
        mesh=split,
        in_specs=(
            P(INDEX, None),
            P(INDEX + ("reader",), None),
            P(),
            P(INDEX + ("reader",), None),
            P(INDEX, None),
            P(INDEX, None, None, "reader"),
            P(INDEX, "reader"),
            P("reader"),
            P(INDEX, None, "reader"),
        ),
        out_specs=(
            P(INDEX, None),
            P(INDEX + ("reader",)),
            P(INDEX + ("reader",)),
            P(INDEX + ("reader",), None),
        ),
        check_vma=False,
    )
```

```python
import functools
import math

import jax
import jax.numpy as jnp
from jax import lax
from jax.experimental import pallas as pl
from jax.experimental.pallas import tpu as pltpu
from jax.sharding import Mesh, PartitionSpec as P

HEADS = 64
DH = 64
ANS = 16
EPSILON = 1e-06
SOFTMAX_TEMPER = 0.05
EXACT = lax.Precision.HIGHEST
INDEX = ("y", "zq", "zr", "core")
Z = ("zq", "zr")
Z_BY_CLASS = ("zr", "zq")
NEAR = ("reader", "y", "core")
LANES = 128
SLOT = 32
TILE = 256
N_OWNERS = 128
GRANT = 48 << 20
EARLY = (0, 1, 3)
LATE = 2


def shift(x, axis, step):
    size = lax.axis_size(axis)
    return lax.ppermute(x, axis, [((i + step) % size, i) for i in range(size)])


def send_all(x, axis):
    size = lax.axis_size(axis)
    return lax.all_to_all(jnp.broadcast_to(x[None], (size, *x.shape)), axis, 0, 0, tiled=True)


def halves(x):
    high = x.astype(jnp.bfloat16)
    return high, (x - high.astype(jnp.float32)).astype(jnp.bfloat16)


def dot32(a, b):
    return jnp.dot(a, b, preferred_element_type=jnp.float32)


def load(far, near, sems):
    copies = [pltpu.make_async_copy(a, b, sems.at[i]) for i, (a, b) in enumerate(zip(far, near))]
    for copy in copies:
        copy.start()
    return copies


def like(*arrays):
    return [pltpu.VMEM(x.shape, x.dtype) for x in arrays]


def token_copies(r, chunk, tokens, target, sem):
    for j, block in enumerate(tokens):

        @pl.when((r + j) % 4 == chunk)
        def _():
            pltpu.make_async_copy(block, target, sem).start()

    return [pltpu.make_async_copy(target, target, sem)]


def row_copies(place, own, other, target, sem):
    zr, core = place[1], place[2]
    for residue in range(4):
        to = target.at[:, (zr + residue) % 4]
        four = pl.ds(4 * residue, 4)
        pltpu.make_async_copy(own.at[four], to.at[:, core], sem).start()
        pltpu.make_async_copy(other.at[four], to.at[:, 1 - core], sem).start()
    return [pltpu.make_async_copy(target, target, sem)]


def early_keys_kernel(place, *refs):
    tokens, rows, (keys_out, keys, token_v, weight_v, sems) = refs[:4], refs[4:10], refs[10:]
    y, r = place[0], place[3]
    copies = []
    for slot, ahead in enumerate(EARLY):
        own, other = rows[2 * slot], rows[2 * slot + 1]
        copies += row_copies(place, own, other, weight_v.at[slot], sems.at[0, slot])
        copies += token_copies(r, (y + ahead) % 4, tokens, token_v.at[slot], sems.at[1, slot])
    for copy in copies:
        copy.wait()
    tiles = keys.shape[0]

    def leave(t):
        cols = pl.ds(pl.multiple_of(t * TILE, TILE), TILE)
        return pltpu.make_async_copy(keys.at[t], keys_out.at[:, cols], sems.at[2, t])

    @pl.loop(0, tiles)
    def _(t):
        cols = pl.ds(pl.multiple_of(t * TILE, TILE), TILE)
        total = dot32(token_v[0], weight_v[0, :, :, :, :, cols].reshape(-1, TILE))
        for slot in range(1, len(EARLY)):
            total += dot32(token_v[slot], weight_v[slot, :, :, :, :, cols].reshape(-1, TILE))
        keys[t] = total
        leave(t).start()

    @pl.loop(0, tiles)
    def _(t):
        leave(t).wait()


def attend(keys, offset, dec, gain, live, column_v):
    group, n = dec.shape[0], live.shape[1]
    cols = pl.ds(pl.multiple_of(offset, TILE), TILE)
    same = (
        lax.broadcasted_iota(jnp.int32, (TILE, TILE), 0) // DH
        == lax.broadcasted_iota(jnp.int32, (TILE, TILE), 1) // DH
    ).astype(jnp.bfloat16)
    mine = (
        lax.broadcasted_iota(jnp.int32, (TILE // DH * ANS, TILE), 0) // ANS
        == lax.broadcasted_iota(jnp.int32, (TILE // DH * ANS, TILE), 1) // DH
    )
    high, low = halves(keys * keys)
    square = (dot32(high, same) + dot32(low, same)) / DH
    unit = (keys * lax.rsqrt(square + EPSILON) * gain[:, cols]).astype(jnp.bfloat16)
    for g in range(group):
        answer = dec[g, :, cols].astype(jnp.float32)
        answer = jnp.concatenate([answer] * (TILE // DH), axis=0)
        answer = jnp.where(mine, answer, 0.0).astype(jnp.bfloat16)
        similarity = lax.dot_general(
            answer,
            unit[g * n : (g + 1) * n],
            (((1,), (1,)), ((), ())),
            preferred_element_type=jnp.float32,
        ) / math.sqrt(DH)
        weight = jnp.where(live[g : g + 1, :] > 0, jnp.exp(similarity), 0.0)
        weight = weight / jnp.sum(weight, axis=1, keepdims=True)
        column_v[g : g + 1, :] += jnp.sum(weight, axis=0, keepdims=True)


def late_heads_kernel(place, *refs):
    tokens, (own, other), refs = refs[:4], refs[4:6], refs[6:]
    far, (out, own_scores), near, refs = refs[:5], refs[5:7], refs[7:12], refs[12:]
    token_v, weight_v, column_v, load_sems, sems = refs
    y, r = place[0], place[3]
    loads = load(far, near, load_sems)
    early, dec, gain, live, states = near
    copies = row_copies(place, own, other, weight_v, sems.at[0])
    copies += token_copies(r, (y + LATE) % 4, tokens, token_v, sems.at[1])
    column_v[...] = jnp.zeros_like(column_v)

    lane = lax.broadcasted_iota(jnp.int32, (1, LANES), 1)
    for copy in loads:
        copy.wait()
    found = states[...]
    fetched = jnp.where(lane < 20, jnp.sum(found, axis=0, keepdims=True), 0.0)
    expo = jnp.where(lane < 20, jnp.exp(fetched), 0.0)
    total = jnp.sum(expo, axis=1, keepdims=True)
    log_prob = fetched - jnp.log(total)
    best = jnp.max(found, axis=0, keepdims=True)
    own_scores[...] = jnp.broadcast_to(jnp.where(lane == 20, best, log_prob), own_scores.shape)
    scores = expo / total + pltpu.roll(fetched, LANES // 2, 1)
    out[:, LANES:] = jnp.broadcast_to(scores, (out.shape[0], LANES))

    for copy in copies:
        copy.wait()

    @pl.loop(0, early.shape[1] // TILE)
    def _(t):
        cols = pl.ds(pl.multiple_of(t * TILE, TILE), TILE)
        keys = early[:, cols] + dot32(token_v[...], weight_v[:, :, :, :, cols].reshape(-1, TILE))
        attend(keys, t * TILE, dec, gain, live, column_v)

    n = live.shape[1]
    mass = jnp.zeros((8, LANES), jnp.float32)
    for g in range(dec.shape[0]):
        column = jnp.broadcast_to(column_v[g : g + 1, :], (8, n))
        to = (
            lax.broadcasted_iota(jnp.int32, (n, LANES), 0) // 8 + g * SLOT
            == lax.broadcasted_iota(jnp.int32, (n, LANES), 1)
        ).astype(jnp.float32)
        mass += jnp.dot(column, to, precision=EXACT, preferred_element_type=jnp.float32)
    out[:, :LANES] = jnp.broadcast_to(mass[:1] / (HEADS * ANS), (out.shape[0], LANES))


def attention_packet(place, tokens, rows, dec, gain, live, states):
    vmem = pl.BlockSpec(memory_space=pltpu.VMEM)
    anywhere = pl.BlockSpec(memory_space=pl.ANY)
    smem = pl.BlockSpec(memory_space=pltpu.SMEM)
    token_rows, width = tokens[0].shape
    block = (4, 4, 2, *rows[0][0].shape[1:])

    def cost(count, size):
        return pl.CostEstimate(
            flops=2 * token_rows * count * width * width,
            bytes_accessed=size << 20,
            transcendentals=0,
        )

    early = pl.pallas_call(
        early_keys_kernel,
        out_shape=jax.ShapeDtypeStruct((token_rows, width), jnp.float32),
        in_specs=[smem] + [anywhere] * 10,
        out_specs=anywhere,
        scratch_shapes=[
            pltpu.VMEM((width // TILE, token_rows, TILE), jnp.float32),
            pltpu.VMEM((3, token_rows, width), jnp.bfloat16),
            pltpu.VMEM((3, *block), jnp.bfloat16),
            pltpu.SemaphoreType.DMA((3, 4)),
        ],
        compiler_params=pltpu.CompilerParams(vmem_limit_bytes=GRANT),
        cost_estimate=cost(12, 13),
        name="early_keys",
    )(place, *tokens, *[part for ahead in EARLY for part in rows[ahead]])
    return pl.pallas_call(
        late_heads_kernel,
        out_shape=(
            jax.ShapeDtypeStruct((32, 2 * LANES), jnp.float32),
            jax.ShapeDtypeStruct((8, LANES), jnp.float32),
        ),
        in_specs=[smem] + [anywhere] * 11,
        out_specs=(vmem, vmem),
        scratch_shapes=[
            *like(early, dec, gain, live, states),
            pltpu.VMEM((token_rows, width), jnp.bfloat16),
            pltpu.VMEM(block, jnp.bfloat16),
            pltpu.VMEM((8, live.shape[1]), jnp.float32),
            pltpu.SemaphoreType.DMA((5,)),
            pltpu.SemaphoreType.DMA((2,)),
        ],
        compiler_params=pltpu.CompilerParams(vmem_limit_bytes=GRANT),
        cost_estimate=cost(1, 6),
        name="late_heads",
    )(place, *tokens, *rows[LATE], early, dec, gain, live, states)


def scores_kernel(place, *refs):
    far, (state, *outs), near, refs = refs[:4], refs[4:10], refs[10:14], refs[14:]
    near_outs, (unit_v, ids_v, sems) = refs[:5], refs[5:]
    copies = load(far, near, sems)
    packed, proj, emb, chosen = near
    slots, rows, unit, scale, ordered = near_outs
    shard, r = place[0], place[1]
    n_rows, width = emb.shape
    per_x = state.shape[0]
    cols = rows.shape[1]
    for copy in copies:
        copy.wait()
    feats = packed[:, :, :width].reshape(4 * per_x, width)
    ordered[...] = lax.dot_general(
        chosen[...], feats, (((1,), (1,)), ((), ())), preferred_element_type=jnp.float32
    ).astype(jnp.bfloat16)

    lane = lax.broadcasted_iota(jnp.int32, (per_x, LANES), 1)
    spread = jnp.full((per_x, LANES), -1, jnp.int32)
    for x in range(4):
        coded = packed[8 * x : 8 * x + 8, :, width : width + LANES].reshape(per_x, LANES)
        coded = coded.astype(jnp.float32)
        ids = coded * 256 + pltpu.roll(coded, LANES // 2, 1)
        ids = ids.astype(jnp.int32) - shard * n_rows
        ids_v[x] = ids
        moved = ids if x == 0 else pltpu.roll(ids, SLOT * x, 1)
        spread = jnp.where((lane // SLOT == x) & (lane % SLOT < 20), moved, spread)
    slots[...] = spread

    vec = dot32(feats, proj[...])
    scale_all = lax.rsqrt(jnp.sum(vec * vec, axis=1, keepdims=True) + EPSILON)
    spread = jnp.zeros((per_x, LANES), jnp.float32)
    for x in range(4):
        spread = jnp.where(lane // SLOT == x, scale_all[x * per_x : (x + 1) * per_x], spread)
    scale[...] = spread
    unit_all = vec * scale_all
    unit_v[...] = unit_all
    emb_all = emb[...]
    row_unit = emb_all * lax.rsqrt(jnp.sum(emb_all * emb_all, axis=1, keepdims=True) + EPSILON)
    for x in range(4):

        @pl.when(r == x)
        def _():
            rows[...] = row_unit[:, x * cols : (x + 1) * cols]
            unit[...] = unit_all[:, x * cols : (x + 1) * cols]

    copies = load(near_outs, outs, sems)
    share = unit_v[pl.ds(pl.multiple_of(r * per_x, per_x), per_x), :]
    found = (
        lax.dot_general(
            share,
            row_unit,
            (((1,), (1,)), ((), ())),
            precision=EXACT,
            preferred_element_type=jnp.float32,
        )
        / SOFTMAX_TEMPER
    )
    places = ids_v[r]
    row = lax.broadcasted_iota(jnp.int32, (per_x, n_rows), 1)
    total = jnp.where(lane == 20, jnp.max(found, axis=1, keepdims=True), 0.0)
    for k in range(20):
        picked = jnp.where(places[:, k : k + 1] == row, found, 0.0)
        total = jnp.where(lane == k, jnp.sum(picked, axis=1, keepdims=True), total)
    state[...] = total
    for copy in copies:
        copy.wait()


def coef_kernel(packets, out):
    lane = lax.broadcasted_iota(jnp.int32, (8, LANES), 1)
    target = prob = fetched = jnp.zeros((8, LANES), jnp.float32)
    for x in range(4):
        target += packets[x, :, :LANES]
        scores = packets[x, :, LANES:]
        own = (lane // SLOT == x) & (lane % SLOT < 20)
        moved = scores if x == 0 else pltpu.roll(scores, SLOT * x, 1)
        prob += jnp.where(own, moved, 0.0)
        moved = pltpu.roll(scores, (SLOT * x + LANES // 2) % LANES, 1)
        fetched += jnp.where(own, moved, 0.0)
    gap = prob - target
    to = (
        lax.broadcasted_iota(jnp.int32, (LANES, LANES), 0) // SLOT * SLOT + 20
        == lax.broadcasted_iota(jnp.int32, (LANES, LANES), 1)
    ).astype(jnp.float32)
    along = jnp.dot(gap * fetched, to, precision=EXACT, preferred_element_type=jnp.float32)
    packed = gap / SOFTMAX_TEMPER + along / N_OWNERS
    out[...] = jnp.broadcast_to(packed[None], out.shape)


def gradient_kernel(coef, *refs):
    far, (keep, send, matrix_v), near, sems = refs[:5], refs[5:8], refs[8:13], refs[13]
    copies = load(far, near, sems)
    slot, scale, rows, unit, ordered = near
    copies[0].wait()
    copies[1].wait()
    n_rows = matrix_v.shape[1]
    blocks = coef.shape[0]

    @pl.loop(0, blocks // 8)
    def _(b):
        eight = pl.ds(pl.multiple_of(b * 8, 8), 8)
        row = lax.broadcasted_iota(jnp.int32, (8, n_rows), 1)
        values = coef[pl.ds(b // 2 + b % 2 * 64, 8, stride=8), :] * scale[eight, :]
        places = slot[eight, :]
        for x in range(4):
            total = jnp.zeros((8, n_rows), jnp.float32)
            for k in range(SLOT * x, SLOT * x + 20):
                total += jnp.where(places[:, k : k + 1] == row, values[:, k : k + 1], 0.0)
            matrix_v[pl.ds(pl.multiple_of(x * blocks + b * 8, 8), 8), :] = total

    for copy in copies[2:]:
        copy.wait()
    along_all = jnp.concatenate([coef[pl.ds(p, 16, stride=8), :] for p in range(8)], axis=0)
    along_all = along_all * scale[...]
    row_high, row_low = halves(rows[...])
    parts_high, parts_low = [], []
    for x in range(4):
        mine = slice(x * blocks, (x + 1) * blocks)
        high, low = halves(matrix_v[mine, :])
        part = dot32(high, row_high) + (dot32(high, row_low) + dot32(low, row_high))
        along = along_all[:, SLOT * x + 20 : SLOT * x + 21]
        part = part - unit[mine, :] * along
        high, low = halves(part)
        parts_high.append(high)
        parts_low.append(low)
    high, low = jnp.concatenate(parts_high, axis=0), jnp.concatenate(parts_low, axis=0)
    half = keep.shape[0]
    keep[...] = dot32(ordered[:half, :], high) + dot32(ordered[:half, :], low)
    send[...] = dot32(ordered[half:, :], high) + dot32(ordered[half:, :], low)


def body(
    index_emb,
    query_feat,
    query_proj,
    passage_id,
    passage_len,
    enc_out,
    key_proj,
    key_gain,
    dec_query,
):
    y, zq, zr, core, r = (lax.axis_index(a) for a in (*INDEX, "reader"))
    ny, nz, ncore, nx = 4, 16, 2, 4
    z = zq * 4 + zr
    n_index = ny * nz * ncore
    n_pair = ny * ncore
    my_shard = (y * nz + z) * ncore + core
    shard_rows, width = index_emb.shape
    topk = passage_id.shape[1]

    group, _, plen, feats_here = enc_out.shape
    token_rows = group * topk * plen
    with jax.named_scope("gather_enc_out"):
        token_own = enc_out.reshape(token_rows, feats_here)
        token_after, token_before = shift(token_own, "reader", 1), shift(token_own, "reader", -1)

    width_here = key_proj.shape[1]
    ids_high = (passage_id // 256).astype(jnp.bfloat16)
    ids_low = (passage_id % 256).astype(jnp.bfloat16)
    gap = ((0, 0), (0, LANES // 2 - topk))
    coded = jnp.concatenate([query_feat, jnp.pad(ids_high, gap), jnp.pad(ids_low, gap)], axis=1)
    coded = jnp.pad(coded, ((0, 0), (0, width_here - coded.shape[1])))
    with jax.named_scope("gather_key_proj"):
        own = send_all(jnp.concatenate([key_proj, coded]), "zq")
        after, before = shift(own, Z, 1), shift(own, Z, -1)
        classes = (own, after, shift(own, Z, 2), before)
        own = jnp.concatenate([block[:, :-1] for block in classes])
        own, token_after, token_before = lax.optimization_barrier((own, token_after, token_before))
        after, before = shift(own, "y", 1), shift(own, "y", -1)
    token_far = shift(token_after, "reader", 1)

    with jax.named_scope("gather_queries"):
        coded = jnp.concatenate([block[:, -1] for block in classes])
        coded = jnp.roll(coded.reshape(4, 4, width_here), zr, axis=0).reshape(nz, width_here)
        packed = send_all(coded[:, : width + LANES], NEAR)

    cols = width // nx
    six = width // n_index
    place = lax.broadcasted_iota(jnp.int32, (width, 1), 0)
    to_core, to_y = place // (ny * nz * six), place // (nz * six) % ny
    to_z, within = place // six % nz, place % six
    column = ((to_y * nz + to_z) * ncore + (to_core + core) % ncore) * six + within
    chosen = (lax.broadcasted_iota(jnp.int32, (1, width), 1) == column).astype(jnp.bfloat16)

    vmem = pl.BlockSpec(memory_space=pltpu.VMEM)
    with jax.named_scope("scores"):
        queries = n_index * nx
        operands = (packed, query_proj, index_emb, chosen)
        results = (
            jax.ShapeDtypeStruct((n_index, LANES), jnp.int32),
            jax.ShapeDtypeStruct((shard_rows, cols), jnp.float32),
            jax.ShapeDtypeStruct((queries, cols), jnp.float32),
            jax.ShapeDtypeStruct((n_index, LANES), jnp.float32),
            jax.ShapeDtypeStruct((width, queries), jnp.bfloat16),
        )
        anywhere = pl.BlockSpec(memory_space=pl.ANY)
        state, slots, my_rows, my_unit, query_scale, ordered = pl.pallas_call(
            scores_kernel,
            out_shape=(jax.ShapeDtypeStruct((n_index, LANES), jnp.float32), *results),
            in_specs=[pl.BlockSpec(memory_space=pltpu.SMEM)] + [anywhere] * 4,
            out_specs=(vmem,) + (anywhere,) * 5,
            scratch_shapes=[
                *like(*operands, *results),
                pltpu.VMEM((queries, width), jnp.float32),
                pltpu.VMEM((nx, n_index, LANES), jnp.int32),
                pltpu.SemaphoreType.DMA((5,)),
            ],
            compiler_params=pltpu.CompilerParams(vmem_limit_bytes=GRANT),
            cost_estimate=pl.CostEstimate(
                flops=64 << 30, bytes_accessed=8 << 20, transcendentals=0
            ),
            name="scores",
        )(jnp.stack([my_shard, r]).astype(jnp.int32), *operands)

    with jax.named_scope("gather_key_proj"):
        after, before, state, token_far = lax.optimization_barrier(
            (after, before, state, token_far)
        )
        far = jnp.concatenate([shift(after[:8], "y", 1), shift(before[8:], "y", -1)])
        key_rows = [(block, shift(block, "core", 1)) for block in (own, after, far, before)]
    tokens = (token_own, token_after, token_far, token_before)

    with jax.named_scope("reduce_scores"):
        states = lax.all_to_all(state, ("y", "core", *Z_BY_CLASS), 0, 0, tiled=True)

    with jax.named_scope("attention"):
        answer = dec_query.shape[1]
        heads_here = feats_here // DH
        decoded = dec_query.astype(jnp.float32).reshape(group, answer, heads_here, DH)
        dec_unit = (
            decoded * lax.rsqrt(jnp.mean(decoded * decoded, axis=3, keepdims=True) + EPSILON)
        ).astype(jnp.bfloat16)
        positions = lax.broadcasted_iota(jnp.int32, (group, topk, plen), 2)
        live = (positions < passage_len[:, :, None]).reshape(group, topk * plen)
        packet, own_scores = attention_packet(
            jnp.stack([y, zr, core, r]).astype(jnp.int32),
            tokens,
            key_rows,
            dec_unit.reshape(group, answer, feats_here),
            key_gain.astype(jnp.float32).reshape(1, feats_here),
            live.astype(jnp.float32),
            states,
        )

    with jax.named_scope("targets"):
        packets = lax.all_to_all(packet, NEAR, 0, 0, tiled=True).reshape(nx, n_pair, 2 * LANES)
        coef = pl.pallas_call(
            coef_kernel,
            out_shape=jax.ShapeDtypeStruct((nz, n_pair, LANES), jnp.float32),
            in_specs=[vmem],
            out_specs=vmem,
            name="coef",
        )(packets)
        coef = lax.all_to_all(coef, Z_BY_CLASS, 0, 0, tiled=True).reshape(n_index, LANES)

    with jax.named_scope("gradient"):
        part = jax.ShapeDtypeStruct((width // ncore, cols), jnp.float32)
        keep, send = pl.pallas_call(
            gradient_kernel,
            out_shape=(part, part),
            in_specs=[vmem] + [anywhere] * 5,
            out_specs=(vmem, vmem),
            scratch_shapes=[
                pltpu.VMEM((queries, shard_rows), jnp.float32),
                *like(slots, query_scale, my_rows, my_unit, ordered),
                pltpu.SemaphoreType.DMA((5,)),
            ],
            compiler_params=pltpu.CompilerParams(vmem_limit_bytes=40 << 20),
            name="gradient",
        )(coef, slots, query_scale, my_rows, my_unit, ordered)

    with jax.named_scope("reduce_gradient"):
        term = (keep + shift(send, "core", 1)).reshape(ny, nz * six, cols)
        term = jnp.sum(lax.all_to_all(term, "y", 0, 0, tiled=True), axis=0)
        term = term.reshape(nz, six, cols)
        term = jnp.sum(lax.all_to_all(term, Z, 0, 0, tiled=True), axis=0)
        grad_proj = send_all(term, "reader")
        grad_proj = grad_proj.transpose(1, 0, 2).reshape(six, width)

    mass = jnp.sum(lax.dynamic_index_in_dim(packets, y * ncore + core, 1, False), axis=0)
    my_target = lax.dynamic_slice_in_dim(mass, r * SLOT, topk, 0)
    log_target = jnp.log(my_target)
    retr_loss = jnp.sum(my_target * (log_target - own_scores[0, :topk]))
    slab_best = own_scores[0, topk : topk + 1]
    return (grad_proj, slab_best, retr_loss[None], log_target[None])


def solution(mesh):
    split = Mesh(mesh.devices.reshape(4, 4, 4, 2, 4), INDEX + ("reader",))
    return jax.shard_map(
        body,
        mesh=split,
        in_specs=(
            P(INDEX, None),
            P(INDEX + ("reader",), None),
            P(),
            P(INDEX + ("reader",), None),
            P(INDEX, None),
            P(INDEX, None, None, "reader"),
            P(INDEX, "reader"),
            P("reader"),
            P(INDEX, None, "reader"),
        ),
        out_specs=(
            P(INDEX, None),
            P(INDEX + ("reader",)),
            P(INDEX + ("reader",)),
            P(INDEX + ("reader",), None),
        ),
        check_vma=False,
    )
```

```python
import functools
import math

import jax
import jax.numpy as jnp
from jax import lax
from jax.experimental import pallas as pl
from jax.experimental.pallas import tpu as pltpu
from jax.sharding import Mesh, PartitionSpec as P

HEADS = 64
DH = 64
ANS = 16
EPSILON = 1e-06
SOFTMAX_TEMPER = 0.05
EXACT = lax.Precision.HIGHEST
INDEX = ("y", "zq", "zr", "core")
Z = ("zq", "zr")
Z_BY_CLASS = ("zr", "zq")
NEAR = ("reader", "y", "core")
LANES = 128
SLOT = 32
TILE = 256
N_OWNERS = 128
GRANT = 48 << 20
EARLY = (0, 1, 3)
LATE = 2


def shift(x, axis, step):
    size = lax.axis_size(axis)
    return lax.ppermute(x, axis, [((i + step) % size, i) for i in range(size)])


def send_all(x, axis):
    size = lax.axis_size(axis)
    return lax.all_to_all(jnp.broadcast_to(x[None], (size, *x.shape)), axis, 0, 0, tiled=True)


def halves(x):
    high = x.astype(jnp.bfloat16)
    return high, (x - high.astype(jnp.float32)).astype(jnp.bfloat16)


def dot32(a, b):
    return jnp.dot(a, b, preferred_element_type=jnp.float32)


def load(far, near, sems):
    copies = [pltpu.make_async_copy(a, b, sem) for a, b, sem in zip(far, near, sems)]
    for copy in copies:
        copy.start()
    return copies


def each(sems, arrays):
    return [sems.at[i] for i in range(len(arrays))]


def like(*arrays):
    return [pltpu.VMEM(x.shape, x.dtype) for x in arrays]


def row_copies(place, own, other, target, sem):
    zr, core = place[1], place[2]
    for residue in range(4):
        to = target.at[:, (zr + residue) % 4]
        four = pl.ds(4 * residue, 4)
        pltpu.make_async_copy(own.at[four], to.at[:, core], sem).start()
        pltpu.make_async_copy(other.at[four], to.at[:, 1 - core], sem).start()
    return [pltpu.make_async_copy(target, target, sem)]


def early_keys_kernel(place, *refs):
    tokens, rows, (keys_out, keys, token_v, weight_v, sems) = refs[0], refs[1:7], refs[7:]
    y = place[0]
    copies = []
    for slot, ahead in enumerate(EARLY):
        own, other = rows[2 * slot], rows[2 * slot + 1]
        copies += row_copies(place, own, other, weight_v.at[slot], sems.at[0, slot])
        copies += load([tokens.at[(y + ahead) % 4]], [token_v.at[slot]], [sems.at[1, slot]])
    for copy in copies:
        copy.wait()
    tiles = keys.shape[0]

    def leave(t):
        cols = pl.ds(pl.multiple_of(t * TILE, TILE), TILE)
        return pltpu.make_async_copy(keys.at[t], keys_out.at[:, cols], sems.at[2, t])

    @pl.loop(0, tiles)
    def _(t):
        cols = pl.ds(pl.multiple_of(t * TILE, TILE), TILE)
        total = dot32(token_v[0], weight_v[0, :, :, :, :, cols].reshape(-1, TILE))
        for slot in range(1, len(EARLY)):
            total += dot32(token_v[slot], weight_v[slot, :, :, :, :, cols].reshape(-1, TILE))
        keys[t] = total
        leave(t).start()

    @pl.loop(0, tiles)
    def _(t):
        leave(t).wait()


def attend(keys, offset, dec, gain, live, column_v):
    group, n = dec.shape[0], live.shape[1]
    cols = pl.ds(pl.multiple_of(offset, TILE), TILE)
    same = (
        lax.broadcasted_iota(jnp.int32, (TILE, TILE), 0) // DH
        == lax.broadcasted_iota(jnp.int32, (TILE, TILE), 1) // DH
    ).astype(jnp.bfloat16)
    mine = (
        lax.broadcasted_iota(jnp.int32, (TILE // DH * ANS, TILE), 0) // ANS
        == lax.broadcasted_iota(jnp.int32, (TILE // DH * ANS, TILE), 1) // DH
    )
    high, low = halves(keys * keys)
    square = (dot32(high, same) + dot32(low, same)) / DH
    unit = (keys * lax.rsqrt(square + EPSILON) * gain[:, cols]).astype(jnp.bfloat16)
    for g in range(group):
        answer = dec[g, :, cols].astype(jnp.float32)
        answer = jnp.concatenate([answer] * (TILE // DH), axis=0)
        answer = jnp.where(mine, answer, 0.0).astype(jnp.bfloat16)
        similarity = lax.dot_general(
            answer,
            unit[g * n : (g + 1) * n],
            (((1,), (1,)), ((), ())),
            preferred_element_type=jnp.float32,
        ) / math.sqrt(DH)
        weight = jnp.where(live[g : g + 1, :] > 0, jnp.exp(similarity), 0.0)
        weight = weight / jnp.sum(weight, axis=1, keepdims=True)
        column_v[g : g + 1, :] += jnp.sum(weight, axis=0, keepdims=True)


def late_heads_kernel(place, *refs):
    tokens, (own, other), refs = refs[0], refs[1:3], refs[3:]
    far, (out, own_scores), near, refs = refs[:5], refs[5:7], refs[7:12], refs[12:]
    token_v, weight_v, column_v, load_sems, sems = refs
    y = place[0]
    loads = load(far, near, each(load_sems, far))
    early, dec, gain, live, states = near
    copies = row_copies(place, own, other, weight_v, sems.at[0])
    copies += load([tokens.at[(y + LATE) % 4]], [token_v], [sems.at[1]])
    column_v[...] = jnp.zeros_like(column_v)

    lane = lax.broadcasted_iota(jnp.int32, (1, LANES), 1)
    for copy in loads:
        copy.wait()
    found = states[...]
    fetched = jnp.where(lane < 20, jnp.sum(found, axis=0, keepdims=True), 0.0)
    expo = jnp.where(lane < 20, jnp.exp(fetched), 0.0)
    total = jnp.sum(expo, axis=1, keepdims=True)
    log_prob = fetched - jnp.log(total)
    best = jnp.max(found, axis=0, keepdims=True)
    own_scores[...] = jnp.broadcast_to(jnp.where(lane == 20, best, log_prob), own_scores.shape)
    scores = expo / total + pltpu.roll(fetched, LANES // 2, 1)
    out[:, LANES:] = jnp.broadcast_to(scores, (out.shape[0], LANES))

    for copy in copies:
        copy.wait()

    @pl.loop(0, early.shape[1] // TILE)
    def _(t):
        cols = pl.ds(pl.multiple_of(t * TILE, TILE), TILE)
        keys = early[:, cols] + dot32(token_v[...], weight_v[:, :, :, :, cols].reshape(-1, TILE))
        attend(keys, t * TILE, dec, gain, live, column_v)

    n = live.shape[1]
    mass = jnp.zeros((8, LANES), jnp.float32)
    for g in range(dec.shape[0]):
        column = jnp.broadcast_to(column_v[g : g + 1, :], (8, n))
        to = (
            lax.broadcasted_iota(jnp.int32, (n, LANES), 0) // 8 + g * SLOT
            == lax.broadcasted_iota(jnp.int32, (n, LANES), 1)
        ).astype(jnp.float32)
        mass += jnp.dot(column, to, precision=EXACT, preferred_element_type=jnp.float32)
    out[:, :LANES] = jnp.broadcast_to(mass[:1] / (HEADS * ANS), (out.shape[0], LANES))


def attention_packet(place, tokens, rows, dec, gain, live, states):
    vmem = pl.BlockSpec(memory_space=pltpu.VMEM)
    anywhere = pl.BlockSpec(memory_space=pl.ANY)
    smem = pl.BlockSpec(memory_space=pltpu.SMEM)
    _, token_rows, width = tokens.shape
    block = (4, 4, 2, *rows[0][0].shape[1:])

    def cost(count, size):
        return pl.CostEstimate(
            flops=2 * token_rows * count * width * width,
            bytes_accessed=size << 20,
            transcendentals=0,
        )

    early = pl.pallas_call(
        early_keys_kernel,
        out_shape=jax.ShapeDtypeStruct((token_rows, width), jnp.float32),
        in_specs=[smem] + [anywhere] * 7,
        out_specs=anywhere,
        scratch_shapes=[
            pltpu.VMEM((width // TILE, token_rows, TILE), jnp.float32),
            pltpu.VMEM((3, token_rows, width), jnp.bfloat16),
            pltpu.VMEM((3, *block), jnp.bfloat16),
            pltpu.SemaphoreType.DMA((3, 4)),
        ],
        compiler_params=pltpu.CompilerParams(vmem_limit_bytes=GRANT),
        cost_estimate=cost(5, 13),
        name="early_keys",
    )(place, tokens, *[part for ahead in EARLY for part in rows[ahead]])
    return pl.pallas_call(
        late_heads_kernel,
        out_shape=(
            jax.ShapeDtypeStruct((32, 2 * LANES), jnp.float32),
            jax.ShapeDtypeStruct((8, LANES), jnp.float32),
        ),
        in_specs=[smem] + [anywhere] * 8,
        out_specs=(vmem, vmem),
        scratch_shapes=[
            *like(early, dec, gain, live, states),
            pltpu.VMEM((token_rows, width), jnp.bfloat16),
            pltpu.VMEM(block, jnp.bfloat16),
            pltpu.VMEM((8, live.shape[1]), jnp.float32),
            pltpu.SemaphoreType.DMA((5,)),
            pltpu.SemaphoreType.DMA((2,)),
        ],
        compiler_params=pltpu.CompilerParams(vmem_limit_bytes=GRANT),
        cost_estimate=cost(1, 6),
        name="late_heads",
    )(place, tokens, *rows[LATE], early, dec, gain, live, states)


def scores_kernel(place, *refs):
    far, (state, *outs), near, refs = refs[:4], refs[4:10], refs[10:14], refs[14:]
    near_outs, (unit_v, ids_v, sems) = refs[:5], refs[5:]
    copies = load(far, near, each(sems, far))
    packed, proj, emb, chosen = near
    slots, rows, unit, scale, ordered = near_outs
    shard, r = place[0], place[1]
    n_rows, width = emb.shape
    per_x = state.shape[0]
    cols = rows.shape[1]
    for copy in copies:
        copy.wait()
    feats = packed[:, :, :width].reshape(4 * per_x, width)
    ordered[...] = lax.dot_general(
        chosen[...], feats, (((1,), (1,)), ((), ())), preferred_element_type=jnp.float32
    ).astype(jnp.bfloat16)

    lane = lax.broadcasted_iota(jnp.int32, (per_x, LANES), 1)
    spread = jnp.full((per_x, LANES), -1, jnp.int32)
    for x in range(4):
        coded = packed[8 * x : 8 * x + 8, :, width : width + LANES].reshape(per_x, LANES)
        coded = coded.astype(jnp.float32)
        ids = coded * 256 + pltpu.roll(coded, LANES // 2, 1)
        ids = ids.astype(jnp.int32) - shard * n_rows
        ids_v[x] = ids
        moved = ids if x == 0 else pltpu.roll(ids, SLOT * x, 1)
        spread = jnp.where((lane // SLOT == x) & (lane % SLOT < 20), moved, spread)
    slots[...] = spread

    vec = dot32(feats, proj[...])
    scale_all = lax.rsqrt(jnp.sum(vec * vec, axis=1, keepdims=True) + EPSILON)
    spread = jnp.zeros((per_x, LANES), jnp.float32)
    for x in range(4):
        spread = jnp.where(lane // SLOT == x, scale_all[x * per_x : (x + 1) * per_x], spread)
    scale[...] = spread
    unit_all = vec * scale_all
    unit_v[...] = unit_all
    emb_all = emb[...]
    row_unit = emb_all * lax.rsqrt(jnp.sum(emb_all * emb_all, axis=1, keepdims=True) + EPSILON)
    for x in range(4):

        @pl.when(r == x)
        def _():
            rows[...] = row_unit[:, x * cols : (x + 1) * cols]
            unit[...] = unit_all[:, x * cols : (x + 1) * cols]

    copies = load(near_outs, outs, each(sems, outs))
    share = unit_v[pl.ds(pl.multiple_of(r * per_x, per_x), per_x), :]
    found = (
        lax.dot_general(
            share,
            row_unit,
            (((1,), (1,)), ((), ())),
            precision=EXACT,
            preferred_element_type=jnp.float32,
        )
        / SOFTMAX_TEMPER
    )
    places = ids_v[r]
    row = lax.broadcasted_iota(jnp.int32, (per_x, n_rows), 1)
    total = jnp.where(lane == 20, jnp.max(found, axis=1, keepdims=True), 0.0)
    for k in range(20):
        picked = jnp.where(places[:, k : k + 1] == row, found, 0.0)
        total = jnp.where(lane == k, jnp.sum(picked, axis=1, keepdims=True), total)
    state[...] = total
    for copy in copies:
        copy.wait()


def coef_kernel(packets, out):
    lane = lax.broadcasted_iota(jnp.int32, (8, LANES), 1)
    target = prob = fetched = jnp.zeros((8, LANES), jnp.float32)
    for x in range(4):
        target += packets[x, :, :LANES]
        scores = packets[x, :, LANES:]
        own = (lane // SLOT == x) & (lane % SLOT < 20)
        moved = scores if x == 0 else pltpu.roll(scores, SLOT * x, 1)
        prob += jnp.where(own, moved, 0.0)
        moved = pltpu.roll(scores, (SLOT * x + LANES // 2) % LANES, 1)
        fetched += jnp.where(own, moved, 0.0)
    gap = prob - target
    to = (
        lax.broadcasted_iota(jnp.int32, (LANES, LANES), 0) // SLOT * SLOT + 20
        == lax.broadcasted_iota(jnp.int32, (LANES, LANES), 1)
    ).astype(jnp.float32)
    along = jnp.dot(gap * fetched, to, precision=EXACT, preferred_element_type=jnp.float32)
    packed = gap / SOFTMAX_TEMPER + along / N_OWNERS
    out[...] = jnp.broadcast_to(packed[None], out.shape)


def gradient_kernel(coef, *refs):
    far, (keep, send, matrix_v), near, sems = refs[:5], refs[5:8], refs[8:13], refs[13]
    copies = load(far, near, each(sems, far))
    slot, scale, rows, unit, ordered = near
    copies[0].wait()
    copies[1].wait()
    n_rows = matrix_v.shape[1]
    blocks = coef.shape[0]

    @pl.loop(0, blocks // 8)
    def _(b):
        eight = pl.ds(pl.multiple_of(b * 8, 8), 8)
        row = lax.broadcasted_iota(jnp.int32, (8, n_rows), 1)
        values = coef[pl.ds(b // 2 + b % 2 * 64, 8, stride=8), :] * scale[eight, :]
        places = slot[eight, :]
        for x in range(4):
            total = jnp.zeros((8, n_rows), jnp.float32)
            for k in range(SLOT * x, SLOT * x + 20):
                total += jnp.where(places[:, k : k + 1] == row, values[:, k : k + 1], 0.0)
            matrix_v[pl.ds(pl.multiple_of(x * blocks + b * 8, 8), 8), :] = total

    for copy in copies[2:]:
        copy.wait()
    along_all = jnp.concatenate([coef[pl.ds(p, 16, stride=8), :] for p in range(8)], axis=0)
    along_all = along_all * scale[...]
    row_high, row_low = halves(rows[...])
    parts_high, parts_low = [], []
    for x in range(4):
        mine = slice(x * blocks, (x + 1) * blocks)
        high, low = halves(matrix_v[mine, :])
        part = dot32(high, row_high) + (dot32(high, row_low) + dot32(low, row_high))
        along = along_all[:, SLOT * x + 20 : SLOT * x + 21]
        part = part - unit[mine, :] * along
        high, low = halves(part)
        parts_high.append(high)
        parts_low.append(low)
    high, low = jnp.concatenate(parts_high, axis=0), jnp.concatenate(parts_low, axis=0)
    half = keep.shape[0]
    keep[...] = dot32(ordered[:half, :], high) + dot32(ordered[:half, :], low)
    send[...] = dot32(ordered[half:, :], high) + dot32(ordered[half:, :], low)


def body(
    index_emb,
    query_feat,
    query_proj,
    passage_id,
    passage_len,
    enc_out,
    key_proj,
    key_gain,
    dec_query,
):
    y, zq, zr, core, r = (lax.axis_index(a) for a in (*INDEX, "reader"))
    ny, nz, ncore, nx = 4, 16, 2, 4
    z = zq * 4 + zr
    n_index = ny * nz * ncore
    n_pair = ny * ncore
    my_shard = (y * nz + z) * ncore + core
    shard_rows, width = index_emb.shape
    topk = passage_id.shape[1]

    group, _, plen, feats_here = enc_out.shape
    token_rows = group * topk * plen
    with jax.named_scope("gather_enc_out"):
        tokens = lax.all_gather(enc_out.reshape(token_rows, feats_here), "reader")

    width_here = key_proj.shape[1]
    ids_high = (passage_id // 256).astype(jnp.bfloat16)
    ids_low = (passage_id % 256).astype(jnp.bfloat16)
    gap = ((0, 0), (0, LANES // 2 - topk))
    coded = jnp.concatenate([query_feat, jnp.pad(ids_high, gap), jnp.pad(ids_low, gap)], axis=1)
    coded = jnp.pad(coded, ((0, 0), (0, width_here - coded.shape[1])))
    with jax.named_scope("gather_key_proj"):
        own = send_all(jnp.concatenate([key_proj, coded]), "zq")
        after, before = shift(own, Z, 1), shift(own, Z, -1)
        classes = (own, after, shift(own, Z, 2), before)
        own = jnp.concatenate([block[:, :-1] for block in classes])
        after, before = shift(own, "y", 1), shift(own, "y", -1)

    with jax.named_scope("gather_queries"):
        coded = jnp.concatenate([block[:, -1] for block in classes])
        coded = jnp.roll(coded.reshape(4, 4, width_here), zr, axis=0).reshape(nz, width_here)
        packed = send_all(coded[:, : width + LANES], NEAR)

    cols = width // nx
    six = width // n_index
    place = lax.broadcasted_iota(jnp.int32, (width, 1), 0)
    to_core, to_y = place // (ny * nz * six), place // (nz * six) % ny
    to_z, within = place // six % nz, place % six
    column = ((to_y * nz + to_z) * ncore + (to_core + core) % ncore) * six + within
    chosen = (lax.broadcasted_iota(jnp.int32, (1, width), 1) == column).astype(jnp.bfloat16)

    vmem = pl.BlockSpec(memory_space=pltpu.VMEM)
    with jax.named_scope("scores"):
        queries = n_index * nx
        operands = (packed, query_proj, index_emb, chosen)
        results = (
            jax.ShapeDtypeStruct((n_index, LANES), jnp.int32),
            jax.ShapeDtypeStruct((shard_rows, cols), jnp.float32),
            jax.ShapeDtypeStruct((queries, cols), jnp.float32),
            jax.ShapeDtypeStruct((n_index, LANES), jnp.float32),
            jax.ShapeDtypeStruct((width, queries), jnp.bfloat16),
        )
        anywhere = pl.BlockSpec(memory_space=pl.ANY)
        state, slots, my_rows, my_unit, query_scale, ordered = pl.pallas_call(
            scores_kernel,
            out_shape=(jax.ShapeDtypeStruct((n_index, LANES), jnp.float32), *results),
            in_specs=[pl.BlockSpec(memory_space=pltpu.SMEM)] + [anywhere] * 4,
            out_specs=(vmem,) + (anywhere,) * 5,
            scratch_shapes=[
                *like(*operands, *results),
                pltpu.VMEM((queries, width), jnp.float32),
                pltpu.VMEM((nx, n_index, LANES), jnp.int32),
                pltpu.SemaphoreType.DMA((5,)),
            ],
            compiler_params=pltpu.CompilerParams(vmem_limit_bytes=GRANT),
            cost_estimate=pl.CostEstimate(
                flops=10 << 30, bytes_accessed=8 << 20, transcendentals=0
            ),
            name="scores",
        )(jnp.stack([my_shard, r]).astype(jnp.int32), *operands)

    with jax.named_scope("gather_key_proj"):
        after, before, state = lax.optimization_barrier((after, before, state))
        far = jnp.concatenate([shift(after[:8], "y", 1), shift(before[8:], "y", -1)])
        key_rows = [(block, shift(block, "core", 1)) for block in (own, after, far, before)]

    with jax.named_scope("reduce_scores"):
        states = lax.all_to_all(state, ("y", "core", *Z_BY_CLASS), 0, 0, tiled=True)
        key_rows[0], states = lax.optimization_barrier((key_rows[0], states))

    with jax.named_scope("attention"):
        answer = dec_query.shape[1]
        heads_here = feats_here // DH
        decoded = dec_query.astype(jnp.float32).reshape(group, answer, heads_here, DH)
        dec_unit = (
            decoded * lax.rsqrt(jnp.mean(decoded * decoded, axis=3, keepdims=True) + EPSILON)
        ).astype(jnp.bfloat16)
        positions = lax.broadcasted_iota(jnp.int32, (group, topk, plen), 2)
        live = (positions < passage_len[:, :, None]).reshape(group, topk * plen)
        packet, own_scores = attention_packet(
            jnp.stack([y, zr, core]).astype(jnp.int32),
            tokens,
            key_rows,
            dec_unit.reshape(group, answer, feats_here),
            key_gain.astype(jnp.float32).reshape(1, feats_here),
            live.astype(jnp.float32),
            states,
        )

    with jax.named_scope("targets"):
        packets = lax.all_to_all(packet, NEAR, 0, 0, tiled=True).reshape(nx, n_pair, 2 * LANES)
        coef = pl.pallas_call(
            coef_kernel,
            out_shape=jax.ShapeDtypeStruct((nz, n_pair, LANES), jnp.float32),
            in_specs=[vmem],
            out_specs=vmem,
            name="coef",
        )(packets)
        coef = lax.all_to_all(coef, Z_BY_CLASS, 0, 0, tiled=True).reshape(n_index, LANES)

    with jax.named_scope("gradient"):
        part = jax.ShapeDtypeStruct((width // ncore, cols), jnp.float32)
        keep, send = pl.pallas_call(
            gradient_kernel,
            out_shape=(part, part),
            in_specs=[vmem] + [anywhere] * 5,
            out_specs=(vmem, vmem),
            scratch_shapes=[
                pltpu.VMEM((queries, shard_rows), jnp.float32),
                *like(slots, query_scale, my_rows, my_unit, ordered),
                pltpu.SemaphoreType.DMA((5,)),
            ],
            compiler_params=pltpu.CompilerParams(vmem_limit_bytes=40 << 20),
            name="gradient",
        )(coef, slots, query_scale, my_rows, my_unit, ordered)

    with jax.named_scope("reduce_gradient"):
        term = (keep + shift(send, "core", 1)).reshape(ny, nz * six, cols)
        term = jnp.sum(lax.all_to_all(term, "y", 0, 0, tiled=True), axis=0)
        term = term.reshape(nz, six, cols)
        term = jnp.sum(lax.all_to_all(term, Z, 0, 0, tiled=True), axis=0)
        grad_proj = send_all(term, "reader")
        grad_proj = grad_proj.transpose(1, 0, 2).reshape(six, width)

    mass = jnp.sum(lax.dynamic_index_in_dim(packets, y * ncore + core, 1, False), axis=0)
    my_target = lax.dynamic_slice_in_dim(mass, r * SLOT, topk, 0)
    log_target = jnp.log(my_target)
    retr_loss = jnp.sum(my_target * (log_target - own_scores[0, :topk]))
    slab_best = own_scores[0, topk : topk + 1]
    return (grad_proj, slab_best, retr_loss[None], log_target[None])


def solution(mesh):
    split = Mesh(mesh.devices.reshape(4, 4, 4, 2, 4), INDEX + ("reader",))
    return jax.shard_map(
        body,
        mesh=split,
        in_specs=(
            P(INDEX, None),
            P(INDEX + ("reader",), None),
            P(),
            P(INDEX + ("reader",), None),
            P(INDEX, None),
            P(INDEX, None, None, "reader"),
            P(INDEX, "reader"),
            P("reader"),
            P(INDEX, None, "reader"),
        ),
        out_specs=(
            P(INDEX, None),
            P(INDEX + ("reader",)),
            P(INDEX + ("reader",)),
            P(INDEX + ("reader",), None),
        ),
        check_vma=False,
    )
```

```python
import functools
import math

import jax
import jax.numpy as jnp
from jax import lax
from jax.experimental import pallas as pl
from jax.experimental.pallas import tpu as pltpu
from jax.sharding import Mesh, PartitionSpec as P

HEADS = 64
DH = 64
ANS = 16
EPSILON = 1e-06
SOFTMAX_TEMPER = 0.05
EXACT = lax.Precision.HIGHEST
INDEX = ("y", "zq", "zr", "core")
Z = ("zq", "zr")
Z_BY_CLASS = ("zr", "zq")
NEAR = ("reader", "y", "core")
LANES = 128
SLOT = 32
TILE = 256
N_OWNERS = 128
GRANT = 48 << 20
EARLY = (0, 1, 3)
LATE = 2


def shift(x, axis, step):
    size = lax.axis_size(axis)
    return lax.ppermute(x, axis, [((i + step) % size, i) for i in range(size)])


def send_all(x, axis):
    size = lax.axis_size(axis)
    return lax.all_to_all(jnp.broadcast_to(x[None], (size, *x.shape)), axis, 0, 0, tiled=True)


def halves(x):
    high = x.astype(jnp.bfloat16)
    return high, (x - high.astype(jnp.float32)).astype(jnp.bfloat16)


def dot32(a, b):
    return jnp.dot(a, b, preferred_element_type=jnp.float32)


def load(far, near, sems):
    copies = [pltpu.make_async_copy(a, b, sem) for a, b, sem in zip(far, near, sems)]
    for copy in copies:
        copy.start()
    return copies


def each(sems, arrays):
    return [sems.at[i] for i in range(len(arrays))]


def like(*arrays):
    return [pltpu.VMEM(x.shape, x.dtype) for x in arrays]


def row_copies(place, own, other, target, sem):
    zr, core = place[1], place[2]
    for residue in range(4):
        to = target.at[:, (zr + residue) % 4]
        four = pl.ds(4 * residue, 4)
        pltpu.make_async_copy(own.at[four], to.at[:, core], sem).start()
        pltpu.make_async_copy(other.at[four], to.at[:, 1 - core], sem).start()
    return [pltpu.make_async_copy(target, target, sem)]


def early_keys_kernel(place, *refs):
    tokens, rows, (keys_out, keys, token_v, weight_v, sems) = refs[0], refs[1:7], refs[7:]
    y = place[0]
    copies = []
    for slot, ahead in enumerate(EARLY):
        own, other = rows[2 * slot], rows[2 * slot + 1]
        copies += row_copies(place, own, other, weight_v.at[slot], sems.at[0, slot])
        copies += load([tokens.at[(y + ahead) % 4]], [token_v.at[slot]], [sems.at[1, slot]])
    for copy in copies:
        copy.wait()
    tiles = keys.shape[0]

    def leave(t):
        cols = pl.ds(pl.multiple_of(t * TILE, TILE), TILE)
        return pltpu.make_async_copy(keys.at[t], keys_out.at[:, cols], sems.at[2, t])

    @pl.loop(0, tiles)
    def _(t):
        cols = pl.ds(pl.multiple_of(t * TILE, TILE), TILE)
        total = dot32(token_v[0], weight_v[0, :, :, :, :, cols].reshape(-1, TILE))
        for slot in range(1, len(EARLY)):
            total += dot32(token_v[slot], weight_v[slot, :, :, :, :, cols].reshape(-1, TILE))
        keys[t] = total
        leave(t).start()

    @pl.loop(0, tiles)
    def _(t):
        leave(t).wait()


def attend(keys, offset, dec, gain, live, column_v):
    group, n = dec.shape[0], live.shape[1]
    cols = pl.ds(pl.multiple_of(offset, TILE), TILE)
    same = (
        lax.broadcasted_iota(jnp.int32, (TILE, TILE), 0) // DH
        == lax.broadcasted_iota(jnp.int32, (TILE, TILE), 1) // DH
    ).astype(jnp.bfloat16)
    mine = (
        lax.broadcasted_iota(jnp.int32, (TILE // DH * ANS, TILE), 0) // ANS
        == lax.broadcasted_iota(jnp.int32, (TILE // DH * ANS, TILE), 1) // DH
    )
    high, low = halves(keys * keys)
    square = (dot32(high, same) + dot32(low, same)) / DH
    unit = (keys * lax.rsqrt(square + EPSILON) * gain[:, cols]).astype(jnp.bfloat16)
    for g in range(group):
        answer = dec[g, :, cols].astype(jnp.float32)
        answer = jnp.concatenate([answer] * (TILE // DH), axis=0)
        answer = jnp.where(mine, answer, 0.0).astype(jnp.bfloat16)
        similarity = lax.dot_general(
            answer,
            unit[g * n : (g + 1) * n],
            (((1,), (1,)), ((), ())),
            preferred_element_type=jnp.float32,
        ) / math.sqrt(DH)
        weight = jnp.where(live[g : g + 1, :] > 0, jnp.exp(similarity), 0.0)
        weight = weight / jnp.sum(weight, axis=1, keepdims=True)
        column_v[g : g + 1, :] += jnp.sum(weight, axis=0, keepdims=True)


def late_heads_kernel(place, *refs):
    tokens, (own, other), refs = refs[0], refs[1:3], refs[3:]
    far, (out, own_scores), near, refs = refs[:5], refs[5:7], refs[7:12], refs[12:]
    token_v, weight_v, column_v, load_sems, sems = refs
    y = place[0]
    loads = load(far, near, each(load_sems, far))
    early, dec, gain, live, states = near
    copies = row_copies(place, own, other, weight_v, sems.at[0])
    copies += load([tokens.at[(y + LATE) % 4]], [token_v], [sems.at[1]])
    column_v[...] = jnp.zeros_like(column_v)

    lane = lax.broadcasted_iota(jnp.int32, (1, LANES), 1)
    for copy in loads:
        copy.wait()
    found = states[...]
    fetched = jnp.where(lane < 20, jnp.sum(found, axis=0, keepdims=True), 0.0)
    expo = jnp.where(lane < 20, jnp.exp(fetched), 0.0)
    total = jnp.sum(expo, axis=1, keepdims=True)
    log_prob = fetched - jnp.log(total)
    best = jnp.max(found, axis=0, keepdims=True)
    own_scores[...] = jnp.broadcast_to(jnp.where(lane == 20, best, log_prob), own_scores.shape)
    scores = expo / total + pltpu.roll(fetched, LANES // 2, 1)
    out[:, LANES:] = jnp.broadcast_to(scores, (out.shape[0], LANES))

    for copy in copies:
        copy.wait()

    @pl.loop(0, early.shape[1] // TILE)
    def _(t):
        cols = pl.ds(pl.multiple_of(t * TILE, TILE), TILE)
        keys = early[:, cols] + dot32(token_v[...], weight_v[:, :, :, :, cols].reshape(-1, TILE))
        attend(keys, t * TILE, dec, gain, live, column_v)

    n = live.shape[1]
    mass = jnp.zeros((8, LANES), jnp.float32)
    for g in range(dec.shape[0]):
        column = jnp.broadcast_to(column_v[g : g + 1, :], (8, n))
        to = (
            lax.broadcasted_iota(jnp.int32, (n, LANES), 0) // 8 + g * SLOT
            == lax.broadcasted_iota(jnp.int32, (n, LANES), 1)
        ).astype(jnp.float32)
        mass += jnp.dot(column, to, precision=EXACT, preferred_element_type=jnp.float32)
    out[:, :LANES] = jnp.broadcast_to(mass[:1] / (HEADS * ANS), (out.shape[0], LANES))


def attention_packet(place, tokens, rows, dec, gain, live, states):
    vmem = pl.BlockSpec(memory_space=pltpu.VMEM)
    anywhere = pl.BlockSpec(memory_space=pl.ANY)
    smem = pl.BlockSpec(memory_space=pltpu.SMEM)
    _, token_rows, width = tokens.shape
    block = (4, 4, 2, *rows[0][0].shape[1:])

    def cost(count, size):
        return pl.CostEstimate(
            flops=2 * token_rows * count * width * width,
            bytes_accessed=size << 20,
            transcendentals=0,
        )

    early = pl.pallas_call(
        early_keys_kernel,
        out_shape=jax.ShapeDtypeStruct((token_rows, width), jnp.float32),
        in_specs=[smem] + [anywhere] * 7,
        out_specs=anywhere,
        scratch_shapes=[
            pltpu.VMEM((width // TILE, token_rows, TILE), jnp.float32),
            pltpu.VMEM((3, token_rows, width), jnp.bfloat16),
            pltpu.VMEM((3, *block), jnp.bfloat16),
            pltpu.SemaphoreType.DMA((3, 4)),
        ],
        compiler_params=pltpu.CompilerParams(vmem_limit_bytes=56 << 20),
        cost_estimate=cost(5, 13),
        name="early_keys",
    )(place, tokens, *[part for ahead in EARLY for part in rows[ahead]])
    return pl.pallas_call(
        late_heads_kernel,
        out_shape=(
            jax.ShapeDtypeStruct((32, 2 * LANES), jnp.float32),
            jax.ShapeDtypeStruct((8, LANES), jnp.float32),
        ),
        in_specs=[smem] + [anywhere] * 8,
        out_specs=(vmem, vmem),
        scratch_shapes=[
            *like(early, dec, gain, live, states),
            pltpu.VMEM((token_rows, width), jnp.bfloat16),
            pltpu.VMEM(block, jnp.bfloat16),
            pltpu.VMEM((8, live.shape[1]), jnp.float32),
            pltpu.SemaphoreType.DMA((5,)),
            pltpu.SemaphoreType.DMA((2,)),
        ],
        compiler_params=pltpu.CompilerParams(vmem_limit_bytes=GRANT),
        cost_estimate=cost(1, 6),
        name="late_heads",
    )(place, tokens, *rows[LATE], early, dec, gain, live, states)


def scores_kernel(place, *refs):
    far, (state, *outs), near, refs = refs[:4], refs[4:10], refs[10:14], refs[14:]
    near_outs, (unit_v, ids_v, sems) = refs[:5], refs[5:]
    copies = load(far, near, each(sems, far))
    packed, proj, emb, chosen = near
    slots, rows, unit, scale, ordered = near_outs
    shard, r = place[0], place[1]
    n_rows, width = emb.shape
    per_x = state.shape[0]
    cols = rows.shape[1]
    for copy in copies:
        copy.wait()
    feats = packed[:, :, :width].reshape(4 * per_x, width)
    ordered[...] = lax.dot_general(
        chosen[...], feats, (((1,), (1,)), ((), ())), preferred_element_type=jnp.float32
    ).astype(jnp.bfloat16)

    lane = lax.broadcasted_iota(jnp.int32, (per_x, LANES), 1)
    spread = jnp.full((per_x, LANES), -1, jnp.int32)
    for x in range(4):
        coded = packed[8 * x : 8 * x + 8, :, width : width + LANES].reshape(per_x, LANES)
        coded = coded.astype(jnp.float32)
        ids = coded * 256 + pltpu.roll(coded, LANES // 2, 1)
        ids = ids.astype(jnp.int32) - shard * n_rows
        ids_v[x] = ids
        moved = ids if x == 0 else pltpu.roll(ids, SLOT * x, 1)
        spread = jnp.where((lane // SLOT == x) & (lane % SLOT < 20), moved, spread)
    slots[...] = spread

    vec = dot32(feats, proj[...])
    scale_all = lax.rsqrt(jnp.sum(vec * vec, axis=1, keepdims=True) + EPSILON)
    spread = jnp.zeros((per_x, LANES), jnp.float32)
    for x in range(4):
        spread = jnp.where(lane // SLOT == x, scale_all[x * per_x : (x + 1) * per_x], spread)
    scale[...] = spread
    unit_all = vec * scale_all
    unit_v[...] = unit_all
    emb_all = emb[...]
    row_unit = emb_all * lax.rsqrt(jnp.sum(emb_all * emb_all, axis=1, keepdims=True) + EPSILON)
    for x in range(4):

        @pl.when(r == x)
        def _():
            rows[...] = row_unit[:, x * cols : (x + 1) * cols]
            unit[...] = unit_all[:, x * cols : (x + 1) * cols]

    copies = load(near_outs, outs, each(sems, outs))
    share = unit_v[pl.ds(pl.multiple_of(r * per_x, per_x), per_x), :]
    found = (
        lax.dot_general(
            share,
            row_unit,
            (((1,), (1,)), ((), ())),
            precision=EXACT,
            preferred_element_type=jnp.float32,
        )
        / SOFTMAX_TEMPER
    )
    places = ids_v[r]
    row = lax.broadcasted_iota(jnp.int32, (per_x, n_rows), 1)
    total = jnp.where(lane == 20, jnp.max(found, axis=1, keepdims=True), 0.0)
    for k in range(20):
        picked = jnp.where(places[:, k : k + 1] == row, found, 0.0)
        total = jnp.where(lane == k, jnp.sum(picked, axis=1, keepdims=True), total)
    state[...] = total
    for copy in copies:
        copy.wait()


def coef_kernel(packets, out):
    lane = lax.broadcasted_iota(jnp.int32, (8, LANES), 1)
    target = prob = fetched = jnp.zeros((8, LANES), jnp.float32)
    for x in range(4):
        target += packets[x, :, :LANES]
        scores = packets[x, :, LANES:]
        own = (lane // SLOT == x) & (lane % SLOT < 20)
        moved = scores if x == 0 else pltpu.roll(scores, SLOT * x, 1)
        prob += jnp.where(own, moved, 0.0)
        moved = pltpu.roll(scores, (SLOT * x + LANES // 2) % LANES, 1)
        fetched += jnp.where(own, moved, 0.0)
    gap = prob - target
    to = (
        lax.broadcasted_iota(jnp.int32, (LANES, LANES), 0) // SLOT * SLOT + 20
        == lax.broadcasted_iota(jnp.int32, (LANES, LANES), 1)
    ).astype(jnp.float32)
    along = jnp.dot(gap * fetched, to, precision=EXACT, preferred_element_type=jnp.float32)
    packed = gap / SOFTMAX_TEMPER + along / N_OWNERS
    out[...] = jnp.broadcast_to(packed[None], out.shape)


def gradient_kernel(coef, *refs):
    far, (keep, send, matrix_v), near, sems = refs[:5], refs[5:8], refs[8:13], refs[13]
    copies = load(far, near, each(sems, far))
    slot, scale, rows, unit, ordered = near
    copies[0].wait()
    copies[1].wait()
    n_rows = matrix_v.shape[1]
    blocks = coef.shape[0]

    @pl.loop(0, blocks // 8)
    def _(b):
        eight = pl.ds(pl.multiple_of(b * 8, 8), 8)
        row = lax.broadcasted_iota(jnp.int32, (8, n_rows), 1)
        values = coef[pl.ds(b // 2 + b % 2 * 64, 8, stride=8), :] * scale[eight, :]
        places = slot[eight, :]
        for x in range(4):
            total = jnp.zeros((8, n_rows), jnp.float32)
            for k in range(SLOT * x, SLOT * x + 20):
                total += jnp.where(places[:, k : k + 1] == row, values[:, k : k + 1], 0.0)
            matrix_v[pl.ds(pl.multiple_of(x * blocks + b * 8, 8), 8), :] = total

    for copy in copies[2:]:
        copy.wait()
    along_all = jnp.concatenate([coef[pl.ds(p, 16, stride=8), :] for p in range(8)], axis=0)
    along_all = along_all * scale[...]
    row_high, row_low = halves(rows[...])
    parts_high, parts_low = [], []
    for x in range(4):
        mine = slice(x * blocks, (x + 1) * blocks)
        high, low = halves(matrix_v[mine, :])
        part = dot32(high, row_high) + (dot32(high, row_low) + dot32(low, row_high))
        along = along_all[:, SLOT * x + 20 : SLOT * x + 21]
        part = part - unit[mine, :] * along
        high, low = halves(part)
        parts_high.append(high)
        parts_low.append(low)
    high, low = jnp.concatenate(parts_high, axis=0), jnp.concatenate(parts_low, axis=0)
    half = keep.shape[0]
    keep[...] = dot32(ordered[:half, :], high) + dot32(ordered[:half, :], low)
    send[...] = dot32(ordered[half:, :], high) + dot32(ordered[half:, :], low)


def body(
    index_emb,
    query_feat,
    query_proj,
    passage_id,
    passage_len,
    enc_out,
    key_proj,
    key_gain,
    dec_query,
):
    y, zq, zr, core, r = (lax.axis_index(a) for a in (*INDEX, "reader"))
    ny, nz, ncore, nx = 4, 16, 2, 4
    z = zq * 4 + zr
    n_index = ny * nz * ncore
    n_pair = ny * ncore
    my_shard = (y * nz + z) * ncore + core
    shard_rows, width = index_emb.shape
    topk = passage_id.shape[1]

    group, _, plen, feats_here = enc_out.shape
    token_rows = group * topk * plen
    with jax.named_scope("gather_enc_out"):
        tokens = lax.all_gather(enc_out.reshape(token_rows, feats_here), "reader")

    width_here = key_proj.shape[1]
    ids_high = (passage_id // 256).astype(jnp.bfloat16)
    ids_low = (passage_id % 256).astype(jnp.bfloat16)
    gap = ((0, 0), (0, LANES // 2 - topk))
    coded = jnp.concatenate([query_feat, jnp.pad(ids_high, gap), jnp.pad(ids_low, gap)], axis=1)
    coded = jnp.pad(coded, ((0, 0), (0, width_here - coded.shape[1])))
    with jax.named_scope("gather_key_proj"):
        own = send_all(jnp.concatenate([key_proj, coded]), "zq")
        after, before = shift(own, Z, 1), shift(own, Z, -1)
        classes = (own, after, shift(own, Z, 2), before)
        own = jnp.concatenate([block[:, :-1] for block in classes])
        after, before = shift(own, "y", 1), shift(own, "y", -1)

    with jax.named_scope("gather_queries"):
        coded = jnp.concatenate([block[:, -1] for block in classes])
        coded = jnp.roll(coded.reshape(4, 4, width_here), zr, axis=0).reshape(nz, width_here)
        packed = send_all(coded[:, : width + LANES], NEAR)

    cols = width // nx
    six = width // n_index
    place = lax.broadcasted_iota(jnp.int32, (width, 1), 0)
    to_core, to_y = place // (ny * nz * six), place // (nz * six) % ny
    to_z, within = place // six % nz, place % six
    column = ((to_y * nz + to_z) * ncore + (to_core + core) % ncore) * six + within
    chosen = (lax.broadcasted_iota(jnp.int32, (1, width), 1) == column).astype(jnp.bfloat16)

    vmem = pl.BlockSpec(memory_space=pltpu.VMEM)
    with jax.named_scope("scores"):
        queries = n_index * nx
        operands = (packed, query_proj, index_emb, chosen)
        results = (
            jax.ShapeDtypeStruct((n_index, LANES), jnp.int32),
            jax.ShapeDtypeStruct((shard_rows, cols), jnp.float32),
            jax.ShapeDtypeStruct((queries, cols), jnp.float32),
            jax.ShapeDtypeStruct((n_index, LANES), jnp.float32),
            jax.ShapeDtypeStruct((width, queries), jnp.bfloat16),
        )
        anywhere = pl.BlockSpec(memory_space=pl.ANY)
        state, slots, my_rows, my_unit, query_scale, ordered = pl.pallas_call(
            scores_kernel,
            out_shape=(jax.ShapeDtypeStruct((n_index, LANES), jnp.float32), *results),
            in_specs=[pl.BlockSpec(memory_space=pltpu.SMEM)] + [anywhere] * 4,
            out_specs=(vmem,) + (anywhere,) * 5,
            scratch_shapes=[
                *like(*operands, *results),
                pltpu.VMEM((queries, width), jnp.float32),
                pltpu.VMEM((nx, n_index, LANES), jnp.int32),
                pltpu.SemaphoreType.DMA((5,)),
            ],
            compiler_params=pltpu.CompilerParams(vmem_limit_bytes=56 << 20),
            cost_estimate=pl.CostEstimate(
                flops=1 << 30, bytes_accessed=4 << 20, transcendentals=0
            ),
            name="scores",
        )(jnp.stack([my_shard, r]).astype(jnp.int32), *operands)

    with jax.named_scope("gather_key_proj"):
        after, before, state = lax.optimization_barrier((after, before, state))
        far = jnp.concatenate([shift(after[:8], "y", 1), shift(before[8:], "y", -1)])
        key_rows = [(block, shift(block, "core", 1)) for block in (own, after, far, before)]

    with jax.named_scope("reduce_scores"):
        states = lax.all_to_all(state, ("y", "core", *Z_BY_CLASS), 0, 0, tiled=True)

    with jax.named_scope("attention"):
        answer = dec_query.shape[1]
        heads_here = feats_here // DH
        decoded = dec_query.astype(jnp.float32).reshape(group, answer, heads_here, DH)
        dec_unit = (
            decoded * lax.rsqrt(jnp.mean(decoded * decoded, axis=3, keepdims=True) + EPSILON)
        ).astype(jnp.bfloat16)
        positions = lax.broadcasted_iota(jnp.int32, (group, topk, plen), 2)
        live = (positions < passage_len[:, :, None]).reshape(group, topk * plen)
        packet, own_scores = attention_packet(
            jnp.stack([y, zr, core]).astype(jnp.int32),
            tokens,
            key_rows,
            dec_unit.reshape(group, answer, feats_here),
            key_gain.astype(jnp.float32).reshape(1, feats_here),
            live.astype(jnp.float32),
            states,
        )

    with jax.named_scope("targets"):
        packets = lax.all_to_all(packet, NEAR, 0, 0, tiled=True).reshape(nx, n_pair, 2 * LANES)
        coef = pl.pallas_call(
            coef_kernel,
            out_shape=jax.ShapeDtypeStruct((nz, n_pair, LANES), jnp.float32),
            in_specs=[vmem],
            out_specs=vmem,
            name="coef",
        )(packets)
        coef = lax.all_to_all(coef, Z_BY_CLASS, 0, 0, tiled=True).reshape(n_index, LANES)

    with jax.named_scope("gradient"):
        part = jax.ShapeDtypeStruct((width // ncore, cols), jnp.float32)
        keep, send = pl.pallas_call(
            gradient_kernel,
            out_shape=(part, part),
            in_specs=[vmem] + [anywhere] * 5,
            out_specs=(vmem, vmem),
            scratch_shapes=[
                pltpu.VMEM((queries, shard_rows), jnp.float32),
                *like(slots, query_scale, my_rows, my_unit, ordered),
                pltpu.SemaphoreType.DMA((5,)),
            ],
            compiler_params=pltpu.CompilerParams(vmem_limit_bytes=40 << 20),
            name="gradient",
        )(coef, slots, query_scale, my_rows, my_unit, ordered)

    with jax.named_scope("reduce_gradient"):
        term = (keep + shift(send, "core", 1)).reshape(ny, nz * six, cols)
        term = jnp.sum(lax.all_to_all(term, "y", 0, 0, tiled=True), axis=0)
        term = term.reshape(nz, six, cols)
        term = jnp.sum(lax.all_to_all(term, Z, 0, 0, tiled=True), axis=0)
        grad_proj = send_all(term, "reader")
        grad_proj = grad_proj.transpose(1, 0, 2).reshape(six, width)

    mass = jnp.sum(lax.dynamic_index_in_dim(packets, y * ncore + core, 1, False), axis=0)
    my_target = lax.dynamic_slice_in_dim(mass, r * SLOT, topk, 0)
    log_target = jnp.log(my_target)
    retr_loss = jnp.sum(my_target * (log_target - own_scores[0, :topk]))
    slab_best = own_scores[0, topk : topk + 1]
    return (grad_proj, slab_best, retr_loss[None], log_target[None])


def solution(mesh):
    split = Mesh(mesh.devices.reshape(4, 4, 4, 2, 4), INDEX + ("reader",))
    return jax.shard_map(
        body,
        mesh=split,
        in_specs=(
            P(INDEX, None),
            P(INDEX + ("reader",), None),
            P(),
            P(INDEX + ("reader",), None),
            P(INDEX, None),
            P(INDEX, None, None, "reader"),
            P(INDEX, "reader"),
            P("reader"),
            P(INDEX, None, "reader"),
        ),
        out_specs=(
            P(INDEX, None),
            P(INDEX + ("reader",)),
            P(INDEX + ("reader",)),
            P(INDEX + ("reader",), None),
        ),
        check_vma=False,
    )
```

```python
import functools
import math

import jax
import jax.numpy as jnp
from jax import lax
from jax.experimental import pallas as pl
from jax.experimental.pallas import tpu as pltpu
from jax.sharding import Mesh, PartitionSpec as P

HEADS = 64
DH = 64
ANS = 16
EPSILON = 1e-06
SOFTMAX_TEMPER = 0.05
EXACT = lax.Precision.HIGHEST
INDEX = ("y", "zq", "zr", "core")
Z = ("zq", "zr")
Z_BY_CLASS = ("zr", "zq")
NEAR = ("reader", "y", "core")
LANES = 128
SLOT = 32
TILE = 256
N_OWNERS = 128
GRANT = 48 << 20
EARLY = (0, 1, 3)
LATE = 2


def shift(x, axis, step):
    size = lax.axis_size(axis)
    return lax.ppermute(x, axis, [((i + step) % size, i) for i in range(size)])


def send_all(x, axis):
    size = lax.axis_size(axis)
    return lax.all_to_all(jnp.broadcast_to(x[None], (size, *x.shape)), axis, 0, 0, tiled=True)


def halves(x):
    high = x.astype(jnp.bfloat16)
    return high, (x - high.astype(jnp.float32)).astype(jnp.bfloat16)


def dot32(a, b):
    return jnp.dot(a, b, preferred_element_type=jnp.float32)


def load(far, near, sems):
    copies = [pltpu.make_async_copy(a, b, sems.at[i]) for i, (a, b) in enumerate(zip(far, near))]
    for copy in copies:
        copy.start()
    return copies


def like(*arrays):
    return [pltpu.VMEM(x.shape, x.dtype) for x in arrays]


def token_copies(r, chunk, tokens, target, sem):
    for j, block in enumerate(tokens):

        @pl.when((r + j) % 4 == chunk)
        def _():
            pltpu.make_async_copy(block, target, sem).start()

    return [pltpu.make_async_copy(target, target, sem)]


def row_copies(place, own, other, target, sem):
    zr, core = place[1], place[2]
    for residue in range(4):
        to = target.at[:, (zr + residue) % 4]
        four = pl.ds(4 * residue, 4)
        pltpu.make_async_copy(own.at[four], to.at[:, core], sem).start()
        pltpu.make_async_copy(other.at[four], to.at[:, 1 - core], sem).start()
    return [pltpu.make_async_copy(target, target, sem)]


def early_keys_kernel(place, *refs):
    tokens, rows, (keys_out, keys, token_v, weight_v, sems) = refs[:4], refs[4:10], refs[10:]
    y, r = place[0], place[3]
    copies = []
    for slot, ahead in enumerate(EARLY):
        own, other = rows[2 * slot], rows[2 * slot + 1]
        copies += row_copies(place, own, other, weight_v.at[slot], sems.at[0, slot])
        copies += token_copies(r, (y + ahead) % 4, tokens, token_v.at[slot], sems.at[1, slot])
    for copy in copies:
        copy.wait()
    tiles = keys.shape[0]

    def leave(t):
        cols = pl.ds(pl.multiple_of(t * TILE, TILE), TILE)
        return pltpu.make_async_copy(keys.at[t], keys_out.at[:, cols], sems.at[2, t])

    @pl.loop(0, tiles)
    def _(t):
        cols = pl.ds(pl.multiple_of(t * TILE, TILE), TILE)
        total = dot32(token_v[0], weight_v[0, :, :, :, :, cols].reshape(-1, TILE))
        for slot in range(1, len(EARLY)):
            total += dot32(token_v[slot], weight_v[slot, :, :, :, :, cols].reshape(-1, TILE))
        keys[t] = total
        leave(t).start()

    @pl.loop(0, tiles)
    def _(t):
        leave(t).wait()


def attend(keys, offset, dec, gain, live, column_v):
    group, n = dec.shape[0], live.shape[1]
    cols = pl.ds(pl.multiple_of(offset, TILE), TILE)
    same = (
        lax.broadcasted_iota(jnp.int32, (TILE, TILE), 0) // DH
        == lax.broadcasted_iota(jnp.int32, (TILE, TILE), 1) // DH
    ).astype(jnp.bfloat16)
    mine = (
        lax.broadcasted_iota(jnp.int32, (TILE // DH * ANS, TILE), 0) // ANS
        == lax.broadcasted_iota(jnp.int32, (TILE // DH * ANS, TILE), 1) // DH
    )
    high, low = halves(keys * keys)
    square = (dot32(high, same) + dot32(low, same)) / DH
    unit = (keys * lax.rsqrt(square + EPSILON) * gain[:, cols]).astype(jnp.bfloat16)
    for g in range(group):
        answer = dec[g, :, cols].astype(jnp.float32)
        answer = jnp.concatenate([answer] * (TILE // DH), axis=0)
        answer = jnp.where(mine, answer, 0.0).astype(jnp.bfloat16)
        similarity = lax.dot_general(
            answer,
            unit[g * n : (g + 1) * n],
            (((1,), (1,)), ((), ())),
            preferred_element_type=jnp.float32,
        ) / math.sqrt(DH)
        weight = jnp.where(live[g : g + 1, :] > 0, jnp.exp(similarity), 0.0)
        weight = weight / jnp.sum(weight, axis=1, keepdims=True)
        column_v[g : g + 1, :] += jnp.sum(weight, axis=0, keepdims=True)


def late_heads_kernel(place, *refs):
    tokens, (own, other), refs = refs[:4], refs[4:6], refs[6:]
    far, (out, own_scores), near, refs = refs[:5], refs[5:7], refs[7:12], refs[12:]
    token_v, weight_v, column_v, load_sems, sems = refs
    y, r = place[0], place[3]
    loads = load(far, near, load_sems)
    early, dec, gain, live, states = near
    copies = row_copies(place, own, other, weight_v, sems.at[0])
    copies += token_copies(r, (y + LATE) % 4, tokens, token_v, sems.at[1])
    column_v[...] = jnp.zeros_like(column_v)

    lane = lax.broadcasted_iota(jnp.int32, (1, LANES), 1)
    for copy in loads:
        copy.wait()
    found = states[...]
    fetched = jnp.where(lane < 20, jnp.sum(found, axis=0, keepdims=True), 0.0)
    expo = jnp.where(lane < 20, jnp.exp(fetched), 0.0)
    total = jnp.sum(expo, axis=1, keepdims=True)
    log_prob = fetched - jnp.log(total)
    best = jnp.max(found, axis=0, keepdims=True)
    own_scores[...] = jnp.broadcast_to(jnp.where(lane == 20, best, log_prob), own_scores.shape)
    scores = expo / total + pltpu.roll(fetched, LANES // 2, 1)
    out[:, LANES:] = jnp.broadcast_to(scores, (out.shape[0], LANES))

    for copy in copies:
        copy.wait()

    @pl.loop(0, early.shape[1] // TILE)
    def _(t):
        cols = pl.ds(pl.multiple_of(t * TILE, TILE), TILE)
        keys = early[:, cols] + dot32(token_v[...], weight_v[:, :, :, :, cols].reshape(-1, TILE))
        attend(keys, t * TILE, dec, gain, live, column_v)

    n = live.shape[1]
    mass = jnp.zeros((8, LANES), jnp.float32)
    for g in range(dec.shape[0]):
        column = jnp.broadcast_to(column_v[g : g + 1, :], (8, n))
        to = (
            lax.broadcasted_iota(jnp.int32, (n, LANES), 0) // 8 + g * SLOT
            == lax.broadcasted_iota(jnp.int32, (n, LANES), 1)
        ).astype(jnp.float32)
        mass += jnp.dot(column, to, precision=EXACT, preferred_element_type=jnp.float32)
    out[:, :LANES] = jnp.broadcast_to(mass[:1] / (HEADS * ANS), (out.shape[0], LANES))


def attention_packet(place, tokens, rows, dec, gain, live, states):
    vmem = pl.BlockSpec(memory_space=pltpu.VMEM)
    anywhere = pl.BlockSpec(memory_space=pl.ANY)
    smem = pl.BlockSpec(memory_space=pltpu.SMEM)
    token_rows, width = tokens[0].shape
    block = (4, 4, 2, *rows[0][0].shape[1:])

    def cost(count, size):
        return pl.CostEstimate(
            flops=2 * token_rows * count * width * width,
            bytes_accessed=size << 20,
            transcendentals=0,
        )

    early = pl.pallas_call(
        early_keys_kernel,
        out_shape=jax.ShapeDtypeStruct((token_rows, width), jnp.float32),
        in_specs=[smem] + [anywhere] * 10,
        out_specs=anywhere,
        scratch_shapes=[
            pltpu.VMEM((width // TILE, token_rows, TILE), jnp.float32),
            pltpu.VMEM((3, token_rows, width), jnp.bfloat16),
            pltpu.VMEM((3, *block), jnp.bfloat16),
            pltpu.SemaphoreType.DMA((3, 4)),
        ],
        compiler_params=pltpu.CompilerParams(vmem_limit_bytes=56 << 20),
        cost_estimate=cost(12, 13),
        name="early_keys",
    )(place, *tokens, *[part for ahead in EARLY for part in rows[ahead]])
    return pl.pallas_call(
        late_heads_kernel,
        out_shape=(
            jax.ShapeDtypeStruct((32, 2 * LANES), jnp.float32),
            jax.ShapeDtypeStruct((8, LANES), jnp.float32),
        ),
        in_specs=[smem] + [anywhere] * 11,
        out_specs=(vmem, vmem),
        scratch_shapes=[
            *like(early, dec, gain, live, states),
            pltpu.VMEM((token_rows, width), jnp.bfloat16),
            pltpu.VMEM(block, jnp.bfloat16),
            pltpu.VMEM((8, live.shape[1]), jnp.float32),
            pltpu.SemaphoreType.DMA((5,)),
            pltpu.SemaphoreType.DMA((2,)),
        ],
        compiler_params=pltpu.CompilerParams(vmem_limit_bytes=GRANT),
        cost_estimate=cost(1, 6),
        name="late_heads",
    )(place, *tokens, *rows[LATE], early, dec, gain, live, states)


def scores_kernel(place, *refs):
    far, (state, *outs), near, refs = refs[:4], refs[4:10], refs[10:14], refs[14:]
    near_outs, (unit_v, ids_v, sems) = refs[:5], refs[5:]
    copies = load(far, near, sems)
    packed, proj, emb, chosen = near
    slots, rows, unit, scale, ordered = near_outs
    shard, r = place[0], place[1]
    n_rows, width = emb.shape
    per_x = state.shape[0]
    cols = rows.shape[1]
    for copy in copies:
        copy.wait()
    feats = packed[:, :, :width].reshape(4 * per_x, width)
    ordered[...] = lax.dot_general(
        chosen[...], feats, (((1,), (1,)), ((), ())), preferred_element_type=jnp.float32
    ).astype(jnp.bfloat16)

    lane = lax.broadcasted_iota(jnp.int32, (per_x, LANES), 1)
    spread = jnp.full((per_x, LANES), -1, jnp.int32)
    for x in range(4):
        coded = packed[8 * x : 8 * x + 8, :, width : width + LANES].reshape(per_x, LANES)
        coded = coded.astype(jnp.float32)
        ids = coded * 256 + pltpu.roll(coded, LANES // 2, 1)
        ids = ids.astype(jnp.int32) - shard * n_rows
        ids_v[x] = ids
        moved = ids if x == 0 else pltpu.roll(ids, SLOT * x, 1)
        spread = jnp.where((lane // SLOT == x) & (lane % SLOT < 20), moved, spread)
    slots[...] = spread

    vec = dot32(feats, proj[...])
    scale_all = lax.rsqrt(jnp.sum(vec * vec, axis=1, keepdims=True) + EPSILON)
    spread = jnp.zeros((per_x, LANES), jnp.float32)
    for x in range(4):
        spread = jnp.where(lane // SLOT == x, scale_all[x * per_x : (x + 1) * per_x], spread)
    scale[...] = spread
    unit_all = vec * scale_all
    unit_v[...] = unit_all
    emb_all = emb[...]
    row_unit = emb_all * lax.rsqrt(jnp.sum(emb_all * emb_all, axis=1, keepdims=True) + EPSILON)
    for x in range(4):

        @pl.when(r == x)
        def _():
            rows[...] = row_unit[:, x * cols : (x + 1) * cols]
            unit[...] = unit_all[:, x * cols : (x + 1) * cols]

    copies = load(near_outs, outs, sems)
    share = unit_v[pl.ds(pl.multiple_of(r * per_x, per_x), per_x), :]
    found = (
        lax.dot_general(
            share,
            row_unit,
            (((1,), (1,)), ((), ())),
            precision=EXACT,
            preferred_element_type=jnp.float32,
        )
        / SOFTMAX_TEMPER
    )
    places = ids_v[r]
    row = lax.broadcasted_iota(jnp.int32, (per_x, n_rows), 1)
    total = jnp.where(lane == 20, jnp.max(found, axis=1, keepdims=True), 0.0)
    for k in range(20):
        picked = jnp.where(places[:, k : k + 1] == row, found, 0.0)
        total = jnp.where(lane == k, jnp.sum(picked, axis=1, keepdims=True), total)
    state[...] = total
    for copy in copies:
        copy.wait()


def coef_kernel(packets, out):
    lane = lax.broadcasted_iota(jnp.int32, (8, LANES), 1)
    target = prob = fetched = jnp.zeros((8, LANES), jnp.float32)
    for x in range(4):
        target += packets[x, :, :LANES]
        scores = packets[x, :, LANES:]
        own = (lane // SLOT == x) & (lane % SLOT < 20)
        moved = scores if x == 0 else pltpu.roll(scores, SLOT * x, 1)
        prob += jnp.where(own, moved, 0.0)
        moved = pltpu.roll(scores, (SLOT * x + LANES // 2) % LANES, 1)
        fetched += jnp.where(own, moved, 0.0)
    gap = prob - target
    to = (
        lax.broadcasted_iota(jnp.int32, (LANES, LANES), 0) // SLOT * SLOT + 20
        == lax.broadcasted_iota(jnp.int32, (LANES, LANES), 1)
    ).astype(jnp.float32)
    along = jnp.dot(gap * fetched, to, precision=EXACT, preferred_element_type=jnp.float32)
    packed = gap / SOFTMAX_TEMPER + along / N_OWNERS
    out[...] = jnp.broadcast_to(packed[None], out.shape)


def gradient_kernel(coef, *refs):
    far, (keep, send, matrix_v), near, sems = refs[:5], refs[5:8], refs[8:13], refs[13]
    copies = load(far, near, sems)
    slot, scale, rows, unit, ordered = near
    copies[0].wait()
    copies[1].wait()
    n_rows = matrix_v.shape[1]
    blocks = coef.shape[0]

    @pl.loop(0, blocks // 8)
    def _(b):
        eight = pl.ds(pl.multiple_of(b * 8, 8), 8)
        row = lax.broadcasted_iota(jnp.int32, (8, n_rows), 1)
        values = coef[pl.ds(b // 2 + b % 2 * 64, 8, stride=8), :] * scale[eight, :]
        places = slot[eight, :]
        for x in range(4):
            total = jnp.zeros((8, n_rows), jnp.float32)
            for k in range(SLOT * x, SLOT * x + 20):
                total += jnp.where(places[:, k : k + 1] == row, values[:, k : k + 1], 0.0)
            matrix_v[pl.ds(pl.multiple_of(x * blocks + b * 8, 8), 8), :] = total

    for copy in copies[2:]:
        copy.wait()
    along_all = jnp.concatenate([coef[pl.ds(p, 16, stride=8), :] for p in range(8)], axis=0)
    along_all = along_all * scale[...]
    row_high, row_low = halves(rows[...])
    parts_high, parts_low = [], []
    for x in range(4):
        mine = slice(x * blocks, (x + 1) * blocks)
        high, low = halves(matrix_v[mine, :])
        part = dot32(high, row_high) + (dot32(high, row_low) + dot32(low, row_high))
        along = along_all[:, SLOT * x + 20 : SLOT * x + 21]
        part = part - unit[mine, :] * along
        high, low = halves(part)
        parts_high.append(high)
        parts_low.append(low)
    high, low = jnp.concatenate(parts_high, axis=0), jnp.concatenate(parts_low, axis=0)
    half = keep.shape[0]
    keep[...] = dot32(ordered[:half, :], high) + dot32(ordered[:half, :], low)
    send[...] = dot32(ordered[half:, :], high) + dot32(ordered[half:, :], low)


def body(
    index_emb,
    query_feat,
    query_proj,
    passage_id,
    passage_len,
    enc_out,
    key_proj,
    key_gain,
    dec_query,
):
    y, zq, zr, core, r = (lax.axis_index(a) for a in (*INDEX, "reader"))
    ny, nz, ncore, nx = 4, 16, 2, 4
    z = zq * 4 + zr
    n_index = ny * nz * ncore
    n_pair = ny * ncore
    my_shard = (y * nz + z) * ncore + core
    shard_rows, width = index_emb.shape
    topk = passage_id.shape[1]

    group, _, plen, feats_here = enc_out.shape
    token_rows = group * topk * plen
    with jax.named_scope("gather_enc_out"):
        token_own = enc_out.reshape(token_rows, feats_here)
        token_after, token_before = shift(token_own, "reader", 1), shift(token_own, "reader", -1)

    width_here = key_proj.shape[1]
    ids_high = (passage_id // 256).astype(jnp.bfloat16)
    ids_low = (passage_id % 256).astype(jnp.bfloat16)
    gap = ((0, 0), (0, LANES // 2 - topk))
    coded = jnp.concatenate([query_feat, jnp.pad(ids_high, gap), jnp.pad(ids_low, gap)], axis=1)
    coded = jnp.pad(coded, ((0, 0), (0, width_here - coded.shape[1])))
    with jax.named_scope("gather_key_proj"):
        own = send_all(jnp.concatenate([key_proj, coded]), "zq")
        after, before = shift(own, Z, 1), shift(own, Z, -1)
        classes = (own, after, shift(own, Z, 2), before)
        own = jnp.concatenate([block[:, :-1] for block in classes])
        after, before = shift(own, "y", 1), shift(own, "y", -1)
        far = jnp.concatenate([shift(after[:8], "y", 1), shift(before[8:], "y", -1)])
        key_rows = [(block, shift(block, "core", 1)) for block in (own, after, far, before)]
    token_far = shift(token_after, "reader", 1)
    tokens = (token_own, token_after, token_far, token_before)

    with jax.named_scope("gather_queries"):
        coded = jnp.concatenate([block[:, -1] for block in classes])
        coded = jnp.roll(coded.reshape(4, 4, width_here), zr, axis=0).reshape(nz, width_here)
        packed = send_all(coded[:, : width + LANES], NEAR)

    cols = width // nx
    six = width // n_index
    place = lax.broadcasted_iota(jnp.int32, (width, 1), 0)
    to_core, to_y = place // (ny * nz * six), place // (nz * six) % ny
    to_z, within = place // six % nz, place % six
    column = ((to_y * nz + to_z) * ncore + (to_core + core) % ncore) * six + within
    chosen = (lax.broadcasted_iota(jnp.int32, (1, width), 1) == column).astype(jnp.bfloat16)

    vmem = pl.BlockSpec(memory_space=pltpu.VMEM)
    with jax.named_scope("scores"):
        queries = n_index * nx
        operands = (packed, query_proj, index_emb, chosen)
        results = (
            jax.ShapeDtypeStruct((n_index, LANES), jnp.int32),
            jax.ShapeDtypeStruct((shard_rows, cols), jnp.float32),
            jax.ShapeDtypeStruct((queries, cols), jnp.float32),
            jax.ShapeDtypeStruct((n_index, LANES), jnp.float32),
            jax.ShapeDtypeStruct((width, queries), jnp.bfloat16),
        )
        anywhere = pl.BlockSpec(memory_space=pl.ANY)
        state, slots, my_rows, my_unit, query_scale, ordered = pl.pallas_call(
            scores_kernel,
            out_shape=(jax.ShapeDtypeStruct((n_index, LANES), jnp.float32), *results),
            in_specs=[pl.BlockSpec(memory_space=pltpu.SMEM)] + [anywhere] * 4,
            out_specs=(vmem,) + (anywhere,) * 5,
            scratch_shapes=[
                *like(*operands, *results),
                pltpu.VMEM((queries, width), jnp.float32),
                pltpu.VMEM((nx, n_index, LANES), jnp.int32),
                pltpu.SemaphoreType.DMA((5,)),
            ],
            compiler_params=pltpu.CompilerParams(vmem_limit_bytes=56 << 20),
            cost_estimate=pl.CostEstimate(
                flops=64 << 30, bytes_accessed=8 << 20, transcendentals=0
            ),
            name="scores",
        )(jnp.stack([my_shard, r]).astype(jnp.int32), *operands)

    with jax.named_scope("reduce_scores"):
        states = lax.all_to_all(state, ("y", "core", *Z_BY_CLASS), 0, 0, tiled=True)

    with jax.named_scope("attention"):
        answer = dec_query.shape[1]
        heads_here = feats_here // DH
        decoded = dec_query.astype(jnp.float32).reshape(group, answer, heads_here, DH)
        dec_unit = (
            decoded * lax.rsqrt(jnp.mean(decoded * decoded, axis=3, keepdims=True) + EPSILON)
        ).astype(jnp.bfloat16)
        positions = lax.broadcasted_iota(jnp.int32, (group, topk, plen), 2)
        live = (positions < passage_len[:, :, None]).reshape(group, topk * plen)
        packet, own_scores = attention_packet(
            jnp.stack([y, zr, core, r]).astype(jnp.int32),
            tokens,
            key_rows,
            dec_unit.reshape(group, answer, feats_here),
            key_gain.astype(jnp.float32).reshape(1, feats_here),
            live.astype(jnp.float32),
            states,
        )

    with jax.named_scope("targets"):
        packets = lax.all_to_all(packet, NEAR, 0, 0, tiled=True).reshape(nx, n_pair, 2 * LANES)
        coef = pl.pallas_call(
            coef_kernel,
            out_shape=jax.ShapeDtypeStruct((nz, n_pair, LANES), jnp.float32),
            in_specs=[vmem],
            out_specs=vmem,
            name="coef",
        )(packets)
        coef = lax.all_to_all(coef, Z_BY_CLASS, 0, 0, tiled=True).reshape(n_index, LANES)

    with jax.named_scope("gradient"):
        part = jax.ShapeDtypeStruct((width // ncore, cols), jnp.float32)
        keep, send = pl.pallas_call(
            gradient_kernel,
            out_shape=(part, part),
            in_specs=[vmem] + [anywhere] * 5,
            out_specs=(vmem, vmem),
            scratch_shapes=[
                pltpu.VMEM((queries, shard_rows), jnp.float32),
                *like(slots, query_scale, my_rows, my_unit, ordered),
                pltpu.SemaphoreType.DMA((5,)),
            ],
            compiler_params=pltpu.CompilerParams(vmem_limit_bytes=40 << 20),
            name="gradient",
        )(coef, slots, query_scale, my_rows, my_unit, ordered)

    with jax.named_scope("reduce_gradient"):
        term = (keep + shift(send, "core", 1)).reshape(ny, nz * six, cols)
        term = jnp.sum(lax.all_to_all(term, "y", 0, 0, tiled=True), axis=0)
        term = term.reshape(nz, six, cols)
        term = jnp.sum(lax.all_to_all(term, Z, 0, 0, tiled=True), axis=0)
        grad_proj = send_all(term, "reader")
        grad_proj = grad_proj.transpose(1, 0, 2).reshape(six, width)

    mass = jnp.sum(lax.dynamic_index_in_dim(packets, y * ncore + core, 1, False), axis=0)
    my_target = lax.dynamic_slice_in_dim(mass, r * SLOT, topk, 0)
    log_target = jnp.log(my_target)
    retr_loss = jnp.sum(my_target * (log_target - own_scores[0, :topk]))
    slab_best = own_scores[0, topk : topk + 1]
    return (grad_proj, slab_best, retr_loss[None], log_target[None])


def solution(mesh):
    split = Mesh(mesh.devices.reshape(4, 4, 4, 2, 4), INDEX + ("reader",))
    return jax.shard_map(
        body,
        mesh=split,
        in_specs=(
            P(INDEX, None),
            P(INDEX + ("reader",), None),
            P(),
            P(INDEX + ("reader",), None),
            P(INDEX, None),
            P(INDEX, None, None, "reader"),
            P(INDEX, "reader"),
            P("reader"),
            P(INDEX, None, "reader"),
        ),
        out_specs=(
            P(INDEX, None),
            P(INDEX + ("reader",)),
            P(INDEX + ("reader",)),
            P(INDEX + ("reader",), None),
        ),
        check_vma=False,
    )
```

```python
import functools
import math

import jax
import jax.numpy as jnp
from jax import lax
from jax.experimental import pallas as pl
from jax.experimental.pallas import tpu as pltpu
from jax.sharding import Mesh, PartitionSpec as P

HEADS = 64
DH = 64
ANS = 16
EPSILON = 1e-06
SOFTMAX_TEMPER = 0.05
EXACT = lax.Precision.HIGHEST
INDEX = ("y", "zq", "zr", "core")
Z = ("zq", "zr")
Z_BY_CLASS = ("zr", "zq")
NEAR = ("reader", "y", "core")
LANES = 128
SLOT = 32
TILE = 256
N_OWNERS = 128
GRANT = 48 << 20
EARLY = (0, 1, 3)
LATE = 2


def shift(x, axis, step):
    size = lax.axis_size(axis)
    return lax.ppermute(x, axis, [((i + step) % size, i) for i in range(size)])


def send_all(x, axis):
    size = lax.axis_size(axis)
    return lax.all_to_all(jnp.broadcast_to(x[None], (size, *x.shape)), axis, 0, 0, tiled=True)


def halves(x):
    high = x.astype(jnp.bfloat16)
    return high, (x - high.astype(jnp.float32)).astype(jnp.bfloat16)


def dot32(a, b):
    return jnp.dot(a, b, preferred_element_type=jnp.float32)


def load(far, near, sems):
    copies = [pltpu.make_async_copy(a, b, sems.at[i]) for i, (a, b) in enumerate(zip(far, near))]
    for copy in copies:
        copy.start()
    return copies


def like(*arrays):
    return [pltpu.VMEM(x.shape, x.dtype) for x in arrays]


def token_copies(r, chunk, tokens, target, sem):
    for j, block in enumerate(tokens):

        @pl.when((r + j) % 4 == chunk)
        def _():
            pltpu.make_async_copy(block, target, sem).start()

    return [pltpu.make_async_copy(target, target, sem)]


def row_copies(place, own, other, target, sem):
    zr, core = place[1], place[2]
    for residue in range(4):
        to = target.at[:, (zr + residue) % 4]
        four = pl.ds(4 * residue, 4)
        pltpu.make_async_copy(own.at[four], to.at[:, core], sem).start()
        pltpu.make_async_copy(other.at[four], to.at[:, 1 - core], sem).start()
    return [pltpu.make_async_copy(target, target, sem)]


def early_keys_kernel(place, *refs):
    tokens, rows, (keys_out, keys, token_v, weight_v, sems) = refs[:4], refs[4:10], refs[10:]
    y, r = place[0], place[3]
    copies = []
    for slot, ahead in enumerate(EARLY):
        own, other = rows[2 * slot], rows[2 * slot + 1]
        copies += row_copies(place, own, other, weight_v.at[slot], sems.at[0, slot])
        copies += token_copies(r, (y + ahead) % 4, tokens, token_v.at[slot], sems.at[1, slot])
    for copy in copies:
        copy.wait()
    keys[...] = dot32(token_v[0], weight_v[0].reshape(-1, keys.shape[1]))
    for slot in range(1, len(EARLY)):
        keys[...] += dot32(token_v[slot], weight_v[slot].reshape(-1, keys.shape[1]))
    copy = pltpu.make_async_copy(keys, keys_out, sems.at[2, 0])
    copy.start()
    copy.wait()


def attend(keys, offset, dec, gain, live, column_v):
    group, n = dec.shape[0], live.shape[1]
    cols = pl.ds(pl.multiple_of(offset, TILE), TILE)
    same = (
        lax.broadcasted_iota(jnp.int32, (TILE, TILE), 0) // DH
        == lax.broadcasted_iota(jnp.int32, (TILE, TILE), 1) // DH
    ).astype(jnp.bfloat16)
    mine = (
        lax.broadcasted_iota(jnp.int32, (TILE // DH * ANS, TILE), 0) // ANS
        == lax.broadcasted_iota(jnp.int32, (TILE // DH * ANS, TILE), 1) // DH
    )
    high, low = halves(keys * keys)
    square = (dot32(high, same) + dot32(low, same)) / DH
    unit = (keys * lax.rsqrt(square + EPSILON) * gain[:, cols]).astype(jnp.bfloat16)
    for g in range(group):
        answer = dec[g, :, cols].astype(jnp.float32)
        answer = jnp.concatenate([answer] * (TILE // DH), axis=0)
        answer = jnp.where(mine, answer, 0.0).astype(jnp.bfloat16)
        similarity = lax.dot_general(
            answer,
            unit[g * n : (g + 1) * n],
            (((1,), (1,)), ((), ())),
            preferred_element_type=jnp.float32,
        ) / math.sqrt(DH)
        weight = jnp.where(live[g : g + 1, :] > 0, jnp.exp(similarity), 0.0)
        weight = weight / jnp.sum(weight, axis=1, keepdims=True)
        column_v[g : g + 1, :] += jnp.sum(weight, axis=0, keepdims=True)


def late_heads_kernel(place, *refs):
    tokens, (own, other), refs = refs[:4], refs[4:6], refs[6:]
    far, (out, own_scores), near, refs = refs[:5], refs[5:7], refs[7:12], refs[12:]
    token_v, weight_v, column_v, load_sems, sems = refs
    y, r = place[0], place[3]
    loads = load(far, near, load_sems)
    early, dec, gain, live, states = near
    copies = row_copies(place, own, other, weight_v, sems.at[0])
    copies += token_copies(r, (y + LATE) % 4, tokens, token_v, sems.at[1])
    column_v[...] = jnp.zeros_like(column_v)

    lane = lax.broadcasted_iota(jnp.int32, (1, LANES), 1)
    for copy in loads:
        copy.wait()
    found = states[...]
    fetched = jnp.where(lane < 20, jnp.sum(found, axis=0, keepdims=True), 0.0)
    expo = jnp.where(lane < 20, jnp.exp(fetched), 0.0)
    total = jnp.sum(expo, axis=1, keepdims=True)
    log_prob = fetched - jnp.log(total)
    best = jnp.max(found, axis=0, keepdims=True)
    own_scores[...] = jnp.broadcast_to(jnp.where(lane == 20, best, log_prob), own_scores.shape)
    scores = expo / total + pltpu.roll(fetched, LANES // 2, 1)
    out[:, LANES:] = jnp.broadcast_to(scores, (out.shape[0], LANES))

    for copy in copies:
        copy.wait()

    early[...] += dot32(token_v[...], weight_v[...].reshape(-1, early.shape[1]))

    @pl.loop(0, early.shape[1] // TILE)
    def _(t):
        cols = pl.ds(pl.multiple_of(t * TILE, TILE), TILE)
        attend(early[:, cols], t * TILE, dec, gain, live, column_v)

    n = live.shape[1]
    mass = jnp.zeros((8, LANES), jnp.float32)
    for g in range(dec.shape[0]):
        column = jnp.broadcast_to(column_v[g : g + 1, :], (8, n))
        to = (
            lax.broadcasted_iota(jnp.int32, (n, LANES), 0) // 8 + g * SLOT
            == lax.broadcasted_iota(jnp.int32, (n, LANES), 1)
        ).astype(jnp.float32)
        mass += jnp.dot(column, to, precision=EXACT, preferred_element_type=jnp.float32)
    out[:, :LANES] = jnp.broadcast_to(mass[:1] / (HEADS * ANS), (out.shape[0], LANES))


def attention_packet(place, tokens, rows, dec, gain, live, states):
    vmem = pl.BlockSpec(memory_space=pltpu.VMEM)
    anywhere = pl.BlockSpec(memory_space=pl.ANY)
    smem = pl.BlockSpec(memory_space=pltpu.SMEM)
    token_rows, width = tokens[0].shape
    block = (4, 4, 2, *rows[0][0].shape[1:])

    def cost(count, size):
        return pl.CostEstimate(
            flops=2 * token_rows * count * width * width,
            bytes_accessed=size << 20,
            transcendentals=0,
        )

    early = pl.pallas_call(
        early_keys_kernel,
        out_shape=jax.ShapeDtypeStruct((token_rows, width), jnp.float32),
        in_specs=[smem] + [anywhere] * 10,
        out_specs=anywhere,
        scratch_shapes=[
            pltpu.VMEM((token_rows, width), jnp.float32),
            pltpu.VMEM((3, token_rows, width), jnp.bfloat16),
            pltpu.VMEM((3, *block), jnp.bfloat16),
            pltpu.SemaphoreType.DMA((3, 4)),
        ],
        compiler_params=pltpu.CompilerParams(vmem_limit_bytes=56 << 20),
        cost_estimate=cost(12, 13),
        name="early_keys",
    )(place, *tokens, *[part for ahead in EARLY for part in rows[ahead]])
    return pl.pallas_call(
        late_heads_kernel,
        out_shape=(
            jax.ShapeDtypeStruct((32, 2 * LANES), jnp.float32),
            jax.ShapeDtypeStruct((8, LANES), jnp.float32),
        ),
        in_specs=[smem] + [anywhere] * 11,
        out_specs=(vmem, vmem),
        scratch_shapes=[
            *like(early, dec, gain, live, states),
            pltpu.VMEM((token_rows, width), jnp.bfloat16),
            pltpu.VMEM(block, jnp.bfloat16),
            pltpu.VMEM((8, live.shape[1]), jnp.float32),
            pltpu.SemaphoreType.DMA((5,)),
            pltpu.SemaphoreType.DMA((2,)),
        ],
        compiler_params=pltpu.CompilerParams(vmem_limit_bytes=GRANT),
        cost_estimate=cost(1, 6),
        name="late_heads",
    )(place, *tokens, *rows[LATE], early, dec, gain, live, states)


def scores_kernel(place, *refs):
    far, (state, *outs), near, refs = refs[:4], refs[4:10], refs[10:14], refs[14:]
    near_outs, (unit_v, ids_v, sems) = refs[:5], refs[5:]
    copies = load(far, near, sems)
    packed, proj, emb, chosen = near
    slots, rows, unit, scale, ordered = near_outs
    shard, r = place[0], place[1]
    n_rows, width = emb.shape
    per_x = state.shape[0]
    cols = rows.shape[1]
    for copy in copies:
        copy.wait()
    feats = packed[:, :, :width].reshape(4 * per_x, width)
    ordered[...] = lax.dot_general(
        chosen[...], feats, (((1,), (1,)), ((), ())), preferred_element_type=jnp.float32
    ).astype(jnp.bfloat16)

    lane = lax.broadcasted_iota(jnp.int32, (per_x, LANES), 1)
    spread = jnp.full((per_x, LANES), -1, jnp.int32)
    for x in range(4):
        coded = packed[8 * x : 8 * x + 8, :, width : width + LANES].reshape(per_x, LANES)
        coded = coded.astype(jnp.float32)
        ids = coded * 256 + pltpu.roll(coded, LANES // 2, 1)
        ids = ids.astype(jnp.int32) - shard * n_rows
        ids_v[x] = ids
        moved = ids if x == 0 else pltpu.roll(ids, SLOT * x, 1)
        spread = jnp.where((lane // SLOT == x) & (lane % SLOT < 20), moved, spread)
    slots[...] = spread

    vec = dot32(feats, proj[...])
    scale_all = lax.rsqrt(jnp.sum(vec * vec, axis=1, keepdims=True) + EPSILON)
    spread = jnp.zeros((per_x, LANES), jnp.float32)
    for x in range(4):
        spread = jnp.where(lane // SLOT == x, scale_all[x * per_x : (x + 1) * per_x], spread)
    scale[...] = spread
    unit_all = vec * scale_all
    unit_v[...] = unit_all
    emb_all = emb[...]
    row_unit = emb_all * lax.rsqrt(jnp.sum(emb_all * emb_all, axis=1, keepdims=True) + EPSILON)
    for x in range(4):

        @pl.when(r == x)
        def _():
            rows[...] = row_unit[:, x * cols : (x + 1) * cols]
            unit[...] = unit_all[:, x * cols : (x + 1) * cols]

    copies = load(near_outs, outs, sems)
    share = unit_v[pl.ds(pl.multiple_of(r * per_x, per_x), per_x), :]
    found = (
        lax.dot_general(
            share,
            row_unit,
            (((1,), (1,)), ((), ())),
            precision=EXACT,
            preferred_element_type=jnp.float32,
        )
        / SOFTMAX_TEMPER
    )
    places = ids_v[r]
    row = lax.broadcasted_iota(jnp.int32, (per_x, n_rows), 1)
    total = jnp.where(lane == 20, jnp.max(found, axis=1, keepdims=True), 0.0)
    for k in range(20):
        picked = jnp.where(places[:, k : k + 1] == row, found, 0.0)
        total = jnp.where(lane == k, jnp.sum(picked, axis=1, keepdims=True), total)
    state[...] = total
    for copy in copies:
        copy.wait()


def coef_kernel(packets, out):
    lane = lax.broadcasted_iota(jnp.int32, (8, LANES), 1)
    target = prob = fetched = jnp.zeros((8, LANES), jnp.float32)
    for x in range(4):
        target += packets[x, :, :LANES]
        scores = packets[x, :, LANES:]
        own = (lane // SLOT == x) & (lane % SLOT < 20)
        moved = scores if x == 0 else pltpu.roll(scores, SLOT * x, 1)
        prob += jnp.where(own, moved, 0.0)
        moved = pltpu.roll(scores, (SLOT * x + LANES // 2) % LANES, 1)
        fetched += jnp.where(own, moved, 0.0)
    gap = prob - target
    to = (
        lax.broadcasted_iota(jnp.int32, (LANES, LANES), 0) // SLOT * SLOT + 20
        == lax.broadcasted_iota(jnp.int32, (LANES, LANES), 1)
    ).astype(jnp.float32)
    along = jnp.dot(gap * fetched, to, precision=EXACT, preferred_element_type=jnp.float32)
    packed = gap / SOFTMAX_TEMPER + along / N_OWNERS
    out[...] = jnp.broadcast_to(packed[None], out.shape)


def gradient_kernel(coef, *refs):
    far, (keep, send, matrix_v), near, sems = refs[:5], refs[5:8], refs[8:13], refs[13]
    copies = load(far, near, sems)
    slot, scale, rows, unit, ordered = near
    copies[0].wait()
    copies[1].wait()
    n_rows = matrix_v.shape[1]
    blocks = coef.shape[0]

    @pl.loop(0, blocks // 8)
    def _(b):
        eight = pl.ds(pl.multiple_of(b * 8, 8), 8)
        row = lax.broadcasted_iota(jnp.int32, (8, n_rows), 1)
        values = coef[pl.ds(b // 2 + b % 2 * 64, 8, stride=8), :] * scale[eight, :]
        places = slot[eight, :]
        for x in range(4):
            total = jnp.zeros((8, n_rows), jnp.float32)
            for k in range(SLOT * x, SLOT * x + 20):
                total += jnp.where(places[:, k : k + 1] == row, values[:, k : k + 1], 0.0)
            matrix_v[pl.ds(pl.multiple_of(x * blocks + b * 8, 8), 8), :] = total

    for copy in copies[2:]:
        copy.wait()
    along_all = jnp.concatenate([coef[pl.ds(p, 16, stride=8), :] for p in range(8)], axis=0)
    along_all = along_all * scale[...]
    row_high, row_low = halves(rows[...])
    parts_high, parts_low = [], []
    for x in range(4):
        mine = slice(x * blocks, (x + 1) * blocks)
        high, low = halves(matrix_v[mine, :])
        part = dot32(high, row_high) + (dot32(high, row_low) + dot32(low, row_high))
        along = along_all[:, SLOT * x + 20 : SLOT * x + 21]
        part = part - unit[mine, :] * along
        high, low = halves(part)
        parts_high.append(high)
        parts_low.append(low)
    high, low = jnp.concatenate(parts_high, axis=0), jnp.concatenate(parts_low, axis=0)
    half = keep.shape[0]
    keep[...] = dot32(ordered[:half, :], high) + dot32(ordered[:half, :], low)
    send[...] = dot32(ordered[half:, :], high) + dot32(ordered[half:, :], low)


def body(
    index_emb,
    query_feat,
    query_proj,
    passage_id,
    passage_len,
    enc_out,
    key_proj,
    key_gain,
    dec_query,
):
    y, zq, zr, core, r = (lax.axis_index(a) for a in (*INDEX, "reader"))
    ny, nz, ncore, nx = 4, 16, 2, 4
    z = zq * 4 + zr
    n_index = ny * nz * ncore
    n_pair = ny * ncore
    my_shard = (y * nz + z) * ncore + core
    shard_rows, width = index_emb.shape
    topk = passage_id.shape[1]

    group, _, plen, feats_here = enc_out.shape
    token_rows = group * topk * plen
    with jax.named_scope("gather_enc_out"):
        token_own = enc_out.reshape(token_rows, feats_here)
        token_after, token_before = shift(token_own, "reader", 1), shift(token_own, "reader", -1)

    width_here = key_proj.shape[1]
    ids_high = (passage_id // 256).astype(jnp.bfloat16)
    ids_low = (passage_id % 256).astype(jnp.bfloat16)
    gap = ((0, 0), (0, LANES // 2 - topk))
    coded = jnp.concatenate([query_feat, jnp.pad(ids_high, gap), jnp.pad(ids_low, gap)], axis=1)
    coded = jnp.pad(coded, ((0, 0), (0, width_here - coded.shape[1])))
    with jax.named_scope("gather_key_proj"):
        own = send_all(jnp.concatenate([key_proj, coded]), "zq")
        after, before = shift(own, Z, 1), shift(own, Z, -1)
        classes = (own, after, shift(own, Z, 2), before)
        own = jnp.concatenate([block[:, :-1] for block in classes])
        after, before = shift(own, "y", 1), shift(own, "y", -1)
        far = jnp.concatenate([shift(after[:8], "y", 1), shift(before[8:], "y", -1)])
        key_rows = [(block, shift(block, "core", 1)) for block in (own, after, far, before)]
    token_far = shift(token_after, "reader", 1)
    tokens = (token_own, token_after, token_far, token_before)

    with jax.named_scope("gather_queries"):
        coded = jnp.concatenate([block[:, -1] for block in classes])
        coded = jnp.roll(coded.reshape(4, 4, width_here), zr, axis=0).reshape(nz, width_here)
        packed = send_all(coded[:, : width + LANES], NEAR)

    cols = width // nx
    six = width // n_index
    place = lax.broadcasted_iota(jnp.int32, (width, 1), 0)
    to_core, to_y = place // (ny * nz * six), place // (nz * six) % ny
    to_z, within = place // six % nz, place % six
    column = ((to_y * nz + to_z) * ncore + (to_core + core) % ncore) * six + within
    chosen = (lax.broadcasted_iota(jnp.int32, (1, width), 1) == column).astype(jnp.bfloat16)

    vmem = pl.BlockSpec(memory_space=pltpu.VMEM)
    with jax.named_scope("scores"):
        queries = n_index * nx
        operands = (packed, query_proj, index_emb, chosen)
        results = (
            jax.ShapeDtypeStruct((n_index, LANES), jnp.int32),
            jax.ShapeDtypeStruct((shard_rows, cols), jnp.float32),
            jax.ShapeDtypeStruct((queries, cols), jnp.float32),
            jax.ShapeDtypeStruct((n_index, LANES), jnp.float32),
            jax.ShapeDtypeStruct((width, queries), jnp.bfloat16),
        )
        anywhere = pl.BlockSpec(memory_space=pl.ANY)
        in_hbm = pl.BlockSpec(memory_space=pltpu.HBM)
        state, slots, my_rows, my_unit, query_scale, ordered = pl.pallas_call(
            scores_kernel,
            out_shape=(jax.ShapeDtypeStruct((n_index, LANES), jnp.float32), *results),
            in_specs=[pl.BlockSpec(memory_space=pltpu.SMEM)] + [anywhere] * 4,
            out_specs=(vmem,) + (in_hbm,) * 5,
            scratch_shapes=[
                *like(*operands, *results),
                pltpu.VMEM((queries, width), jnp.float32),
                pltpu.VMEM((nx, n_index, LANES), jnp.int32),
                pltpu.SemaphoreType.DMA((5,)),
            ],
            compiler_params=pltpu.CompilerParams(vmem_limit_bytes=56 << 20),
            cost_estimate=pl.CostEstimate(
                flops=64 << 30, bytes_accessed=8 << 20, transcendentals=0
            ),
            name="scores",
        )(jnp.stack([my_shard, r]).astype(jnp.int32), *operands)

    with jax.named_scope("reduce_scores"):
        states = lax.all_to_all(state, ("y", "core", *Z_BY_CLASS), 0, 0, tiled=True)

    with jax.named_scope("attention"):
        answer = dec_query.shape[1]
        heads_here = feats_here // DH
        decoded = dec_query.astype(jnp.float32).reshape(group, answer, heads_here, DH)
        dec_unit = (
            decoded * lax.rsqrt(jnp.mean(decoded * decoded, axis=3, keepdims=True) + EPSILON)
        ).astype(jnp.bfloat16)
        positions = lax.broadcasted_iota(jnp.int32, (group, topk, plen), 2)
        live = (positions < passage_len[:, :, None]).reshape(group, topk * plen)
        packet, own_scores = attention_packet(
            jnp.stack([y, zr, core, r]).astype(jnp.int32),
            tokens,
            key_rows,
            dec_unit.reshape(group, answer, feats_here),
            key_gain.astype(jnp.float32).reshape(1, feats_here),
            live.astype(jnp.float32),
            states,
        )

    with jax.named_scope("targets"):
        packets = lax.all_to_all(packet, NEAR, 0, 0, tiled=True).reshape(nx, n_pair, 2 * LANES)
        coef = pl.pallas_call(
            coef_kernel,
            out_shape=jax.ShapeDtypeStruct((nz, n_pair, LANES), jnp.float32),
            in_specs=[vmem],
            out_specs=vmem,
            name="coef",
        )(packets)
        coef = lax.all_to_all(coef, Z_BY_CLASS, 0, 0, tiled=True).reshape(n_index, LANES)

    with jax.named_scope("gradient"):
        part = jax.ShapeDtypeStruct((width // ncore, cols), jnp.float32)
        keep, send = pl.pallas_call(
            gradient_kernel,
            out_shape=(part, part),
            in_specs=[vmem] + [in_hbm] * 5,
            out_specs=(vmem, vmem),
            scratch_shapes=[
                pltpu.VMEM((queries, shard_rows), jnp.float32),
                *like(slots, query_scale, my_rows, my_unit, ordered),
                pltpu.SemaphoreType.DMA((5,)),
            ],
            compiler_params=pltpu.CompilerParams(vmem_limit_bytes=40 << 20),
            name="gradient",
        )(coef, slots, query_scale, my_rows, my_unit, ordered)

    with jax.named_scope("reduce_gradient"):
        term = (keep + shift(send, "core", 1)).reshape(ny, nz * six, cols)
        term = jnp.sum(lax.all_to_all(term, "y", 0, 0, tiled=True), axis=0)
        term = term.reshape(nz, six, cols)
        term = jnp.sum(lax.all_to_all(term, Z, 0, 0, tiled=True), axis=0)
        grad_proj = send_all(term, "reader")
        grad_proj = grad_proj.transpose(1, 0, 2).reshape(six, width)

    mass = jnp.sum(lax.dynamic_index_in_dim(packets, y * ncore + core, 1, False), axis=0)
    my_target = lax.dynamic_slice_in_dim(mass, r * SLOT, topk, 0)
    log_target = jnp.log(my_target)
    retr_loss = jnp.sum(my_target * (log_target - own_scores[0, :topk]))
    slab_best = own_scores[0, topk : topk + 1]
    return (grad_proj, slab_best, retr_loss[None], log_target[None])


def solution(mesh):
    split = Mesh(mesh.devices.reshape(4, 4, 4, 2, 4), INDEX + ("reader",))
    return jax.shard_map(
        body,
        mesh=split,
        in_specs=(
            P(INDEX, None),
            P(INDEX + ("reader",), None),
            P(),
            P(INDEX + ("reader",), None),
            P(INDEX, None),
            P(INDEX, None, None, "reader"),
            P(INDEX, "reader"),
            P("reader"),
            P(INDEX, None, "reader"),
        ),
        out_specs=(
            P(INDEX, None),
            P(INDEX + ("reader",)),
            P(INDEX + ("reader",)),
            P(INDEX + ("reader",), None),
        ),
        check_vma=False,
    )
```

```python
import functools
import math

import jax
import jax.numpy as jnp
from jax import lax
from jax.experimental import pallas as pl
from jax.experimental.pallas import tpu as pltpu
from jax.sharding import Mesh, PartitionSpec as P

HEADS = 64
DH = 64
ANS = 16
EPSILON = 1e-06
SOFTMAX_TEMPER = 0.05
EXACT = lax.Precision.HIGHEST
INDEX = ("y", "zq", "zr", "core")
Z = ("zq", "zr")
Z_BY_CLASS = ("zr", "zq")
NEAR = ("reader", "y", "core")
LANES = 128
SLOT = 32
TILE = 256
N_OWNERS = 128
GRANT = 48 << 20
EARLY = (0, 1, 3)
LATE = 2


def shift(x, axis, step):
    size = lax.axis_size(axis)
    return lax.ppermute(x, axis, [((i + step) % size, i) for i in range(size)])


def send_all(x, axis):
    size = lax.axis_size(axis)
    return lax.all_to_all(jnp.broadcast_to(x[None], (size, *x.shape)), axis, 0, 0, tiled=True)


def halves(x):
    high = x.astype(jnp.bfloat16)
    return high, (x - high.astype(jnp.float32)).astype(jnp.bfloat16)


def dot32(a, b):
    return jnp.dot(a, b, preferred_element_type=jnp.float32)


def load(far, near, sems):
    copies = [pltpu.make_async_copy(a, b, sems.at[i]) for i, (a, b) in enumerate(zip(far, near))]
    for copy in copies:
        copy.start()
    return copies


def like(*arrays):
    return [pltpu.VMEM(x.shape, x.dtype) for x in arrays]


def token_copies(r, chunk, tokens, target, sem):
    for j, block in enumerate(tokens):

        @pl.when((r + j) % 4 == chunk)
        def _():
            pltpu.make_async_copy(block, target, sem).start()

    return [pltpu.make_async_copy(target, target, sem)]


def row_copies(place, own, other, target, sem):
    zr, core = place[1], place[2]
    for residue in range(4):
        to = target.at[:, (zr + residue) % 4]
        four = pl.ds(4 * residue, 4)
        pltpu.make_async_copy(own.at[four], to.at[:, core], sem).start()
        pltpu.make_async_copy(other.at[four], to.at[:, 1 - core], sem).start()
    return [pltpu.make_async_copy(target, target, sem)]


def early_keys_kernel(place, *refs):
    tokens, rows, (keys_out, keys, token_v, weight_v, sems) = refs[:4], refs[4:10], refs[10:]
    y, r = place[0], place[3]
    copies = []
    for slot, ahead in enumerate(EARLY):
        own, other = rows[2 * slot], rows[2 * slot + 1]
        copies += row_copies(place, own, other, weight_v.at[slot], sems.at[0, slot])
        copies += token_copies(r, (y + ahead) % 4, tokens, token_v.at[slot], sems.at[1, slot])
    for copy in copies:
        copy.wait()
    keys[...] = dot32(token_v[0], weight_v[0].reshape(-1, keys.shape[1]))
    for slot in range(1, len(EARLY)):
        keys[...] += dot32(token_v[slot], weight_v[slot].reshape(-1, keys.shape[1]))
    copy = pltpu.make_async_copy(keys, keys_out, sems.at[2, 0])
    copy.start()
    copy.wait()


def attend(keys, offset, dec, gain, live, column_v):
    group, n = dec.shape[0], live.shape[1]
    cols = pl.ds(pl.multiple_of(offset, TILE), TILE)
    same = (
        lax.broadcasted_iota(jnp.int32, (TILE, TILE), 0) // DH
        == lax.broadcasted_iota(jnp.int32, (TILE, TILE), 1) // DH
    ).astype(jnp.bfloat16)
    mine = (
        lax.broadcasted_iota(jnp.int32, (TILE // DH * ANS, TILE), 0) // ANS
        == lax.broadcasted_iota(jnp.int32, (TILE // DH * ANS, TILE), 1) // DH
    )
    high, low = halves(keys * keys)
    square = (dot32(high, same) + dot32(low, same)) / DH
    unit = (keys * lax.rsqrt(square + EPSILON) * gain[:, cols]).astype(jnp.bfloat16)
    for g in range(group):
        answer = dec[g, :, cols].astype(jnp.float32)
        answer = jnp.concatenate([answer] * (TILE // DH), axis=0)
        answer = jnp.where(mine, answer, 0.0).astype(jnp.bfloat16)
        similarity = lax.dot_general(
            answer,
            unit[g * n : (g + 1) * n],
            (((1,), (1,)), ((), ())),
            preferred_element_type=jnp.float32,
        ) / math.sqrt(DH)
        weight = jnp.where(live[g : g + 1, :] > 0, jnp.exp(similarity), 0.0)
        weight = weight / jnp.sum(weight, axis=1, keepdims=True)
        column_v[g : g + 1, :] += jnp.sum(weight, axis=0, keepdims=True)


def late_heads_kernel(place, *refs):
    tokens, (own, other), refs = refs[:4], refs[4:6], refs[6:]
    far, (out, own_scores), near, refs = refs[:5], refs[5:7], refs[7:12], refs[12:]
    token_v, weight_v, column_v, load_sems, sems = refs
    y, r = place[0], place[3]
    loads = load(far, near, load_sems)
    early, dec, gain, live, states = near
    copies = row_copies(place, own, other, weight_v, sems.at[0])
    copies += token_copies(r, (y + LATE) % 4, tokens, token_v, sems.at[1])
    column_v[...] = jnp.zeros_like(column_v)

    lane = lax.broadcasted_iota(jnp.int32, (1, LANES), 1)
    for copy in loads:
        copy.wait()
    found = states[...]
    fetched = jnp.where(lane < 20, jnp.sum(found, axis=0, keepdims=True), 0.0)
    expo = jnp.where(lane < 20, jnp.exp(fetched), 0.0)
    total = jnp.sum(expo, axis=1, keepdims=True)
    log_prob = fetched - jnp.log(total)
    best = jnp.max(found, axis=0, keepdims=True)
    own_scores[...] = jnp.broadcast_to(jnp.where(lane == 20, best, log_prob), own_scores.shape)
    scores = expo / total + pltpu.roll(fetched, LANES // 2, 1)
    out[:, LANES:] = jnp.broadcast_to(scores, (out.shape[0], LANES))

    for copy in copies:
        copy.wait()

    early[...] += dot32(token_v[...], weight_v[...].reshape(-1, early.shape[1]))

    @pl.loop(0, early.shape[1] // TILE)
    def _(t):
        cols = pl.ds(pl.multiple_of(t * TILE, TILE), TILE)
        attend(early[:, cols], t * TILE, dec, gain, live, column_v)

    n = live.shape[1]
    mass = jnp.zeros((8, LANES), jnp.float32)
    for g in range(dec.shape[0]):
        column = jnp.broadcast_to(column_v[g : g + 1, :], (8, n))
        to = (
            lax.broadcasted_iota(jnp.int32, (n, LANES), 0) // 8 + g * SLOT
            == lax.broadcasted_iota(jnp.int32, (n, LANES), 1)
        ).astype(jnp.float32)
        mass += jnp.dot(column, to, precision=EXACT, preferred_element_type=jnp.float32)
    out[:, :LANES] = jnp.broadcast_to(mass[:1] / (HEADS * ANS), (out.shape[0], LANES))


def attention_packet(place, tokens, rows, dec, gain, live, states):
    vmem = pl.BlockSpec(memory_space=pltpu.VMEM)
    anywhere = pl.BlockSpec(memory_space=pl.ANY)
    smem = pl.BlockSpec(memory_space=pltpu.SMEM)
    token_rows, width = tokens[0].shape
    block = (4, 4, 2, *rows[0][0].shape[1:])

    def cost(count, size):
        return pl.CostEstimate(
            flops=2 * token_rows * count * width * width,
            bytes_accessed=size << 20,
            transcendentals=0,
        )

    early = pl.pallas_call(
        early_keys_kernel,
        out_shape=jax.ShapeDtypeStruct((token_rows, width), jnp.float32),
        in_specs=[smem] + [anywhere] * 10,
        out_specs=anywhere,
        scratch_shapes=[
            pltpu.VMEM((token_rows, width), jnp.float32),
            pltpu.VMEM((3, token_rows, width), jnp.bfloat16),
            pltpu.VMEM((3, *block), jnp.bfloat16),
            pltpu.SemaphoreType.DMA((3, 4)),
        ],
        compiler_params=pltpu.CompilerParams(vmem_limit_bytes=56 << 20),
        cost_estimate=cost(12, 13),
        name="early_keys",
    )(place, *tokens, *[part for ahead in EARLY for part in rows[ahead]])
    return pl.pallas_call(
        late_heads_kernel,
        out_shape=(
            jax.ShapeDtypeStruct((32, 2 * LANES), jnp.float32),
            jax.ShapeDtypeStruct((8, LANES), jnp.float32),
        ),
        in_specs=[smem] + [anywhere] * 11,
        out_specs=(vmem, vmem),
        scratch_shapes=[
            *like(early, dec, gain, live, states),
            pltpu.VMEM((token_rows, width), jnp.bfloat16),
            pltpu.VMEM(block, jnp.bfloat16),
            pltpu.VMEM((8, live.shape[1]), jnp.float32),
            pltpu.SemaphoreType.DMA((5,)),
            pltpu.SemaphoreType.DMA((2,)),
        ],
        compiler_params=pltpu.CompilerParams(vmem_limit_bytes=GRANT),
        cost_estimate=cost(1, 6),
        name="late_heads",
    )(place, *tokens, *rows[LATE], early, dec, gain, live, states)


def scores_kernel(place, *refs):
    far, (state, *outs), near, refs = refs[:4], refs[4:8], refs[8:12], refs[12:]
    near_outs, (unit_v, ids_v, sems) = refs[:3], refs[3:]
    copies = load(far, near, sems)
    packed, proj, emb, chosen = near
    lanes, sides, ordered = near_outs
    shard, r = place[0], place[1]
    n_rows, width = emb.shape
    per_x = state.shape[0]
    cols = sides.shape[1]
    for copy in copies:
        copy.wait()
    feats = packed[:, :, :width].reshape(4 * per_x, width)
    ordered[...] = lax.dot_general(
        chosen[...], feats, (((1,), (1,)), ((), ())), preferred_element_type=jnp.float32
    ).astype(jnp.bfloat16)

    lane = lax.broadcasted_iota(jnp.int32, (per_x, LANES), 1)
    spread = jnp.full((per_x, LANES), -1, jnp.int32)
    for x in range(4):
        coded = packed[8 * x : 8 * x + 8, :, width : width + LANES].reshape(per_x, LANES)
        coded = coded.astype(jnp.float32)
        ids = coded * 256 + pltpu.roll(coded, LANES // 2, 1)
        ids = ids.astype(jnp.int32) - shard * n_rows
        ids_v[x] = ids
        moved = ids if x == 0 else pltpu.roll(ids, SLOT * x, 1)
        spread = jnp.where((lane // SLOT == x) & (lane % SLOT < 20), moved, spread)
    lanes[:per_x, :] = spread.astype(jnp.float32)

    vec = dot32(feats, proj[...])
    scale_all = lax.rsqrt(jnp.sum(vec * vec, axis=1, keepdims=True) + EPSILON)
    spread = jnp.zeros((per_x, LANES), jnp.float32)
    for x in range(4):
        spread = jnp.where(lane // SLOT == x, scale_all[x * per_x : (x + 1) * per_x], spread)
    lanes[per_x:, :] = spread
    unit_all = vec * scale_all
    unit_v[...] = unit_all
    emb_all = emb[...]
    row_unit = emb_all * lax.rsqrt(jnp.sum(emb_all * emb_all, axis=1, keepdims=True) + EPSILON)
    for x in range(4):

        @pl.when(r == x)
        def _():
            sides[:n_rows, :] = row_unit[:, x * cols : (x + 1) * cols]
            sides[n_rows:, :] = unit_all[:, x * cols : (x + 1) * cols]

    copies = load(near_outs, outs, sems)
    share = unit_v[pl.ds(pl.multiple_of(r * per_x, per_x), per_x), :]
    found = (
        lax.dot_general(
            share,
            row_unit,
            (((1,), (1,)), ((), ())),
            precision=EXACT,
            preferred_element_type=jnp.float32,
        )
        / SOFTMAX_TEMPER
    )
    places = ids_v[r]
    row = lax.broadcasted_iota(jnp.int32, (per_x, n_rows), 1)
    total = jnp.where(lane == 20, jnp.max(found, axis=1, keepdims=True), 0.0)
    for k in range(20):
        picked = jnp.where(places[:, k : k + 1] == row, found, 0.0)
        total = jnp.where(lane == k, jnp.sum(picked, axis=1, keepdims=True), total)
    state[...] = total
    for copy in copies:
        copy.wait()


def coef_kernel(packets, out):
    lane = lax.broadcasted_iota(jnp.int32, (8, LANES), 1)
    target = prob = fetched = jnp.zeros((8, LANES), jnp.float32)
    for x in range(4):
        target += packets[x, :, :LANES]
        scores = packets[x, :, LANES:]
        own = (lane // SLOT == x) & (lane % SLOT < 20)
        moved = scores if x == 0 else pltpu.roll(scores, SLOT * x, 1)
        prob += jnp.where(own, moved, 0.0)
        moved = pltpu.roll(scores, (SLOT * x + LANES // 2) % LANES, 1)
        fetched += jnp.where(own, moved, 0.0)
    gap = prob - target
    to = (
        lax.broadcasted_iota(jnp.int32, (LANES, LANES), 0) // SLOT * SLOT + 20
        == lax.broadcasted_iota(jnp.int32, (LANES, LANES), 1)
    ).astype(jnp.float32)
    along = jnp.dot(gap * fetched, to, precision=EXACT, preferred_element_type=jnp.float32)
    packed = gap / SOFTMAX_TEMPER + along / N_OWNERS
    out[...] = jnp.broadcast_to(packed[None], out.shape)


def gradient_kernel(coef, *refs):
    far, (keep, send, matrix_v), near, sems = refs[:3], refs[3:6], refs[6:9], refs[9]
    copies = load(far, near, sems)
    lanes, sides, ordered = near
    copies[0].wait()
    n_rows = matrix_v.shape[1]
    blocks = coef.shape[0]

    @pl.loop(0, blocks // 8)
    def _(b):
        eight = pl.ds(pl.multiple_of(b * 8, 8), 8)
        scaled = pl.ds(pl.multiple_of(blocks + b * 8, 8), 8)
        row = lax.broadcasted_iota(jnp.int32, (8, n_rows), 1).astype(jnp.float32)
        values = coef[pl.ds(b // 2 + b % 2 * 64, 8, stride=8), :] * lanes[scaled, :]
        places = lanes[eight, :]
        for x in range(4):
            total = jnp.zeros((8, n_rows), jnp.float32)
            for k in range(SLOT * x, SLOT * x + 20):
                total += jnp.where(places[:, k : k + 1] == row, values[:, k : k + 1], 0.0)
            matrix_v[pl.ds(pl.multiple_of(x * blocks + b * 8, 8), 8), :] = total

    for copy in copies[1:]:
        copy.wait()
    along_all = jnp.concatenate([coef[pl.ds(p, 16, stride=8), :] for p in range(8)], axis=0)
    along_all = along_all * lanes[blocks:, :]
    row_high, row_low = halves(sides[:n_rows, :])
    parts_high, parts_low = [], []
    for x in range(4):
        mine = slice(x * blocks, (x + 1) * blocks)
        high, low = halves(matrix_v[mine, :])
        part = dot32(high, row_high) + (dot32(high, row_low) + dot32(low, row_high))
        along = along_all[:, SLOT * x + 20 : SLOT * x + 21]
        part = part - sides[n_rows + x * blocks : n_rows + (x + 1) * blocks, :] * along
        high, low = halves(part)
        parts_high.append(high)
        parts_low.append(low)
    high, low = jnp.concatenate(parts_high, axis=0), jnp.concatenate(parts_low, axis=0)
    half = keep.shape[0]
    keep[...] = dot32(ordered[:half, :], high) + dot32(ordered[:half, :], low)
    send[...] = dot32(ordered[half:, :], high) + dot32(ordered[half:, :], low)


def body(
    index_emb,
    query_feat,
    query_proj,
    passage_id,
    passage_len,
    enc_out,
    key_proj,
    key_gain,
    dec_query,
):
    y, zq, zr, core, r = (lax.axis_index(a) for a in (*INDEX, "reader"))
    ny, nz, ncore, nx = 4, 16, 2, 4
    z = zq * 4 + zr
    n_index = ny * nz * ncore
    n_pair = ny * ncore
    my_shard = (y * nz + z) * ncore + core
    shard_rows, width = index_emb.shape
    topk = passage_id.shape[1]

    group, _, plen, feats_here = enc_out.shape
    token_rows = group * topk * plen
    with jax.named_scope("gather_enc_out"):
        token_own = enc_out.reshape(token_rows, feats_here)
        token_after, token_before = shift(token_own, "reader", 1), shift(token_own, "reader", -1)

    width_here = key_proj.shape[1]
    ids_high = (passage_id // 256).astype(jnp.bfloat16)
    ids_low = (passage_id % 256).astype(jnp.bfloat16)
    gap = ((0, 0), (0, LANES // 2 - topk))
    coded = jnp.concatenate([query_feat, jnp.pad(ids_high, gap), jnp.pad(ids_low, gap)], axis=1)
    coded = jnp.pad(coded, ((0, 0), (0, width_here - coded.shape[1])))
    with jax.named_scope("gather_key_proj"):
        own = send_all(jnp.concatenate([key_proj, coded]), "zq")
        after, before = shift(own, Z, 1), shift(own, Z, -1)
        classes = (own, after, shift(own, Z, 2), before)
        own = jnp.concatenate([block[:, :-1] for block in classes])
        after, before = shift(own, "y", 1), shift(own, "y", -1)
        far = shift(after, "y", 1)
        key_rows = [(block, shift(block, "core", 1)) for block in (own, after, far, before)]
    token_far = shift(token_after, "reader", 1)
    tokens = (token_own, token_after, token_far, token_before)

    with jax.named_scope("gather_queries"):
        coded = jnp.concatenate([block[:, -1] for block in classes])
        coded = jnp.roll(coded.reshape(4, 4, width_here), zr, axis=0).reshape(nz, width_here)
        packed = send_all(coded[:, : width + LANES], NEAR)

    cols = width // nx
    six = width // n_index
    place = lax.broadcasted_iota(jnp.int32, (width, 1), 0)
    to_core, to_y = place // (ny * nz * six), place // (nz * six) % ny
    to_z, within = place // six % nz, place % six
    column = ((to_y * nz + to_z) * ncore + (to_core + core) % ncore) * six + within
    chosen = (lax.broadcasted_iota(jnp.int32, (1, width), 1) == column).astype(jnp.bfloat16)

    vmem = pl.BlockSpec(memory_space=pltpu.VMEM)
    with jax.named_scope("scores"):
        queries = n_index * nx
        operands = (packed, query_proj, index_emb, chosen)
        results = (
            jax.ShapeDtypeStruct((2 * n_index, LANES), jnp.float32),
            jax.ShapeDtypeStruct((shard_rows + queries, cols), jnp.float32),
            jax.ShapeDtypeStruct((width, queries), jnp.bfloat16),
        )
        anywhere = pl.BlockSpec(memory_space=pl.ANY)
        in_hbm = pl.BlockSpec(memory_space=pltpu.HBM)
        state, lanes, sides, ordered = pl.pallas_call(
            scores_kernel,
            out_shape=(jax.ShapeDtypeStruct((n_index, LANES), jnp.float32), *results),
            in_specs=[pl.BlockSpec(memory_space=pltpu.SMEM)] + [anywhere] * 4,
            out_specs=(vmem,) + (in_hbm,) * 3,
            scratch_shapes=[
                *like(*operands, *results),
                pltpu.VMEM((queries, width), jnp.float32),
                pltpu.VMEM((nx, n_index, LANES), jnp.int32),
                pltpu.SemaphoreType.DMA((5,)),
            ],
            compiler_params=pltpu.CompilerParams(vmem_limit_bytes=56 << 20),
            cost_estimate=pl.CostEstimate(
                flops=64 << 30, bytes_accessed=8 << 20, transcendentals=0
            ),
            name="scores",
        )(jnp.stack([my_shard, r]).astype(jnp.int32), *operands)

    with jax.named_scope("reduce_scores"):
        states = lax.all_to_all(state, ("y", "core", *Z_BY_CLASS), 0, 0, tiled=True)

    with jax.named_scope("attention"):
        answer = dec_query.shape[1]
        heads_here = feats_here // DH
        decoded = dec_query.astype(jnp.float32).reshape(group, answer, heads_here, DH)
        dec_unit = (
            decoded * lax.rsqrt(jnp.mean(decoded * decoded, axis=3, keepdims=True) + EPSILON)
        ).astype(jnp.bfloat16)
        positions = lax.broadcasted_iota(jnp.int32, (group, topk, plen), 2)
        live = (positions < passage_len[:, :, None]).reshape(group, topk * plen)
        packet, own_scores = attention_packet(
            jnp.stack([y, zr, core, r]).astype(jnp.int32),
            tokens,
            key_rows,
            dec_unit.reshape(group, answer, feats_here),
            key_gain.astype(jnp.float32).reshape(1, feats_here),
            live.astype(jnp.float32),
            states,
        )

    with jax.named_scope("targets"):
        packets = lax.all_to_all(packet, NEAR, 0, 0, tiled=True).reshape(nx, n_pair, 2 * LANES)
        coef = pl.pallas_call(
            coef_kernel,
            out_shape=jax.ShapeDtypeStruct((nz, n_pair, LANES), jnp.float32),
            in_specs=[vmem],
            out_specs=vmem,
            name="coef",
        )(packets)
        coef = lax.all_to_all(coef, Z_BY_CLASS, 0, 0, tiled=True).reshape(n_index, LANES)

    with jax.named_scope("gradient"):
        part = jax.ShapeDtypeStruct((width // ncore, cols), jnp.float32)
        keep, send = pl.pallas_call(
            gradient_kernel,
            out_shape=(part, part),
            in_specs=[vmem] + [in_hbm] * 3,
            out_specs=(vmem, vmem),
            scratch_shapes=[
                pltpu.VMEM((queries, shard_rows), jnp.float32),
                *like(lanes, sides, ordered),
                pltpu.SemaphoreType.DMA((5,)),
            ],
            compiler_params=pltpu.CompilerParams(vmem_limit_bytes=40 << 20),
            name="gradient",
        )(coef, lanes, sides, ordered)

    with jax.named_scope("reduce_gradient"):
        term = (keep + shift(send, "core", 1)).reshape(ny, nz * six, cols)
        term = jnp.sum(lax.all_to_all(term, "y", 0, 0, tiled=True), axis=0)
        term = term.reshape(nz, six, cols)
        term = jnp.sum(lax.all_to_all(term, Z, 0, 0, tiled=True), axis=0)
        grad_proj = send_all(term, "reader")
        grad_proj = grad_proj.transpose(1, 0, 2).reshape(six, width)

    mass = jnp.sum(lax.dynamic_index_in_dim(packets, y * ncore + core, 1, False), axis=0)
    my_target = lax.dynamic_slice_in_dim(mass, r * SLOT, topk, 0)
    log_target = jnp.log(my_target)
    retr_loss = jnp.sum(my_target * (log_target - own_scores[0, :topk]))
    slab_best = own_scores[0, topk : topk + 1]
    return (grad_proj, slab_best, retr_loss[None], log_target[None])


def solution(mesh):
    split = Mesh(mesh.devices.reshape(4, 4, 4, 2, 4), INDEX + ("reader",))
    return jax.shard_map(
        body,
        mesh=split,
        in_specs=(
            P(INDEX, None),
            P(INDEX + ("reader",), None),
            P(),
            P(INDEX + ("reader",), None),
            P(INDEX, None),
            P(INDEX, None, None, "reader"),
            P(INDEX, "reader"),
            P("reader"),
            P(INDEX, None, "reader"),
        ),
        out_specs=(
            P(INDEX, None),
            P(INDEX + ("reader",)),
            P(INDEX + ("reader",)),
            P(INDEX + ("reader",), None),
        ),
        check_vma=False,
    )
```

```python
import functools
import math

import jax
import jax.numpy as jnp
from jax import lax
from jax.experimental import pallas as pl
from jax.experimental.pallas import tpu as pltpu
from jax.sharding import Mesh, PartitionSpec as P

HEADS = 64
DH = 64
ANS = 16
EPSILON = 1e-06
SOFTMAX_TEMPER = 0.05
EXACT = lax.Precision.HIGHEST
INDEX = ("y", "zq", "zr", "core")
Z = ("zq", "zr")
Z_BY_CLASS = ("zr", "zq")
NEAR = ("reader", "y", "core")
LANES = 128
SLOT = 32
TILE = 256
N_OWNERS = 128
GRANT = 48 << 20
EARLY = (0, 1, 3)
LATE = 2


def shift(x, axis, step):
    size = lax.axis_size(axis)
    return lax.ppermute(x, axis, [((i + step) % size, i) for i in range(size)])


def send_all(x, axis):
    size = lax.axis_size(axis)
    return lax.all_to_all(jnp.broadcast_to(x[None], (size, *x.shape)), axis, 0, 0, tiled=True)


def halves(x):
    high = x.astype(jnp.bfloat16)
    return high, (x - high.astype(jnp.float32)).astype(jnp.bfloat16)


def dot32(a, b):
    return jnp.dot(a, b, preferred_element_type=jnp.float32)


def load(far, near, sems):
    copies = [pltpu.make_async_copy(a, b, sems.at[i]) for i, (a, b) in enumerate(zip(far, near))]
    for copy in copies:
        copy.start()
    return copies


def like(*arrays):
    return [pltpu.VMEM(x.shape, x.dtype) for x in arrays]


def token_copies(r, chunk, tokens, target, sem):
    for j, block in enumerate(tokens):

        @pl.when((r + j) % 4 == chunk)
        def _():
            pltpu.make_async_copy(block, target, sem).start()

    return [pltpu.make_async_copy(target, target, sem)]


def row_copies(place, own, other, target, sem):
    zr, core = place[1], place[2]
    for residue in range(4):
        to = target.at[:, (zr + residue) % 4]
        four = pl.ds(4 * residue, 4)
        pltpu.make_async_copy(own.at[four], to.at[:, core], sem).start()
        pltpu.make_async_copy(other.at[four], to.at[:, 1 - core], sem).start()
    return [pltpu.make_async_copy(target, target, sem)]


def early_keys_kernel(place, *refs):
    tokens, rows, (keys_out, keys, token_v, weight_v, sems) = refs[:4], refs[4:10], refs[10:]
    y, r = place[0], place[3]
    copies = []
    for slot, ahead in enumerate(EARLY):
        own, other = rows[2 * slot], rows[2 * slot + 1]
        copies += row_copies(place, own, other, weight_v.at[slot], sems.at[0, slot])
        copies += token_copies(r, (y + ahead) % 4, tokens, token_v.at[slot], sems.at[1, slot])
    for copy in copies:
        copy.wait()
    keys[...] = dot32(token_v[0], weight_v[0].reshape(-1, keys.shape[1]))
    for slot in range(1, len(EARLY)):
        keys[...] += dot32(token_v[slot], weight_v[slot].reshape(-1, keys.shape[1]))
    copy = pltpu.make_async_copy(keys, keys_out, sems.at[2, 0])
    copy.start()
    copy.wait()


def attend(keys, offset, dec, gain, live, column_v):
    group, n = dec.shape[0], live.shape[1]
    cols = pl.ds(pl.multiple_of(offset, TILE), TILE)
    same = (
        lax.broadcasted_iota(jnp.int32, (TILE, TILE), 0) // DH
        == lax.broadcasted_iota(jnp.int32, (TILE, TILE), 1) // DH
    ).astype(jnp.bfloat16)
    mine = (
        lax.broadcasted_iota(jnp.int32, (TILE // DH * ANS, TILE), 0) // ANS
        == lax.broadcasted_iota(jnp.int32, (TILE // DH * ANS, TILE), 1) // DH
    )
    high, low = halves(keys * keys)
    square = (dot32(high, same) + dot32(low, same)) / DH
    unit = (keys * lax.rsqrt(square + EPSILON) * gain[:, cols]).astype(jnp.bfloat16)
    for g in range(group):
        answer = dec[g, :, cols].astype(jnp.float32)
        answer = jnp.concatenate([answer] * (TILE // DH), axis=0)
        answer = jnp.where(mine, answer, 0.0).astype(jnp.bfloat16)
        similarity = lax.dot_general(
            answer,
            unit[g * n : (g + 1) * n],
            (((1,), (1,)), ((), ())),
            preferred_element_type=jnp.float32,
        ) / math.sqrt(DH)
        weight = jnp.where(live[g : g + 1, :] > 0, jnp.exp(similarity), 0.0)
        weight = weight / jnp.sum(weight, axis=1, keepdims=True)
        column_v[g : g + 1, :] += jnp.sum(weight, axis=0, keepdims=True)


def late_heads_kernel(place, *refs):
    tokens, (own, other), refs = refs[:4], refs[4:6], refs[6:]
    far, (out, own_scores), near, refs = refs[:5], refs[5:7], refs[7:12], refs[12:]
    token_v, weight_v, column_v, load_sems, sems = refs
    y, r = place[0], place[3]
    loads = load(far, near, load_sems)
    early, dec, gain, live, states = near
    copies = row_copies(place, own, other, weight_v, sems.at[0])
    copies += token_copies(r, (y + LATE) % 4, tokens, token_v, sems.at[1])
    column_v[...] = jnp.zeros_like(column_v)

    lane = lax.broadcasted_iota(jnp.int32, (1, LANES), 1)
    for copy in loads:
        copy.wait()
    found = states[...]
    fetched = jnp.where(lane < 20, jnp.sum(found, axis=0, keepdims=True), 0.0)
    expo = jnp.where(lane < 20, jnp.exp(fetched), 0.0)
    total = jnp.sum(expo, axis=1, keepdims=True)
    log_prob = fetched - jnp.log(total)
    best = jnp.max(found, axis=0, keepdims=True)
    own_scores[...] = jnp.broadcast_to(jnp.where(lane == 20, best, log_prob), own_scores.shape)
    scores = expo / total + pltpu.roll(fetched, LANES // 2, 1)
    out[:, LANES:] = jnp.broadcast_to(scores, (out.shape[0], LANES))

    for copy in copies:
        copy.wait()

    early[...] += dot32(token_v[...], weight_v[...].reshape(-1, early.shape[1]))

    @pl.loop(0, early.shape[1] // TILE)
    def _(t):
        cols = pl.ds(pl.multiple_of(t * TILE, TILE), TILE)
        attend(early[:, cols], t * TILE, dec, gain, live, column_v)

    n = live.shape[1]
    mass = jnp.zeros((8, LANES), jnp.float32)
    for g in range(dec.shape[0]):
        column = jnp.broadcast_to(column_v[g : g + 1, :], (8, n))
        to = (
            lax.broadcasted_iota(jnp.int32, (n, LANES), 0) // 8 + g * SLOT
            == lax.broadcasted_iota(jnp.int32, (n, LANES), 1)
        ).astype(jnp.float32)
        mass += jnp.dot(column, to, precision=EXACT, preferred_element_type=jnp.float32)
    out[:, :LANES] = jnp.broadcast_to(mass[:1] / (HEADS * ANS), (out.shape[0], LANES))


def attention_packet(place, tokens, rows, dec, gain, live, states):
    vmem = pl.BlockSpec(memory_space=pltpu.VMEM)
    anywhere = pl.BlockSpec(memory_space=pl.ANY)
    smem = pl.BlockSpec(memory_space=pltpu.SMEM)
    token_rows, width = tokens[0].shape
    block = (4, 4, 2, *rows[0][0].shape[1:])

    def cost(count, size):
        return pl.CostEstimate(
            flops=2 * token_rows * count * width * width,
            bytes_accessed=size << 20,
            transcendentals=0,
        )

    early = pl.pallas_call(
        early_keys_kernel,
        out_shape=jax.ShapeDtypeStruct((token_rows, width), jnp.float32),
        in_specs=[smem] + [anywhere] * 10,
        out_specs=anywhere,
        scratch_shapes=[
            pltpu.VMEM((token_rows, width), jnp.float32),
            pltpu.VMEM((3, token_rows, width), jnp.bfloat16),
            pltpu.VMEM((3, *block), jnp.bfloat16),
            pltpu.SemaphoreType.DMA((3, 4)),
        ],
        compiler_params=pltpu.CompilerParams(vmem_limit_bytes=56 << 20),
        cost_estimate=cost(12, 13),
        name="early_keys",
    )(place, *tokens, *[part for ahead in EARLY for part in rows[ahead]])
    return pl.pallas_call(
        late_heads_kernel,
        out_shape=(
            jax.ShapeDtypeStruct((32, 2 * LANES), jnp.float32),
            jax.ShapeDtypeStruct((8, LANES), jnp.float32),
        ),
        in_specs=[smem] + [anywhere] * 11,
        out_specs=(vmem, vmem),
        scratch_shapes=[
            *like(early, dec, gain, live, states),
            pltpu.VMEM((token_rows, width), jnp.bfloat16),
            pltpu.VMEM(block, jnp.bfloat16),
            pltpu.VMEM((8, live.shape[1]), jnp.float32),
            pltpu.SemaphoreType.DMA((5,)),
            pltpu.SemaphoreType.DMA((2,)),
        ],
        compiler_params=pltpu.CompilerParams(vmem_limit_bytes=GRANT),
        cost_estimate=cost(1, 6),
        name="late_heads",
    )(place, *tokens, *rows[LATE], early, dec, gain, live, states)


def scores_kernel(place, *refs):
    far, (state, *outs), near, refs = refs[:4], refs[4:8], refs[8:12], refs[12:]
    near_outs, (unit_v, ids_v, sems) = refs[:3], refs[3:]
    copies = load(far, near, sems)
    packed, proj, emb, chosen = near
    lanes, sides, ordered = near_outs
    shard, r = place[0], place[1]
    n_rows, width = emb.shape
    per_x = state.shape[0]
    cols = sides.shape[1]
    for copy in copies:
        copy.wait()
    feats = packed[:, :, :width].reshape(4 * per_x, width)
    ordered[...] = lax.dot_general(
        chosen[...], feats, (((1,), (1,)), ((), ())), preferred_element_type=jnp.float32
    ).astype(jnp.bfloat16)

    lane = lax.broadcasted_iota(jnp.int32, (per_x, LANES), 1)
    spread = jnp.full((per_x, LANES), -1, jnp.int32)
    for x in range(4):
        coded = packed[8 * x : 8 * x + 8, :, width : width + LANES].reshape(per_x, LANES)
        coded = coded.astype(jnp.float32)
        ids = coded * 256 + pltpu.roll(coded, LANES // 2, 1)
        ids = ids.astype(jnp.int32) - shard * n_rows
        ids_v[x] = ids
        moved = ids if x == 0 else pltpu.roll(ids, SLOT * x, 1)
        spread = jnp.where((lane // SLOT == x) & (lane % SLOT < 20), moved, spread)
    lanes[:per_x, :] = spread.astype(jnp.float32)

    vec = dot32(feats, proj[...])
    scale_all = lax.rsqrt(jnp.sum(vec * vec, axis=1, keepdims=True) + EPSILON)
    spread = jnp.zeros((per_x, LANES), jnp.float32)
    for x in range(4):
        spread = jnp.where(lane // SLOT == x, scale_all[x * per_x : (x + 1) * per_x], spread)
    lanes[per_x:, :] = spread
    unit_all = vec * scale_all
    unit_v[...] = unit_all
    emb_all = emb[...]
    row_unit = emb_all * lax.rsqrt(jnp.sum(emb_all * emb_all, axis=1, keepdims=True) + EPSILON)
    for x in range(4):

        @pl.when(r == x)
        def _():
            sides[:n_rows, :] = row_unit[:, x * cols : (x + 1) * cols]
            sides[n_rows:, :] = unit_all[:, x * cols : (x + 1) * cols]

    copies = load(near_outs, outs, sems)
    share = unit_v[pl.ds(pl.multiple_of(r * per_x, per_x), per_x), :]
    found = (
        lax.dot_general(
            share,
            row_unit,
            (((1,), (1,)), ((), ())),
            precision=EXACT,
            preferred_element_type=jnp.float32,
        )
        / SOFTMAX_TEMPER
    )
    places = ids_v[r]
    row = lax.broadcasted_iota(jnp.int32, (per_x, n_rows), 1)
    total = jnp.where(lane == 20, jnp.max(found, axis=1, keepdims=True), 0.0)
    for k in range(20):
        picked = jnp.where(places[:, k : k + 1] == row, found, 0.0)
        total = jnp.where(lane == k, jnp.sum(picked, axis=1, keepdims=True), total)
    state[...] = total
    for copy in copies:
        copy.wait()


def coef_kernel(packets, out):
    lane = lax.broadcasted_iota(jnp.int32, (8, LANES), 1)
    target = prob = fetched = jnp.zeros((8, LANES), jnp.float32)
    for x in range(4):
        target += packets[x, :, :LANES]
        scores = packets[x, :, LANES:]
        own = (lane // SLOT == x) & (lane % SLOT < 20)
        moved = scores if x == 0 else pltpu.roll(scores, SLOT * x, 1)
        prob += jnp.where(own, moved, 0.0)
        moved = pltpu.roll(scores, (SLOT * x + LANES // 2) % LANES, 1)
        fetched += jnp.where(own, moved, 0.0)
    gap = prob - target
    to = (
        lax.broadcasted_iota(jnp.int32, (LANES, LANES), 0) // SLOT * SLOT + 20
        == lax.broadcasted_iota(jnp.int32, (LANES, LANES), 1)
    ).astype(jnp.float32)
    along = jnp.dot(gap * fetched, to, precision=EXACT, preferred_element_type=jnp.float32)
    packed = gap / SOFTMAX_TEMPER + along / N_OWNERS
    out[...] = jnp.broadcast_to(packed[None], out.shape)


def gradient_kernel(coef, *refs):
    far, (keep, send, matrix_v), near, sems = refs[:3], refs[3:6], refs[6:9], refs[9]
    copies = load(far, near, sems)
    lanes, sides, ordered = near
    copies[0].wait()
    n_rows = matrix_v.shape[1]
    blocks = coef.shape[0]

    @pl.loop(0, blocks // 8)
    def _(b):
        eight = pl.ds(pl.multiple_of(b * 8, 8), 8)
        scaled = pl.ds(pl.multiple_of(blocks + b * 8, 8), 8)
        row = lax.broadcasted_iota(jnp.int32, (8, n_rows), 1).astype(jnp.float32)
        values = coef[pl.ds(b // 2 + b % 2 * 64, 8, stride=8), :] * lanes[scaled, :]
        places = lanes[eight, :]
        for x in range(4):
            total = jnp.zeros((8, n_rows), jnp.float32)
            for k in range(SLOT * x, SLOT * x + 20):
                total += jnp.where(places[:, k : k + 1] == row, values[:, k : k + 1], 0.0)
            matrix_v[pl.ds(pl.multiple_of(x * blocks + b * 8, 8), 8), :] = total

    for copy in copies[1:]:
        copy.wait()
    along_all = jnp.concatenate([coef[pl.ds(p, 16, stride=8), :] for p in range(8)], axis=0)
    along_all = along_all * lanes[blocks:, :]
    row_high, row_low = halves(sides[:n_rows, :])
    parts_high, parts_low = [], []
    for x in range(4):
        mine = slice(x * blocks, (x + 1) * blocks)
        high, low = halves(matrix_v[mine, :])
        part = dot32(high, row_high) + (dot32(high, row_low) + dot32(low, row_high))
        along = along_all[:, SLOT * x + 20 : SLOT * x + 21]
        part = part - sides[n_rows + x * blocks : n_rows + (x + 1) * blocks, :] * along
        high, low = halves(part)
        parts_high.append(high)
        parts_low.append(low)
    high, low = jnp.concatenate(parts_high, axis=0), jnp.concatenate(parts_low, axis=0)
    half = keep.shape[0]
    keep[...] = dot32(ordered[:half, :], high) + dot32(ordered[:half, :], low)
    send[...] = dot32(ordered[half:, :], high) + dot32(ordered[half:, :], low)


def body(
    index_emb,
    query_feat,
    query_proj,
    passage_id,
    passage_len,
    enc_out,
    key_proj,
    key_gain,
    dec_query,
):
    y, zq, zr, core, r = (lax.axis_index(a) for a in (*INDEX, "reader"))
    ny, nz, ncore, nx = 4, 16, 2, 4
    z = zq * 4 + zr
    n_index = ny * nz * ncore
    n_pair = ny * ncore
    my_shard = (y * nz + z) * ncore + core
    shard_rows, width = index_emb.shape
    topk = passage_id.shape[1]

    group, _, plen, feats_here = enc_out.shape
    token_rows = group * topk * plen
    with jax.named_scope("gather_enc_out"):
        token_own = enc_out.reshape(token_rows, feats_here)
        token_after, token_before = shift(token_own, "reader", 1), shift(token_own, "reader", -1)

    width_here = key_proj.shape[1]
    ids_high = (passage_id // 256).astype(jnp.bfloat16)
    ids_low = (passage_id % 256).astype(jnp.bfloat16)
    gap = ((0, 0), (0, LANES // 2 - topk))
    coded = jnp.concatenate([query_feat, jnp.pad(ids_high, gap), jnp.pad(ids_low, gap)], axis=1)
    coded = jnp.pad(coded, ((0, 0), (0, width_here - coded.shape[1])))
    with jax.named_scope("gather_key_proj"):
        own = send_all(jnp.concatenate([key_proj, coded]), "zq")
        after, before = shift(own, Z, 1), shift(own, Z, -1)
        classes = (own, after, shift(own, Z, 2), before)
        own = jnp.concatenate([block[:, :-1] for block in classes])
        after, before = shift(own, "y", 1), shift(own, "y", -1)
        far = shift(after, "y", 1)
        key_rows = [(block, shift(block, "core", 1)) for block in (own, after, far, before)]
    token_far = shift(token_after, "reader", 1)
    tokens = (token_own, token_after, token_far, token_before)

    with jax.named_scope("gather_queries"):
        coded = jnp.concatenate([block[:, -1] for block in classes])
        coded = jnp.roll(coded.reshape(4, 4, width_here), zr, axis=0).reshape(nz, width_here)
        packed = send_all(coded[:, : width + LANES], NEAR)

    cols = width // nx
    six = width // n_index
    place = lax.broadcasted_iota(jnp.int32, (width, 1), 0)
    to_core, to_y = place // (ny * nz * six), place // (nz * six) % ny
    to_z, within = place // six % nz, place % six
    column = ((to_y * nz + to_z) * ncore + (to_core + core) % ncore) * six + within
    chosen = (lax.broadcasted_iota(jnp.int32, (1, width), 1) == column).astype(jnp.bfloat16)

    vmem = pl.BlockSpec(memory_space=pltpu.VMEM)
    with jax.named_scope("scores"):
        queries = n_index * nx
        operands = (packed, query_proj, index_emb, chosen)
        results = (
            jax.ShapeDtypeStruct((2 * n_index, LANES), jnp.float32),
            jax.ShapeDtypeStruct((shard_rows + queries, cols), jnp.float32),
            jax.ShapeDtypeStruct((width, queries), jnp.bfloat16),
        )
        anywhere = pl.BlockSpec(memory_space=pl.ANY)
        in_hbm = pl.BlockSpec(memory_space=pltpu.HBM)
        state, lanes, sides, ordered = pl.pallas_call(
            scores_kernel,
            out_shape=(jax.ShapeDtypeStruct((n_index, LANES), jnp.float32), *results),
            in_specs=[pl.BlockSpec(memory_space=pltpu.SMEM)] + [anywhere] * 4,
            out_specs=(vmem,) + (in_hbm,) * 3,
            scratch_shapes=[
                *like(*operands, *results),
                pltpu.VMEM((queries, width), jnp.float32),
                pltpu.VMEM((nx, n_index, LANES), jnp.int32),
                pltpu.SemaphoreType.DMA((5,)),
            ],
            compiler_params=pltpu.CompilerParams(vmem_limit_bytes=56 << 20),
            cost_estimate=pl.CostEstimate(
                flops=64 << 30, bytes_accessed=8 << 20, transcendentals=0
            ),
            name="scores",
        )(jnp.stack([my_shard, r]).astype(jnp.int32), *operands)

    with jax.named_scope("reduce_scores"):
        states = lax.all_to_all(state, ("y", "core", *Z_BY_CLASS), 0, 0, tiled=True)

    with jax.named_scope("attention"):
        answer = dec_query.shape[1]
        heads_here = feats_here // DH
        decoded = dec_query.astype(jnp.float32).reshape(group, answer, heads_here, DH)
        dec_unit = (
            decoded * lax.rsqrt(jnp.mean(decoded * decoded, axis=3, keepdims=True) + EPSILON)
        ).astype(jnp.bfloat16)
        positions = lax.broadcasted_iota(jnp.int32, (group, topk, plen), 2)
        live = (positions < passage_len[:, :, None]).reshape(group, topk * plen)
        packet, own_scores = attention_packet(
            jnp.stack([y, zr, core, r]).astype(jnp.int32),
            tokens,
            key_rows,
            dec_unit.reshape(group, answer, feats_here),
            key_gain.astype(jnp.float32).reshape(1, feats_here),
            live.astype(jnp.float32),
            states,
        )

    with jax.named_scope("targets"):
        packets = lax.all_to_all(packet, NEAR, 0, 0, tiled=True).reshape(nx, n_pair, 2 * LANES)
        coef = pl.pallas_call(
            coef_kernel,
            out_shape=jax.ShapeDtypeStruct((nz, n_pair, LANES), jnp.float32),
            in_specs=[vmem],
            out_specs=vmem,
            compiler_params=pltpu.CompilerParams(vmem_limit_bytes=8 << 20),
            name="coef",
        )(packets)
        coef = lax.all_to_all(coef, Z_BY_CLASS, 0, 0, tiled=True).reshape(n_index, LANES)

    with jax.named_scope("gradient"):
        part = jax.ShapeDtypeStruct((width // ncore, cols), jnp.float32)
        keep, send = pl.pallas_call(
            gradient_kernel,
            out_shape=(part, part),
            in_specs=[vmem] + [in_hbm] * 3,
            out_specs=(vmem, vmem),
            scratch_shapes=[
                pltpu.VMEM((queries, shard_rows), jnp.float32),
                *like(lanes, sides, ordered),
                pltpu.SemaphoreType.DMA((5,)),
            ],
            compiler_params=pltpu.CompilerParams(vmem_limit_bytes=40 << 20),
            name="gradient",
        )(coef, lanes, sides, ordered)

    with jax.named_scope("reduce_gradient"):
        term = (keep + shift(send, "core", 1)).reshape(ny, nz * six, cols)
        term = jnp.sum(lax.all_to_all(term, "y", 0, 0, tiled=True), axis=0)
        term = term.reshape(nz, six, cols)
        term = jnp.sum(lax.all_to_all(term, Z, 0, 0, tiled=True), axis=0)
        grad_proj = send_all(term, "reader")
        grad_proj = grad_proj.transpose(1, 0, 2).reshape(six, width)

    mass = jnp.sum(lax.dynamic_index_in_dim(packets, y * ncore + core, 1, False), axis=0)
    my_target = lax.dynamic_slice_in_dim(mass, r * SLOT, topk, 0)
    log_target = jnp.log(my_target)
    retr_loss = jnp.sum(my_target * (log_target - own_scores[0, :topk]))
    slab_best = own_scores[0, topk : topk + 1]
    return (grad_proj, slab_best, retr_loss[None], log_target[None])


def solution(mesh):
    split = Mesh(mesh.devices.reshape(4, 4, 4, 2, 4), INDEX + ("reader",))
    return jax.shard_map(
        body,
        mesh=split,
        in_specs=(
            P(INDEX, None),
            P(INDEX + ("reader",), None),
            P(),
            P(INDEX + ("reader",), None),
            P(INDEX, None),
            P(INDEX, None, None, "reader"),
            P(INDEX, "reader"),
            P("reader"),
            P(INDEX, None, "reader"),
        ),
        out_specs=(
            P(INDEX, None),
            P(INDEX + ("reader",)),
            P(INDEX + ("reader",)),
            P(INDEX + ("reader",), None),
        ),
        check_vma=False,
    )
```
